32 devices in a mesh: seq: 8 (over z, x), head: 4 (over y, core).
Axes of the slice: x: 2, y: 2, z: 4, core: 2. Of those that a mesh axis runs over, the one named last changes fastest.
Arguments:
- tokens: float32 [4096, 1024], P(('seq', 'head')), may hold values from -6 to 6
- w_query: float32 [2, 1024, 1024], P(None, ('seq', 'head')), may hold values from -0.1875 to 0.1875
- w_key: float32 [2, 1024, 1024], P(None, ('seq', 'head')), may hold values from -0.1875 to 0.1875
- w_value: float32 [2, 1024, 1024], P(None, ('seq', 'head')), may hold values from -0.1875 to 0.1875
- w_out: float32 [2, 1024, 1024], P(None, ('seq', 'head')), may hold values from -1.5 to 1.5
- w_gate: float32 [2, 1024, 2816], P(None, ('seq', 'head')), may hold values from -0.1875 to 0.1875
- w_up: float32 [2, 1024, 2816], P(None, ('seq', 'head')), may hold values from -0.1875 to 0.1875
- w_down: float32 [2, 2816, 1024], P(None, ('seq', 'head')), may hold values from -0.109375 to 0.109375
- gain_attn: float32 [2, 1024], P(None, ('seq', 'head')), may hold values from 0.1 to 1.9
- gain_ffn: float32 [2, 1024], P(None, ('seq', 'head')), may hold values from 0.1 to 1.9
- variate_bias: float32 [2, 2, 16], replicated, may hold values from -3 to 3
- doc_starts: int32 [6], replicated, may hold values from 0 to 4095, as said below
- variate_ids: int32 [4096], replicated, may hold values from 0 to 7
- time_ids: int32 [4096], P(('seq', 'head')), may hold values from 0 to 511
- cotangent: float32 [4096, 1024], P(('seq', 'head')), may hold values from -6 to 6
Outputs:
- output: float32 [4096, 1024], P(('seq', 'head'))
- grad_tokens: float32 [4096, 1024], P(('seq', 'head'))
- grad_w_query: float32 [2, 1024, 1024], P(None, ('seq', 'head'))
- grad_w_key: float32 [2, 1024, 1024], P(None, ('seq', 'head'))
- grad_w_value: float32 [2, 1024, 1024], P(None, ('seq', 'head'))
- grad_w_out: float32 [2, 1024, 1024], P(None, ('seq', 'head'))
- grad_w_gate: float32 [2, 1024, 2816], P(None, ('seq', 'head'))
- grad_w_up: float32 [2, 1024, 2816], P(None, ('seq', 'head'))
- grad_w_down: float32 [2, 2816, 1024], P(None, ('seq', 'head'))
- grad_gain_attn: float32 [2, 1024], P(None, ('seq', 'head'))
- grad_gain_ffn: float32 [2, 1024], P(None, ('seq', 'head'))
- grad_variate_bias: float32 [2, 2, 16], replicated
The draws below stay inside these ranges and needn't reach their ends.
Inputs may be any that keep to these rules, and one draw needn't show every extreme that they name: `doc_starts`: strictly increasing with the first entry 0. The first three starts lie among the first 512 tokens, the last three among the last 512 tokens, so that the third document runs from the first 512 tokens into the last 512.
All inputs are finite; a program needn't handle non-finite values.
Results may differ from the reference program's by a relative error of at most 0.04.
Values may be sent and summed in bfloat16 or wider, within the bound.
No kernel may reach another device: no remote copies, remote signals or barrier semaphores. Data moves between devices by JAX's collectives and lax.ppermute only.
A program may use at most 320 MiB of HBM per device.

```python
import math
import jax
import jax.numpy as jnp
from jax import lax

D = 1024
HEADS = 16
HD = 64
FF = 2816
LAYERS = 2
VARIATES = 8
TIMES = 512
SEQ_ROWS = 512
TOKENS = 4096


def draw_doc_starts(key, part):
    key = jax.random.fold_in(key, 11)
    subkeys = jax.random.split(key, 5)
    half_rows = SEQ_ROWS // 2
    quarter_rows = SEQ_ROWS // 4
    second = jax.random.randint(subkeys[0], (1,), 1, half_rows)
    third = jax.random.randint(subkeys[1], (1,), half_rows, SEQ_ROWS)
    fourth = jax.random.randint(subkeys[2], (1,), TOKENS - SEQ_ROWS + 1, TOKENS - half_rows)
    fifth = jax.random.randint(subkeys[3], (1,), TOKENS - half_rows, TOKENS - quarter_rows)
    sixth = jax.random.randint(subkeys[4], (1,), TOKENS - quarter_rows, TOKENS)
    return jnp.concatenate([jnp.zeros((1,), jnp.int32), second, third, fourth, fifth, sixth]).astype(jnp.int32)


def touch_ends(drawn, stream_key, low, largest):
    shape = drawn.shape
    place = [jax.random.randint(jax.random.fold_in(stream_key, axis), (), 0, shape[axis]) for axis in range(len(shape))]
    drawn = drawn.at[tuple(place)].set(low)
    longest = shape.index(max(shape))
    place[longest] = (place[longest] + 1) % shape[longest]
    return drawn.at[tuple(place)].set(largest)


def shard_levels(key, extent, cuts, least, top_value):
    factor_of, own = 1.0, jax.random.fold_in(key, 6)
    for axis_at, parts in cuts:
        steps = jnp.exp(jax.random.uniform(jax.random.fold_in(own, axis_at), (parts,), jnp.float32, least / len(cuts), top_value / len(cuts)))
        factor_of = factor_of * jnp.repeat(steps, extent[axis_at] // parts).reshape([-1 if axis == axis_at else 1 for axis in range(len(extent))])
    return factor_of


def scatter_about(own_key, dims, deviation, reach, pieces=(), kind=jnp.bfloat16):
    array = deviation * jax.random.normal(own_key, dims, jnp.float32)
    if pieces:
        array = array * shard_levels(own_key, dims, pieces, -0.22, 0.18)
    return jnp.clip(array, -reach, reach).astype(kind)


def setup_inputs(seed: int = 0) -> dict:
    arg_keys = jax.random.split(jax.random.key(seed), 16)
    return {
        "tokens": scatter_about(arg_keys[0], (TOKENS, D), 1.0, 6.0, ((0, 32),), jnp.float32),
        "w_query": scatter_about(arg_keys[1], (LAYERS, D, D), D ** -0.5, 0.1875, ((1, 32),), jnp.float32),
        "w_key": scatter_about(arg_keys[2], (LAYERS, D, D), D ** -0.5, 0.1875, ((1, 32),), jnp.float32),
        "w_value": scatter_about(arg_keys[3], (LAYERS, D, D), D ** -0.5, 0.1875, ((1, 32),), jnp.float32),
        "w_out": scatter_about(arg_keys[4], (LAYERS, D, D), (max(1, D * 64 // TOKENS)) ** -0.5, 1.5, ((1, 32),), jnp.float32),
        "w_gate": scatter_about(arg_keys[5], (LAYERS, D, FF), D ** -0.5, 0.1875, ((1, 32),), jnp.float32),
        "w_up": scatter_about(arg_keys[6], (LAYERS, D, FF), D ** -0.5, 0.1875, ((1, 32),), jnp.float32),
        "w_down": scatter_about(arg_keys[7], (LAYERS, FF, D), FF ** -0.5, 0.109375, ((1, 32),), jnp.float32),
        "gain_attn": jnp.clip(1.0 + 0.18 * jax.random.normal(arg_keys[8], (LAYERS, D), jnp.float32), 0.1, 1.9),
        "gain_ffn": jnp.clip(1.0 + 0.18 * jax.random.normal(arg_keys[9], (LAYERS, D), jnp.float32), 0.1, 1.9),
        "variate_bias": scatter_about(arg_keys[10], (LAYERS, 2, HEADS), 1.0, 3.0, (), jnp.float32),
        "doc_starts": draw_doc_starts(jax.random.fold_in(arg_keys[15], 71), 0),
        "variate_ids": touch_ends(jax.random.randint(arg_keys[12], (TOKENS,), 0, VARIATES), jax.random.fold_in(arg_keys[12], 1), 0, VARIATES - 1).astype(jnp.int32),
        "time_ids": touch_ends(jax.random.randint(arg_keys[13], (TOKENS,), 0, TIMES), jax.random.fold_in(arg_keys[13], 1), 0, TIMES - 1).astype(jnp.int32),
        "cotangent": scatter_about(arg_keys[14], (TOKENS, D), 1.0, 6.0, ((0, 32),), jnp.float32),
    }


NORM_EPS = 1e-05

@jax.custom_vjp
def low(v):
    return lax.optimization_barrier(v.astype(jnp.bfloat16)).astype(jnp.float32)

@jax.custom_vjp
def low_back(v):
    return v

def low_keep(v):
    return (low(v), None)

def low_pass(kept, grad):
    return (grad,)

def back_keep(v):
    return (v, None)

def back_low(kept, grad):
    return (low(grad),)
low.defvjp(low_keep, low_pass)
low_back.defvjp(back_keep, back_low)

def rms_scale(values, gain_vec):
    return values * lax.rsqrt(lax.optimization_barrier(jnp.mean(values * values, axis=-1, keepdims=True)) + NORM_EPS) * gain_vec

def rotate(values, cosines, sines):
    half_dim = values.shape[-1] // 2
    former = values[..., :half_dim]
    latter = values[..., half_dim:]
    return jnp.concatenate([former * cosines - latter * sines, latter * cosines + former * sines], axis=-1)

def attention(queries, keys_all, values_all, bias_pair, doc_ids, variate_ids):
    row_block = math.gcd(TOKENS, 512)
    score_scale = 1.0 / math.sqrt(HD)

    def one_block(inputs):
        query_block, query_docs, query_vars = inputs
        scores = jnp.einsum('qhd,khd->hqk', query_block, keys_all, precision=lax.Precision.HIGHEST) * score_scale
        same_var = query_vars[:, None] == variate_ids[None, :]
        scores = scores + jnp.where(same_var[None], bias_pair[0][:, None, None], bias_pair[1][:, None, None])
        scores = low_back(scores)
        allowed = query_docs[:, None] == doc_ids[None, :]
        scores = jnp.where(allowed[None], scores, -1e+30)
        row_max = lax.optimization_barrier(jnp.max(scores, axis=-1, keepdims=True))
        log_total = row_max + jnp.log(lax.optimization_barrier(jnp.sum(jnp.exp(scores - row_max), axis=-1, keepdims=True)))
        probability = low(jnp.exp(scores - log_total))
        return jnp.einsum('hqk,khd->qhd', probability, values_all, precision=lax.Precision.HIGHEST)
    block_count = TOKENS // row_block
    result = lax.map(jax.checkpoint(one_block), (queries.reshape(block_count, row_block, HEADS, HD), doc_ids.reshape(block_count, row_block), variate_ids.reshape(block_count, row_block)))
    return result.reshape(TOKENS, D)

def block_layer(stream, params, bias_pair, cosines, sines, doc_ids, variate_ids):
    query_matrix, key_matrix, value_matrix, output_matrix, gate_matrix, upward_matrix, down_matrix, attention_gain, feedforward_gain = [low(member) for member in params]
    normed = low(rms_scale(stream, attention_gain))
    query_lin = low_back(jnp.dot(normed, query_matrix, precision=lax.Precision.HIGHEST))
    key_lin = low_back(jnp.dot(normed, key_matrix, precision=lax.Precision.HIGHEST))
    value_lin = jnp.dot(normed, value_matrix, precision=lax.Precision.HIGHEST)
    queries = low_back(low(rotate(query_lin.reshape(TOKENS, HEADS, HD), cosines, sines)))
    keys_all = low_back(low(rotate(key_lin.reshape(TOKENS, HEADS, HD), cosines, sines)))
    values_all = low_back(low(value_lin.reshape(TOKENS, HEADS, HD)))
    mixed = low_back(low(attention(queries, keys_all, values_all, bias_pair, doc_ids, variate_ids)))
    middle = stream + low_back(jnp.dot(mixed, output_matrix, precision=lax.Precision.HIGHEST))
    normed_ffn = low(rms_scale(middle, feedforward_gain))
    gate_lin = low_back(jnp.dot(normed_ffn, gate_matrix, precision=lax.Precision.HIGHEST))
    upward_lin = low_back(jnp.dot(normed_ffn, upward_matrix, precision=lax.Precision.HIGHEST))
    hidden = low(jax.nn.silu(gate_lin) * upward_lin)
    return middle + low_back(jnp.dot(hidden, down_matrix, precision=lax.Precision.HIGHEST))

def reference(tokens, w_query, w_key, w_value, w_out, w_gate, w_up, w_down, gain_attn, gain_ffn, variate_bias, doc_starts, variate_ids, time_ids, cotangent):
    positions = jnp.arange(TOKENS, dtype=jnp.int32)
    doc_ids = lax.optimization_barrier(jnp.sum((doc_starts[None, :] <= positions[:, None]).astype(jnp.int32), axis=1)).astype(jnp.int32)
    half_dim = HD // 2
    frequency = jnp.exp(jnp.arange(half_dim).astype(jnp.float32) * (-2.0 * math.log(10000.0) / HD))
    angles = time_ids.astype(jnp.float32)[:, None] * frequency[None, :]
    cosines = jnp.cos(angles)[:, None, :]
    sines = jnp.sin(angles)[:, None, :]

    def forward(stream, *weight_list):
        matrices = weight_list[:9]
        bias_all = weight_list[9]
        for layer_index in range(LAYERS):
            params = [member[layer_index] for member in matrices]
            stream = block_layer(stream, params, bias_all[layer_index], cosines, sines, doc_ids, variate_ids)
        return stream
    primals = (tokens, w_query, w_key, w_value, w_out, w_gate, w_up, w_down, gain_attn, gain_ffn, variate_bias)
    output, pullback = jax.vjp(forward, *primals)
    gradients = pullback(cotangent)
    return (output, gradients[0], gradients[1], gradients[2], gradients[3], gradients[4], gradients[5], gradients[6], gradients[7], gradients[8], gradients[9], gradients[10])
```

```python
import functools
import math

import jax
import jax.numpy as jnp
from jax import lax
from jax.experimental import pallas as pl
from jax.experimental.pallas import tpu as pltpu
from jax.sharding import PartitionSpec as P

D = 1024
HEADS = 16
HD = 64
LAYERS = 2
HALF_HEADS = HEADS // 2
VARIATES = 8
BLOCK = 256

NORM_EPS = 1e-05
FLOOR_SCORE = -1e30
LOW = jnp.bfloat16
BOTH = ("seq", "head")

Y_SWAP = [(0, 2), (2, 0), (1, 3), (3, 1)]
CORE_SWAP = [(0, 1), (1, 0), (2, 3), (3, 2)]
TRANSPOSE = [(0, 0), (1, 2), (2, 1), (3, 3)]
ANTI_TRANSPOSE = [(0, 2), (2, 3), (3, 1), (1, 0)]

NN = (((1,), (0,)), ((), ()))
NT = (((1,), (1,)), ((), ()))
TN = (((0,), (0,)), ((), ()))
TT = (((0,), (1,)), ((), ()))
VMEM_LIMIT = 56 * 1024 * 1024


def dot(left, right, dims):
    return lax.dot_general(left, right, dims, preferred_element_type=jnp.float32)


def forward_kernel(
    first_ref, q_ref, q_aug_ref, q_doc_ref, own_ref, sib_ref, k_aug_ref, k_doc_ref,
    out_ref, lse_ref, *, seq, width,
):
    tile = first_ref[0] + pl.program_id(0)
    sources = ((own_ref, HD), (sib_ref, 0))
    blocks = [(half, s) for half in range(2) for s in range(seq)]
    cols = q_ref.shape[-1]
    q_side = jnp.concatenate([q_ref[0, :HD, :], q_aug_ref[0]], axis=0).T

    def run(edge_tile):
        q_doc = q_doc_ref[0]
        top = jnp.full((cols, 1), FLOOR_SCORE, jnp.float32)
        total = jnp.zeros((cols, 1), jnp.float32)
        acc = jnp.zeros((cols, HD), jnp.float32)
        for start in range(0, len(blocks), width):
            group = blocks[start : start + width]
            parts = []
            for half, s in group:
                ref, low_row = sources[half]
                spot = half * seq + s
                k_side = jnp.concatenate([ref[s, low_row : low_row + HD, :], k_aug_ref[spot]], axis=0)
                score = dot(q_side, k_side, NN)
                if edge_tile or s in (0, seq - 1):
                    score = jnp.where(q_doc == k_doc_ref[spot], score, FLOOR_SCORE)
                parts.append(score)
            peak = functools.reduce(jnp.maximum, parts)
            fresh = jnp.maximum(top, jnp.max(peak, axis=-1, keepdims=True))
            shrink = jnp.exp(top - fresh)
            probs = [jnp.exp(part - fresh) for part in parts]
            total = total * shrink + jnp.sum(sum(probs[1:], probs[0]), axis=-1, keepdims=True)
            acc = acc * shrink
            for prob, (half, s) in zip(probs, group):
                ref, low_row = sources[half]
                values = ref[s, low_row + HD : low_row + 2 * HD, :]
                acc = acc + dot(prob.astype(LOW), values, NT)
            top = fresh
        result = acc / total
        lse = jnp.broadcast_to(top + jnp.log(total), (cols, HD))
        both = jnp.concatenate([result, lse], axis=1).T
        out_ref[0] = both[:HD]
        lse_ref[0] = both[HD : HD + 8]

    edge = jnp.logical_or(tile == 0, tile == seq - 1)
    pl.when(edge)(lambda: run(True))
    pl.when(jnp.logical_not(edge))(lambda: run(False))


def split_rows(row, rows):
    one = row.astype(LOW).astype(jnp.float32)
    two = (row - one).astype(LOW).astype(jnp.float32)
    three = row - one - two
    pad = jnp.zeros((rows - 3, row.shape[-1]), jnp.float32)
    return jnp.concatenate([one, two, three, pad], axis=0).astype(LOW)


def backward_kernel(
    first_ref, q_ref, q_aug_ref, q_doc_ref, lse_ref, out_ref, grad_ref,
    own_ref, sib_ref, k_aug_ref, k_doc_ref,
    dq_ref, dkv_ref, dkv_acc, *, seq,
):
    step = pl.program_id(0)
    tile = first_ref[0] + step
    sources = ((own_ref, HD), (sib_ref, 0))
    cols = q_ref.shape[-1]

    @pl.when(step == 0)
    def _():
        dkv_acc[...] = jnp.zeros_like(dkv_acc)

    q_low = q_ref[0, :HD, :]
    g_low = grad_ref[0]
    row_dot = jnp.sum(g_low.astype(jnp.float32) * out_ref[0], axis=0, keepdims=True)
    aug = jnp.concatenate(
        [q_aug_ref[0, :32, :], split_rows(-lse_ref[0, :1, :], 16), q_aug_ref[0, 48:, :]], axis=0
    )
    q_side = jnp.concatenate([q_low, aug], axis=0).T
    g_side = jnp.concatenate([g_low, split_rows(-row_dot, HD)], axis=0).T
    ones = jnp.concatenate(
        [jnp.ones((16, cols), LOW), jnp.zeros((HD - 16, cols), LOW)], axis=0
    )

    def run(edge_tile):
        q_doc = q_doc_ref[0]
        dq = jnp.zeros((cols, 2 * HD), jnp.float32)
        for half in range(2):
            ref, low_row = sources[half]
            for s in range(seq):
                spot = half * seq + s
                k_side = jnp.concatenate([ref[s, low_row : low_row + HD, :], k_aug_ref[spot]], axis=0)
                v_side = jnp.concatenate([ref[s, low_row + HD : low_row + 2 * HD, :], ones], axis=0)
                prob = jnp.exp(dot(q_side, k_side, NN))
                if edge_tile or s in (0, seq - 1):
                    prob = jnp.where(q_doc == k_doc_ref[spot], prob, 0.0)
                score_grad = (prob * dot(g_side, v_side, NN)).astype(LOW)
                dq = dq + dot(score_grad, k_side, NT)
                dkv_acc[spot, :HD, :] += dot(q_low, score_grad, NN)
                dkv_acc[spot, HD:, :] += dot(g_low, prob.astype(LOW), NN)
        dq_ref[0] = dq.T

    edge = jnp.logical_or(tile == 0, tile == seq - 1)
    pl.when(edge)(lambda: run(True))
    pl.when(jnp.logical_not(edge))(lambda: run(False))

    @pl.when(step == pl.num_programs(0) - 1)
    def _():
        dkv_ref[...] = dkv_acc[...].astype(LOW)


def whole_spec(array):
    rank = array.ndim
    return pl.BlockSpec(array.shape, lambda i, first: (0,) * rank)


def tile_spec(shape):
    rank = len(shape)
    return pl.BlockSpec((1,) + tuple(shape[1:]), lambda i, first: (i,) + (0,) * (rank - 1))


def attention_forward(first, queries, q_aug, q_doc, own, sib, k_aug, k_doc):
    seq, cols, tiles = own.shape[0], own.shape[2], queries.shape[0]
    return pl.pallas_call(
        functools.partial(forward_kernel, seq=seq, width=4),
        grid_spec=pltpu.PrefetchScalarGridSpec(
            num_scalar_prefetch=1,
            grid=(tiles,),
            in_specs=[tile_spec(member.shape) for member in (queries, q_aug, q_doc)]
            + [whole_spec(member) for member in (own, sib, k_aug, k_doc)],
            out_specs=[tile_spec((tiles, HD, cols)), tile_spec((tiles, 8, cols))],
        ),
        out_shape=[
            jax.ShapeDtypeStruct((tiles, HD, cols), jnp.float32),
            jax.ShapeDtypeStruct((tiles, 8, cols), jnp.float32),
        ],
        compiler_params=pltpu.CompilerParams(vmem_limit_bytes=VMEM_LIMIT),
        name="attention_forward",
    )(first, queries, q_aug, q_doc, own, sib, k_aug, k_doc)


def attention_backward(first, queries, q_aug, q_doc, lse, out, grad, own, sib, k_aug, k_doc):
    seq, cols, tiles = own.shape[0], own.shape[2], queries.shape[0]
    dkv_shape = (2 * seq, 2 * HD, cols)
    return pl.pallas_call(
        functools.partial(backward_kernel, seq=seq),
        grid_spec=pltpu.PrefetchScalarGridSpec(
            num_scalar_prefetch=1,
            grid=(tiles,),
            in_specs=[
                tile_spec(member.shape) for member in (queries, q_aug, q_doc, lse, out, grad)
            ]
            + [whole_spec(member) for member in (own, sib, k_aug, k_doc)],
            out_specs=[
                tile_spec((tiles, 2 * HD, cols)),
                pl.BlockSpec(dkv_shape, lambda i, first: (0, 0, 0)),
            ],
            scratch_shapes=[pltpu.VMEM(dkv_shape, jnp.float32)],
        ),
        out_shape=[
            jax.ShapeDtypeStruct((tiles, 2 * HD, cols), jnp.float32),
            jax.ShapeDtypeStruct(dkv_shape, LOW),
        ],
        compiler_params=pltpu.CompilerParams(vmem_limit_bytes=VMEM_LIMIT),
        name="attention_backward",
    )(first, queries, q_aug, q_doc, lse, out, grad, own, sib, k_aug, k_doc)


def silu_parts(gate):
    sigmoid = 1.0 / (1.0 + jnp.exp(-gate))
    return sigmoid, gate * sigmoid


def ffn_forward_kernel(x_ref, w_ref, both_ref, hidden_ref, out_ref, *, unit_rows, down_rows, unit_steps):
    step = pl.program_id(0)
    groups = w_ref.shape[0]

    @pl.when(step < unit_steps)
    def _():
        for place in range(w_ref.shape[1] // unit_rows):
            matrix = w_ref[:, place * unit_rows : (place + 1) * unit_rows, :].reshape(-1, BLOCK)
            both = dot(x_ref[...], matrix, NN)
            both_ref[place] = both
            half = BLOCK // 2
            hidden = silu_parts(both[:, :half])[1] * both[:, half:]
            spot = step * (w_ref.shape[1] // unit_rows) + place
            hidden_ref[:, pl.ds(pl.multiple_of(spot * half, half), half)] = hidden.astype(LOW)

    @pl.when(step >= unit_steps)
    def _():
        for place in range(w_ref.shape[1] // down_rows):
            matrix = w_ref[:, place * down_rows : (place + 1) * down_rows, :].reshape(-1, BLOCK)
            out_ref[:, place * BLOCK : (place + 1) * BLOCK] = dot(hidden_ref[...], matrix, NN)


def ffn_backward_kernel(
    g_ref, w_ref, both_ref, grads_ref, inner_ref, hidden_grad, *, unit_rows, down_rows, down_steps
):
    step = pl.program_id(0)
    half = BLOCK // 2

    @pl.when(step == 0)
    def _():
        hidden_grad[...] = jnp.zeros_like(hidden_grad)
        inner_ref[...] = jnp.zeros_like(inner_ref)

    @pl.when(step < down_steps)
    def _():
        for place in range(w_ref.shape[1] // down_rows):
            matrix = w_ref[:, place * down_rows : (place + 1) * down_rows, :].reshape(-1, BLOCK)
            part = g_ref[:, place * BLOCK : (place + 1) * BLOCK]
            hidden_grad[...] += dot(part, matrix, NT)

    @pl.when(step >= down_steps)
    def _():
        count = w_ref.shape[1] // unit_rows
        total = inner_ref[...]
        for place in range(count):
            matrix = w_ref[:, place * unit_rows : (place + 1) * unit_rows, :].reshape(-1, BLOCK)
            spot = (step - down_steps) * count + place
            gate, upward = both_ref[place, :, :half], both_ref[place, :, half:]
            above = hidden_grad[:, pl.ds(pl.multiple_of(spot * half, half), half)]
            sigmoid, silu = silu_parts(gate)
            grad_gate = above * upward * (sigmoid * (1.0 + gate * (1.0 - sigmoid)))
            grads = jnp.concatenate([grad_gate, above * silu], axis=1).astype(LOW)
            grads_ref[place] = grads
            total = total + dot(grads, matrix, NT)
        inner_ref[...] = total


def ffn_sizes(packed_shape, cols_ff, unit_rows, down_rows):
    rows = 2 * down_rows
    return rows, 2 * cols_ff // BLOCK * unit_rows // rows, D // BLOCK * down_rows // rows


def ffn_forward(x, packed, cols_ff, unit_rows, down_rows):
    groups, tokens = packed.shape[0], x.shape[0]
    rows, unit_steps, down_steps = ffn_sizes(packed.shape, cols_ff, unit_rows, down_rows)
    per_unit, per_down = rows // unit_rows, rows // down_rows
    last = unit_steps - 1
    return pl.pallas_call(
        functools.partial(
            ffn_forward_kernel, unit_rows=unit_rows, down_rows=down_rows, unit_steps=unit_steps
        ),
        grid=(unit_steps + down_steps,),
        in_specs=[
            pl.BlockSpec(x.shape, lambda i: (0, 0)),
            pl.BlockSpec((groups, rows, BLOCK), lambda i: (0, i, 0)),
        ],
        out_specs=[
            pl.BlockSpec((per_unit, tokens, BLOCK), lambda i: (jnp.minimum(i, last), 0, 0)),
            pl.BlockSpec((tokens, cols_ff), lambda i: (0, 0)),
            pl.BlockSpec((tokens, per_down * BLOCK), lambda i: (0, jnp.maximum(i - unit_steps, 0))),
        ],
        out_shape=[
            jax.ShapeDtypeStruct((per_unit * unit_steps, tokens, BLOCK), jnp.float32),
            jax.ShapeDtypeStruct((tokens, cols_ff), LOW),
            jax.ShapeDtypeStruct((tokens, D), jnp.float32),
        ],
        compiler_params=pltpu.CompilerParams(vmem_limit_bytes=VMEM_LIMIT),
        name="ffn_forward",
    )(x, packed)


def ffn_backward(grad, packed, both, cols_ff, unit_rows, down_rows):
    groups, tokens = packed.shape[0], grad.shape[0]
    rows, unit_steps, down_steps = ffn_sizes(packed.shape, cols_ff, unit_rows, down_rows)
    per_unit, per_down = rows // unit_rows, rows // down_rows
    steps = unit_steps + down_steps
    unit_spec = pl.BlockSpec(
        (per_unit, tokens, BLOCK), lambda i: (jnp.maximum(i - down_steps, 0), 0, 0)
    )
    return pl.pallas_call(
        functools.partial(
            ffn_backward_kernel, unit_rows=unit_rows, down_rows=down_rows, down_steps=down_steps
        ),
        grid=(steps,),
        in_specs=[
            pl.BlockSpec(
                (tokens, per_down * BLOCK), lambda i: (0, jnp.minimum(i, down_steps - 1))
            ),
            pl.BlockSpec((groups, rows, BLOCK), lambda i: (0, (i + unit_steps) % steps, 0)),
            unit_spec,
        ],
        out_specs=[unit_spec, pl.BlockSpec((tokens, D), lambda i: (0, 0))],
        out_shape=[
            jax.ShapeDtypeStruct((per_unit * unit_steps, tokens, BLOCK), LOW),
            jax.ShapeDtypeStruct((tokens, D), jnp.float32),
        ],
        scratch_shapes=[pltpu.VMEM((tokens, cols_ff), jnp.float32)],
        compiler_params=pltpu.CompilerParams(vmem_limit_bytes=VMEM_LIMIT),
        name="ffn_backward",
    )(grad, packed, both)


def weight_grad_kernel(left_ref, right_ref, *refs, rows, kind):
    out_ref = refs[-1]
    for place in range(out_ref.shape[1] // rows):
        if kind == "blocks":
            grad = dot(left_ref[...], right_ref[place], NN)
        elif kind == "columns":
            grad = dot(left_ref[...], right_ref[:, place * BLOCK : (place + 1) * BLOCK], NN)
        else:
            grad = dot(left_ref[...], right_ref[place * BLOCK : (place + 1) * BLOCK, :], NT)
        out_ref[:, place * rows : (place + 1) * rows, :] = grad.reshape(-1, rows, BLOCK).astype(LOW)


def weight_grad(buffer, total_rows, left, right, kind, rows, start, per_step):
    tokens = left.shape[1]
    groups = left.shape[0] // rows
    if kind == "blocks":
        count = right.shape[0]
        right_spec = pl.BlockSpec((per_step, tokens, BLOCK), lambda i: (i, 0, 0))
    elif kind == "columns":
        count = right.shape[1] // BLOCK
        right_spec = pl.BlockSpec((tokens, per_step * BLOCK), lambda i: (0, i))
    else:
        count = right.shape[0] // BLOCK
        right_spec = pl.BlockSpec((per_step * BLOCK, tokens), lambda i: (i, 0))
    first = start // (per_step * rows)
    operands, specs = [left, right], [pl.BlockSpec(left.shape, lambda i: (0, 0)), right_spec]
    if buffer is not None:
        operands.append(buffer)
        specs.append(pl.BlockSpec(memory_space=pl.ANY))
    return pl.pallas_call(
        functools.partial(weight_grad_kernel, rows=rows, kind=kind),
        grid=(count // per_step,),
        in_specs=specs,
        out_specs=pl.BlockSpec((groups, per_step * rows, BLOCK), lambda i: (0, first + i, 0)),
        out_shape=jax.ShapeDtypeStruct((groups, total_rows, BLOCK), LOW),
        input_output_aliases={} if buffer is None else {2: 0},
        compiler_params=pltpu.CompilerParams(vmem_limit_bytes=VMEM_LIMIT),
        name="weight_grad_" + kind,
    )(*operands)


def on_device(
    tokens,
    w_query,
    w_key,
    w_value,
    w_out,
    w_gate,
    w_up,
    w_down,
    gain_attn,
    gain_ffn,
    variate_bias,
    doc_starts,
    variate_ids,
    time_ids,
    cotangent,
):
    seq = lax.axis_size("seq")
    spread = seq // HALF_HEADS
    tiles = seq // spread
    tok_rows = tokens.shape[0]
    cols = 2 * tok_rows
    all_rows = variate_ids.shape[0]
    w_rows = w_query.shape[1]
    d_rows = w_down.shape[1]
    padded = -(-d_rows // 16) * 16
    half_ff = 2 * seq * padded
    half_width = HALF_HEADS * HD
    split_heads = 2 * w_rows == HD
    here_seq = lax.axis_index("seq")
    here_y = lax.axis_index("head") // 2
    here_core = lax.axis_index("head") % 2
    head_slot = here_seq // spread
    my_head = 2 * head_slot + here_y
    first_tile = (here_seq % spread) * tiles
    first = jnp.reshape(first_tile, (1,)).astype(jnp.int32)
    row_groups = [
        [4 * s + 2 * y + core for s in range(seq) for core in range(2)] for y in range(2)
    ]
    y_zero = here_y == 0
    core_zero = here_core == 0

    def swap_y(value):
        return lax.ppermute(value, "head", Y_SWAP)

    def beside(value):
        return jnp.concatenate([value, swap_y(value)], axis=0)

    def fold(partial):
        sent = swap_y(partial[tok_rows:].astype(LOW))
        return partial[:tok_rows] + sent.astype(jnp.float32)

    def cross_rows(parts):
        straight = jnp.where(core_zero, parts[0], parts[1])
        crossed = jnp.where(core_zero, parts[1], parts[0])
        straight = lax.ppermute(straight, "head", TRANSPOSE)
        crossed = lax.ppermute(crossed, "head", ANTI_TRANSPOSE)
        return jnp.where(
            y_zero,
            jnp.concatenate([straight, crossed], axis=0),
            jnp.concatenate([crossed, straight], axis=0),
        )

    def cross_back(pair):
        low_part, high_part = pair[:w_rows], pair[w_rows:]
        straight = jnp.where(y_zero, low_part, high_part)
        crossed = jnp.where(y_zero, high_part, low_part)
        straight = lax.ppermute(straight, "head", TRANSPOSE)
        crossed = lax.ppermute(crossed, "head", [(b, a) for a, b in ANTI_TRANSPOSE])
        return jnp.stack(
            [
                jnp.where(core_zero, straight, crossed),
                jnp.where(core_zero, crossed, straight),
            ]
        ).astype(jnp.float32)

    def gather(part):
        return lax.all_gather(part, BOTH, axis=0, tiled=True, axis_index_groups=row_groups)

    def blocks_of(matrix):
        rows, n = matrix.shape
        return matrix.reshape(rows, n // BLOCK, BLOCK).transpose(1, 0, 2).reshape(-1, BLOCK)

    def from_blocks(packed, rows):
        groups, count = packed.shape[0], packed.shape[1] // rows
        parts = packed.reshape(groups, count, rows, BLOCK).transpose(0, 2, 1, 3)
        return parts.reshape(groups * rows, count * BLOCK)

    def scatter(packed):
        part = lax.psum_scatter(
            packed.reshape(-1, packed.shape[-1]),
            BOTH,
            scatter_dimension=0,
            tiled=True,
            axis_index_groups=row_groups,
        )
        return part

    def split_qkv(query, key, value):
        stacked = jnp.stack([query, key, value], axis=0).reshape(3, w_rows, HALF_HEADS, 2, HD)
        return stacked.transpose(3, 1, 2, 0, 4).reshape(2, w_rows, 3 * half_width)

    def join_qkv(parts):
        parts = parts.reshape(2, w_rows, HALF_HEADS, 3, HD)
        return parts.transpose(3, 1, 2, 0, 4).reshape(3, w_rows, D)

    def split_units(gate, upward):
        def halves(matrix):
            parts = matrix.reshape(w_rows, seq, 2, 2, d_rows).transpose(2, 0, 1, 3, 4)
            parts = jnp.pad(parts, ((0, 0),) * 4 + ((0, padded - d_rows),))
            return parts.reshape(2, w_rows, -1, 1, BLOCK // 2)

        both = jnp.concatenate([halves(gate), halves(upward)], axis=3)
        return both.reshape(2, w_rows, 2 * half_ff)

    def join_units(parts):
        parts = parts.reshape(2, w_rows, -1, 2, BLOCK // 2)

        def joined(half):
            half = half.reshape(2, w_rows, seq, 2, padded)[..., :d_rows]
            return half.transpose(1, 2, 0, 3, 4).reshape(w_rows, 4 * seq * d_rows)

        return joined(parts[:, :, :, 0]), joined(parts[:, :, :, 1])

    def whole_out(part):
        matrix = lax.all_gather(part, BOTH, axis=0, tiled=True).reshape(HALF_HEADS, 2, HD, D)
        return lax.dynamic_index_in_dim(matrix, here_y, 1, keepdims=False).reshape(half_width, D)

    def whole_out_back(grad):
        spaced = lax.dynamic_update_slice_in_dim(
            jnp.zeros((HALF_HEADS, 2, HD, D), LOW),
            grad.astype(LOW).reshape(HALF_HEADS, 1, HD, D),
            here_y,
            1,
        )
        return lax.psum_scatter(spaced.reshape(D, D), BOTH, scatter_dimension=0, tiled=True)

    pair_rows = 2 * w_rows
    unit_end = 2 * half_ff // BLOCK * pair_rows
    ffn_end = unit_end + D // BLOCK * padded
    out_end = ffn_end + (D // BLOCK * w_rows if split_heads else 0)
    qkv_end = out_end + 3 * half_width // BLOCK * pair_rows
    layer_weights = []
    for layer in range(LAYERS):
        scale_attn = gain_attn[layer][:, None]
        scale_ffn = gain_ffn[layer][:, None]
        qkv_parts = split_qkv(
            (w_query[layer] * scale_attn).astype(LOW),
            (w_key[layer] * scale_attn).astype(LOW),
            (w_value[layer] * scale_attn).astype(LOW),
        )
        units_part = cross_rows(
            split_units(
                (w_gate[layer] * scale_ffn).astype(LOW), (w_up[layer] * scale_ffn).astype(LOW)
            )
        )
        out_part = w_out[layer].astype(LOW)
        down_part = jnp.pad(w_down[layer].astype(LOW), ((0, padded - d_rows), (0, 0)))
        qkv_matrix = gather(cross_rows(qkv_parts))
        members = [blocks_of(units_part), blocks_of(down_part)]
        if split_heads:
            members.append(blocks_of(out_part))
        packed = gather(jnp.concatenate(members, axis=0)).reshape(2 * seq, -1, BLOCK)
        if split_heads:
            out_matrix = from_blocks(packed[:, ffn_end:], w_rows)
        else:
            out_matrix = whole_out(out_part)
        layer_weights.append((qkv_matrix, out_matrix, packed))

    def placed_ids(ids):
        ids = ids.reshape(seq, 2, 2, tok_rows)
        ids = jnp.where(y_zero, ids, ids[:, ::-1])
        ids = jnp.where(core_zero, ids, ids[:, :, ::-1])
        return ids.transpose(2, 0, 1, 3).reshape(2 * seq, cols)

    def my_tiles(value):
        if spread == 1:
            return value
        return lax.dynamic_slice_in_dim(value, first_tile, tiles, 0)

    positions = jnp.arange(all_rows, dtype=jnp.int32)
    doc_ids = jnp.sum((doc_starts[None, :] <= positions[:, None]).astype(jnp.int32), axis=1)
    docs = placed_ids(doc_ids)
    variates = placed_ids(variate_ids)
    k_doc = docs[:, None, :]
    q_doc = my_tiles(docs[:seq])[:, :, None]
    q_variates = my_tiles(variates[:seq])
    extra_row = jnp.arange(HD, dtype=jnp.int32)[None, :, None]

    def one_hot(ids):
        return ids[:, None, :] == extra_row % VARIATES

    ones_row = (extra_row == 16) | (extra_row == 17) | ((extra_row >= 32) & (extra_row < 35))
    k_aug = jnp.where(one_hot(variates) & (extra_row < 16) | ones_row, 1.0, 0.0).astype(LOW)

    def query_extra(layer):
        same, other = variate_bias[layer, 0, my_head], variate_bias[layer, 1, my_head]
        gap = same - other
        gap_lead, other_lead = (part.astype(LOW).astype(jnp.float32) for part in (gap, other))
        gap_part = jnp.where(extra_row < VARIATES, gap_lead, gap - gap_lead)
        other_part = jnp.where(extra_row == 16, other_lead, other - other_lead)
        spread_gap = jnp.where(one_hot(q_variates), gap_part, 0.0)
        tail = jnp.where(extra_row < 18, other_part, 0.0)
        return jnp.where(extra_row < 16, spread_gap, tail).astype(LOW)

    q_augs = [query_extra(layer) for layer in range(LAYERS)]
    q_onehots = (q_variates[:, None, :] == jnp.arange(VARIATES, dtype=jnp.int32)[:, None]).astype(
        jnp.float32
    )

    def normalize(values):
        inverse = lax.rsqrt(jnp.mean(values * values, axis=-1, keepdims=True) + NORM_EPS)
        return values * inverse, inverse

    def normalize_back(scaled, inverse, inner):
        return inverse * (inner - scaled * jnp.mean(inner * scaled, axis=-1, keepdims=True))

    half_dim = HD // 2
    frequency = jnp.exp(jnp.arange(half_dim).astype(jnp.float32) * (-2.0 * math.log(10000.0) / HD))
    times = beside(time_ids.astype(jnp.float32))
    angles = frequency[:, None] * times[None, :]
    cosines, sines = jnp.cos(angles), jnp.sin(angles)
    start_scaled, start_inverse = normalize(tokens)
    start_normed = beside(start_scaled.astype(LOW))
    start_normed, k_aug, k_doc, q_doc, cosines, sines, *q_augs = lax.optimization_barrier(
        (start_normed, k_aug, k_doc, q_doc, cosines, sines, *q_augs)
    )

    def rotate(values, sines):
        former, latter = values[:, :half_dim], values[:, half_dim:]
        return jnp.concatenate(
            [former * cosines - latter * sines, latter * cosines + former * sines], axis=1
        )

    def to_heads(value):
        if spread > 1:
            value = jnp.repeat(value, spread, axis=0)
        return lax.all_to_all(value, "seq", split_axis=0, concat_axis=0, tiled=True)

    def from_heads(value, whole):
        if spread > 1 and not whole:
            value = lax.dynamic_update_slice_in_dim(
                jnp.zeros((seq,) + value.shape[1:], value.dtype), value, first_tile, 0
            )
        value = lax.all_to_all(value, "seq", split_axis=0, concat_axis=0, tiled=True)
        if spread > 1:
            value = value.reshape((HALF_HEADS, spread) + value.shape[1:])
            value = jnp.sum(value.astype(jnp.float32), axis=1).astype(LOW)
        return value

    stream = tokens
    saved = []
    for layer in range(LAYERS):
        qkv_matrix, out_matrix, packed = layer_weights[layer]
        if layer == 0:
            scaled_one, inverse_one, normed = start_scaled, start_inverse, start_normed
        else:
            scaled_one, inverse_one = normalize(stream)
            normed = beside(scaled_one.astype(LOW))
        projected = dot(qkv_matrix, normed, TT).reshape(HALF_HEADS, 3 * HD, cols)
        query = rotate(projected[:, :HD], sines) * (1.0 / math.sqrt(HD))
        key = rotate(projected[:, HD : 2 * HD], sines)
        sent = jnp.concatenate([query, key, projected[:, 2 * HD :]], axis=1).astype(LOW)
        own = to_heads(sent)
        sib = lax.ppermute(own[:, HD:], "head", CORE_SWAP)
        queries = my_tiles(own)
        q_aug = q_augs[layer]
        out, lse = attention_forward(first, queries, q_aug, q_doc, own, sib, k_aug, k_doc)
        attended = from_heads(out.astype(LOW), False).reshape(half_width, cols)
        middle = stream + fold(dot(attended, out_matrix, TN))
        scaled_two, inverse_two = normalize(middle)
        normed_ffn = beside(scaled_two.astype(LOW))
        both, hidden, partial = ffn_forward(normed_ffn, packed, half_ff, pair_rows, padded)
        saved.append(
            (
                scaled_one, inverse_one, normed, own, sib, queries, q_aug, out, lse, attended,
                scaled_two, inverse_two, normed_ffn, both, hidden,
            )
        )
        stream = middle + fold(partial)

    upstream = cotangent
    layer_grads = [{} for unused in range(LAYERS)]
    bias_parts = [None] * LAYERS
    buffer, sent_last = None, None
    qkv_grad = None

    for layer in reversed(range(LAYERS)):
        qkv_matrix, out_matrix, packed = layer_weights[layer]
        (
            scaled_one, inverse_one, normed, own, sib, queries, q_aug, out, lse, attended,
            scaled_two, inverse_two, normed_ffn, both, hidden,
        ) = saved[layer]
        upstream_low = beside(upstream.astype(LOW))
        grad_units, partial = ffn_backward(upstream_low, packed, both, half_ff, pair_rows, padded)
        inner = fold(partial)
        total_rows = qkv_end if layer < LAYERS - 1 else out_end
        buffer = weight_grad(
            buffer, total_rows, normed_ffn.T, grad_units, "blocks", pair_rows, 0, 2 * padded // pair_rows
        )
        buffer = weight_grad(
            buffer, total_rows, hidden.T, upstream_low, "columns", padded, unit_end, 2
        )
        grad_middle = upstream + normalize_back(scaled_two, inverse_two, inner)
        middle_low = beside(grad_middle.astype(LOW))
        grad_attended = dot(out_matrix, middle_low, NT).astype(LOW)
        if split_heads:
            buffer = weight_grad(
                buffer, total_rows, attended, middle_low, "columns", w_rows, ffn_end, D // BLOCK
            )
        else:
            layer_grads[layer]["out"] = whole_out_back(dot(attended, middle_low, NN))
        if sent_last is not None:
            buffer, sent_last = lax.optimization_barrier((buffer, sent_last))
            layer_grads[layer + 1]["sent"] = sent_last
        buffer, grad_attended = lax.optimization_barrier((buffer, grad_attended))
        sent_last = scatter(buffer)
        out_grad = my_tiles(to_heads(grad_attended.reshape(HALF_HEADS, HD, cols)))
        grad_q, grad_kv = attention_backward(
            first, queries, q_aug, q_doc, lse, out, out_grad, own, sib, k_aug, k_doc
        )
        same_grad = jnp.sum(grad_q[:, HD : HD + VARIATES] * q_onehots)
        all_grad = jnp.sum(grad_q[:, HD + 16])
        crossed = lax.ppermute(grad_kv[seq:], "head", CORE_SWAP)
        grad_kv = (grad_kv[:seq].astype(jnp.float32) + crossed.astype(jnp.float32)).astype(LOW)
        grad_q = (grad_q[:, :HD] * (1.0 / math.sqrt(HD))).astype(LOW)
        if spread > 1:
            grad_q = lax.dynamic_update_slice_in_dim(
                jnp.zeros((seq, HD, cols), LOW), grad_q, first_tile, 0
            )
        grad_heads = from_heads(jnp.concatenate([grad_q, grad_kv], axis=1), True)
        grad_heads = jnp.concatenate(
            [
                rotate(grad_heads[:, :HD].astype(jnp.float32), -sines).astype(LOW),
                rotate(grad_heads[:, HD : 2 * HD].astype(jnp.float32), -sines).astype(LOW),
                grad_heads[:, 2 * HD :],
            ],
            axis=1,
        ).reshape(3 * half_width, cols)
        bias_parts[layer] = jnp.stack([same_grad, all_grad - same_grad])
        if layer > 0:
            buffer = weight_grad(
                None, qkv_end, normed.T, grad_heads, "rows", pair_rows, out_end, 2
            )
        else:
            qkv_grad = dot(normed, grad_heads, TT).astype(LOW)
            qkv_grad, grad_heads, *bias_parts = lax.optimization_barrier(
                (qkv_grad, grad_heads, *bias_parts)
            )
            qkv_grad, sent_last = lax.optimization_barrier((qkv_grad, sent_last))
            layer_grads[0]["sent"] = sent_last
            qkv_grad = scatter(qkv_grad)
        inner = fold(dot(grad_heads, qkv_matrix, TT))
        upstream = grad_middle + normalize_back(scaled_one, inverse_one, inner)

    bias_local = lax.dynamic_update_slice(
        jnp.zeros((LAYERS, 2, HEADS), jnp.float32), jnp.stack(bias_parts)[:, :, None], (0, 0, my_head)
    )
    bias_total = bias_local
    for axis, size in (("head", 4), ("seq", seq)):
        hop = 1
        while hop < size:
            swap = [(place, place ^ hop) for place in range(size)]
            bias_total = bias_total + lax.ppermute(bias_total, axis, swap)
            hop *= 2

    finished = []
    for layer in range(LAYERS):
        sent = layer_grads[layer]["sent"]
        if layer < LAYERS - 1:
            above = sent[out_end:]
            layer_grads[layer + 1]["qkv"] = from_blocks(above[None], pair_rows)
        units_part = from_blocks(sent[None, :unit_end], pair_rows)
        gate_grad, up_grad = join_units(cross_back(units_part))
        down_grad = from_blocks(sent[None, unit_end:ffn_end], padded)[:d_rows].astype(jnp.float32)
        if split_heads:
            out_grad = from_blocks(sent[None, ffn_end:out_end], w_rows)
        else:
            out_grad = layer_grads[layer]["out"]
        qkv_part = qkv_grad if layer == 0 else layer_grads[layer]["qkv"]
        qkv_grads = join_qkv(cross_back(qkv_part))
        gain_one = sum(
            jnp.sum(qkv_grads[place] * member[layer], axis=1)
            for place, member in enumerate((w_query, w_key, w_value))
        )
        gain_two = jnp.sum(gate_grad * w_gate[layer] + up_grad * w_up[layer], axis=1)
        scale_attn = gain_attn[layer][:, None]
        scale_ffn = gain_ffn[layer][:, None]
        finished.append(
            (
                qkv_grads[0] * scale_attn,
                qkv_grads[1] * scale_attn,
                qkv_grads[2] * scale_attn,
                out_grad.astype(jnp.float32),
                gate_grad * scale_ffn,
                up_grad * scale_ffn,
                down_grad,
                gain_one,
                gain_two,
            )
        )
    stacked = [jnp.stack([finished[layer][place] for layer in range(LAYERS)]) for place in range(9)]
    return (stream, upstream, *stacked, bias_total)


def solution(mesh):
    rows = P(BOTH, None)
    middle = P(None, BOTH, None)
    gains = P(None, BOTH)
    return jax.shard_map(
        on_device,
        mesh=mesh,
        in_specs=(rows,) + (middle,) * 7 + (gains,) * 2 + (P(),) * 3 + (P(BOTH), rows),
        out_specs=(rows, rows) + (middle,) * 7 + (gains,) * 2 + (P(),),
        check_vma=False,
    )
```

```python
import functools
import math

import jax
import jax.numpy as jnp
from jax import lax
from jax.experimental import pallas as pl
from jax.experimental.pallas import tpu as pltpu
from jax.sharding import PartitionSpec as P

D = 1024
HEADS = 16
HD = 64
LAYERS = 2
VARIATES = 8
BLOCK = 256

NORM_EPS = 1e-05
FLOOR_SCORE = -1e30
LOW = jnp.bfloat16
BOTH = ("seq", "head")

QUARTERS = 4
QUARTER_HEADS = HEADS // QUARTERS
Q_TILE = 256
Y_SWAP = [(place, place ^ 2) for place in range(4)]
CORE_SWAP = [(place, place ^ 1) for place in range(4)]

NN = (((1,), (0,)), ((), ()))
NT = (((1,), (1,)), ((), ()))
TN = (((0,), (0,)), ((), ()))
TT = (((0,), (1,)), ((), ()))
VMEM_LIMIT = 56 * 1024 * 1024


def cost(flops, operands, results, transcendentals=0):
    moved = sum(member.size * member.dtype.itemsize for member in [*operands, *results])
    return pl.CostEstimate(flops=flops, bytes_accessed=moved, transcendentals=transcendentals)


def dot(left, right, dims):
    return lax.dot_general(left, right, dims, preferred_element_type=jnp.float32)


def forward_kernel(q_ref, q_aug_ref, own_ref, sib_ref, k_aug_ref, out_ref, lse_ref, *, width):
    blocks = own_ref.shape[0]
    sources = ((own_ref, HD), (sib_ref, 0))
    spots = [(half, block) for half in range(2) for block in range(blocks)]
    cols = q_ref.shape[-1]
    q_side = jnp.concatenate([q_ref[0, :HD, :], q_aug_ref[0]], axis=0).T
    top = jnp.full((cols, 1), FLOOR_SCORE, jnp.float32)
    total = jnp.zeros((cols, 1), jnp.float32)
    acc = jnp.zeros((cols, HD), jnp.float32)
    for start in range(0, len(spots), width):
        group = spots[start : start + width]
        parts = []
        for half, block in group:
            ref, low_row = sources[half]
            extra = k_aug_ref[half * blocks + block]
            k_side = jnp.concatenate([ref[block, low_row : low_row + HD, :], extra], axis=0)
            parts.append(dot(q_side, k_side, NN))
        peak = functools.reduce(jnp.maximum, parts)
        fresh = jnp.maximum(top, jnp.max(peak, axis=-1, keepdims=True))
        shrink = jnp.exp(top - fresh)
        probs = [jnp.exp(part - fresh) for part in parts]
        total = total * shrink + jnp.sum(sum(probs[1:], probs[0]), axis=-1, keepdims=True)
        acc = acc * shrink
        for prob, (half, block) in zip(probs, group):
            ref, low_row = sources[half]
            values = ref[block, low_row + HD : low_row + 2 * HD, :]
            acc = acc + dot(prob.astype(LOW), values, NT)
        top = fresh
    result = acc / total
    lse = jnp.broadcast_to(top + jnp.log(total), (cols, HD))
    both = jnp.concatenate([result, lse], axis=1).T
    out_ref[0] = both[:HD].astype(LOW)
    lse_ref[0] = both[HD : HD + 8]


def split_rows(row, rows):
    one = row.astype(LOW).astype(jnp.float32)
    two = (row - one).astype(LOW).astype(jnp.float32)
    three = row - one - two
    pad = jnp.zeros((rows - 3, row.shape[-1]), jnp.float32)
    return jnp.concatenate([one, two, three, pad], axis=0).astype(LOW)


def backward_kernel(
    q_ref, q_aug_ref, lse_ref, out_ref, grad_ref, own_ref, sib_ref, k_aug_ref, dq_ref, dkv_ref, dkv_acc
):
    step = pl.program_id(0)
    blocks = own_ref.shape[0]
    sources = ((own_ref, HD), (sib_ref, 0))
    cols, key_cols = q_ref.shape[-1], own_ref.shape[-1]

    @pl.when(step == 0)
    def _():
        dkv_acc[...] = jnp.zeros_like(dkv_acc)

    q_low = q_ref[0, :HD, :]
    g_low = grad_ref[0]
    row_dot = jnp.sum(
        g_low.astype(jnp.float32) * out_ref[0].astype(jnp.float32), axis=0, keepdims=True
    )
    aug = jnp.concatenate(
        [q_aug_ref[0, :32, :], split_rows(-lse_ref[0, :1, :], 16), q_aug_ref[0, 48:, :]], axis=0
    )
    q_side = jnp.concatenate([q_low, aug], axis=0).T
    g_side = jnp.concatenate([g_low, split_rows(-row_dot, HD)], axis=0).T
    ones = jnp.concatenate(
        [jnp.ones((16, key_cols), LOW), jnp.zeros((HD - 16, key_cols), LOW)], axis=0
    )
    dq = jnp.zeros((cols, 2 * HD), jnp.float32)
    for half in range(2):
        ref, low_row = sources[half]
        for block in range(blocks):
            spot = half * blocks + block
            k_side = jnp.concatenate(
                [ref[block, low_row : low_row + HD, :], k_aug_ref[spot]], axis=0
            )
            v_side = jnp.concatenate([ref[block, low_row + HD : low_row + 2 * HD, :], ones], axis=0)
            prob = jnp.exp(dot(q_side, k_side, NN))
            score_grad = (prob * dot(g_side, v_side, NN)).astype(LOW)
            dq = dq + dot(score_grad, k_side, NT)
            dkv_acc[spot, :HD, :] += dot(q_low, score_grad, NN)
            dkv_acc[spot, HD:, :] += dot(g_low, prob.astype(LOW), NN)
    dq_ref[0] = dq.T

    @pl.when(step == pl.num_programs(0) - 1)
    def _():
        dkv_ref[...] = dkv_acc[...].astype(LOW)


def whole_spec(array):
    rank = array.ndim
    return pl.BlockSpec(array.shape, lambda i: (0,) * rank)


def tile_spec(rows, cols):
    cuts = cols // Q_TILE
    return pl.BlockSpec((1, rows, Q_TILE), lambda i: (i // cuts, 0, i % cuts))


def attention_forward(queries, q_aug, own, sib, k_aug):
    tiles, unused, cols = queries.shape
    pairs = 2 * tiles * own.shape[0] * cols * cols
    results = [
        jax.ShapeDtypeStruct((tiles, HD, cols), LOW),
        jax.ShapeDtypeStruct((tiles, 8, cols), jnp.float32),
    ]
    return pl.pallas_call(
        functools.partial(forward_kernel, width=2),
        grid=(tiles * cols // Q_TILE,),
        in_specs=[tile_spec(3 * HD, cols), tile_spec(HD, cols)]
        + [whole_spec(member) for member in (own, sib, k_aug)],
        out_specs=[tile_spec(HD, cols), tile_spec(8, cols)],
        out_shape=results,
        cost_estimate=cost(16 * HD * pairs, [queries, own, sib], results, pairs),
        compiler_params=pltpu.CompilerParams(vmem_limit_bytes=VMEM_LIMIT),
        name="attention_forward",
    )(queries, q_aug, own, sib, k_aug)


def attention_backward(queries, q_aug, lse, out, grad, own, sib, k_aug):
    tiles, unused, cols = queries.shape
    dkv_shape = (2 * own.shape[0], 2 * HD, cols)
    pairs = 2 * tiles * own.shape[0] * cols * cols
    results = [
        jax.ShapeDtypeStruct((tiles, 2 * HD, cols), jnp.float32),
        jax.ShapeDtypeStruct(dkv_shape, LOW),
    ]
    return pl.pallas_call(
        backward_kernel,
        grid=(tiles * cols // Q_TILE,),
        in_specs=[tile_spec(3 * HD, cols), tile_spec(HD, cols), tile_spec(8, cols)]
        + [tile_spec(HD, cols)] * 2
        + [whole_spec(member) for member in (own, sib, k_aug)],
        out_specs=[tile_spec(2 * HD, cols), pl.BlockSpec(dkv_shape, lambda i: (0, 0, 0))],
        out_shape=results,
        cost_estimate=cost(32 * HD * pairs, [queries, own, sib], results, pairs),
        scratch_shapes=[pltpu.VMEM(dkv_shape, jnp.float32)],
        compiler_params=pltpu.CompilerParams(vmem_limit_bytes=VMEM_LIMIT),
        name="attention_backward",
    )(queries, q_aug, lse, out, grad, own, sib, k_aug)


def silu_parts(gate):
    sigmoid = 1.0 / (1.0 + jnp.exp(-gate))
    return sigmoid, gate * sigmoid


def ffn_forward_kernel(x_ref, w_ref, both_ref, hidden_ref, out_ref, *, unit_rows, down_rows, unit_steps):
    step = pl.program_id(0)
    groups = w_ref.shape[0]

    @pl.when(step < unit_steps)
    def _():
        for place in range(w_ref.shape[1] // unit_rows):
            matrix = w_ref[:, place * unit_rows : (place + 1) * unit_rows, :].reshape(-1, BLOCK)
            both = dot(x_ref[...], matrix, NN)
            both_ref[place] = both
            half = BLOCK // 2
            hidden = silu_parts(both[:, :half])[1] * both[:, half:]
            spot = step * (w_ref.shape[1] // unit_rows) + place
            hidden_ref[:, pl.ds(pl.multiple_of(spot * half, half), half)] = hidden.astype(LOW)

    @pl.when(step >= unit_steps)
    def _():
        for place in range(w_ref.shape[1] // down_rows):
            matrix = w_ref[:, place * down_rows : (place + 1) * down_rows, :].reshape(-1, BLOCK)
            out_ref[:, place * BLOCK : (place + 1) * BLOCK] = dot(hidden_ref[...], matrix, NN)


def ffn_backward_kernel(
    g_ref, w_ref, both_ref, grads_ref, inner_ref, hidden_grad, *, unit_rows, down_rows, down_steps
):
    step = pl.program_id(0)
    half = BLOCK // 2

    @pl.when(step == 0)
    def _():
        hidden_grad[...] = jnp.zeros_like(hidden_grad)
        inner_ref[...] = jnp.zeros_like(inner_ref)

    @pl.when(step < down_steps)
    def _():
        for place in range(w_ref.shape[1] // down_rows):
            matrix = w_ref[:, place * down_rows : (place + 1) * down_rows, :].reshape(-1, BLOCK)
            part = g_ref[:, place * BLOCK : (place + 1) * BLOCK]
            hidden_grad[...] += dot(part, matrix, NT)

    @pl.when(step >= down_steps)
    def _():
        count = w_ref.shape[1] // unit_rows
        total = inner_ref[...]
        for place in range(count):
            matrix = w_ref[:, place * unit_rows : (place + 1) * unit_rows, :].reshape(-1, BLOCK)
            spot = (step - down_steps) * count + place
            gate, upward = both_ref[place, :, :half], both_ref[place, :, half:]
            above = hidden_grad[:, pl.ds(pl.multiple_of(spot * half, half), half)]
            sigmoid, silu = silu_parts(gate)
            grad_gate = above * upward * (sigmoid * (1.0 + gate * (1.0 - sigmoid)))
            grads = jnp.concatenate([grad_gate, above * silu], axis=1).astype(LOW)
            grads_ref[place] = grads
            total = total + dot(grads, matrix, NT)
        inner_ref[...] = total


def ffn_sizes(packed_shape, cols_ff, unit_rows, down_rows):
    rows = D // BLOCK * down_rows
    return rows, 2 * cols_ff // BLOCK * unit_rows // rows, D // BLOCK * down_rows // rows


def ffn_forward(x, packed, cols_ff, unit_rows, down_rows):
    groups, tokens = packed.shape[0], x.shape[0]
    rows, unit_steps, down_steps = ffn_sizes(packed.shape, cols_ff, unit_rows, down_rows)
    per_unit, per_down = rows // unit_rows, rows // down_rows
    last = unit_steps - 1
    results = [
        jax.ShapeDtypeStruct((per_unit * unit_steps, tokens, BLOCK), jnp.float32),
        jax.ShapeDtypeStruct((tokens, cols_ff), LOW),
        jax.ShapeDtypeStruct((tokens, D), jnp.float32),
    ]
    return pl.pallas_call(
        functools.partial(
            ffn_forward_kernel, unit_rows=unit_rows, down_rows=down_rows, unit_steps=unit_steps
        ),
        grid=(unit_steps + down_steps,),
        in_specs=[
            pl.BlockSpec(x.shape, lambda i: (0, 0)),
            pl.BlockSpec((groups, rows, BLOCK), lambda i: (0, i, 0)),
        ],
        out_specs=[
            pl.BlockSpec((per_unit, tokens, BLOCK), lambda i: (jnp.minimum(i, last), 0, 0)),
            pl.BlockSpec((tokens, cols_ff), lambda i: (0, 0)),
            pl.BlockSpec((tokens, per_down * BLOCK), lambda i: (0, jnp.maximum(i - unit_steps, 0))),
        ],
        out_shape=results,
        cost_estimate=cost(6 * tokens * D * cols_ff, [x, packed], results),
        compiler_params=pltpu.CompilerParams(vmem_limit_bytes=VMEM_LIMIT),
        name="ffn_forward",
    )(x, packed)


def ffn_backward(grad, packed, both, cols_ff, unit_rows, down_rows):
    groups, tokens = packed.shape[0], grad.shape[0]
    rows, unit_steps, down_steps = ffn_sizes(packed.shape, cols_ff, unit_rows, down_rows)
    per_unit, per_down = rows // unit_rows, rows // down_rows
    steps = unit_steps + down_steps
    results = [
        jax.ShapeDtypeStruct((per_unit * unit_steps, tokens, BLOCK), LOW),
        jax.ShapeDtypeStruct((tokens, D), jnp.float32),
    ]
    unit_spec = pl.BlockSpec(
        (per_unit, tokens, BLOCK), lambda i: (jnp.maximum(i - down_steps, 0), 0, 0)
    )
    return pl.pallas_call(
        functools.partial(
            ffn_backward_kernel, unit_rows=unit_rows, down_rows=down_rows, down_steps=down_steps
        ),
        grid=(steps,),
        in_specs=[
            pl.BlockSpec(
                (tokens, per_down * BLOCK), lambda i: (0, jnp.minimum(i, down_steps - 1))
            ),
            pl.BlockSpec((groups, rows, BLOCK), lambda i: (0, (i + unit_steps) % steps, 0)),
            unit_spec,
        ],
        out_specs=[unit_spec, pl.BlockSpec((tokens, D), lambda i: (0, 0))],
        out_shape=results,
        cost_estimate=cost(6 * tokens * D * cols_ff, [grad, packed, both], results),
        scratch_shapes=[pltpu.VMEM((tokens, cols_ff), jnp.float32)],
        compiler_params=pltpu.CompilerParams(vmem_limit_bytes=VMEM_LIMIT),
        name="ffn_backward",
    )(grad, packed, both)


def weight_grad_kernel(left_ref, right_ref, *refs, rows, kind):
    out_ref = refs[-1]
    for place in range(out_ref.shape[1] // rows):
        if kind == "blocks":
            grad = dot(left_ref[...], right_ref[place], NN)
        elif kind == "columns":
            grad = dot(left_ref[...], right_ref[:, place * BLOCK : (place + 1) * BLOCK], NN)
        else:
            grad = dot(left_ref[...], right_ref[place * BLOCK : (place + 1) * BLOCK, :], NT)
        out_ref[:, place * rows : (place + 1) * rows, :] = grad.reshape(-1, rows, BLOCK).astype(LOW)


def weight_grad(buffer, total_rows, left, right, kind, rows, start, per_step):
    tokens = left.shape[1]
    groups = left.shape[0] // rows
    if kind == "blocks":
        count = right.shape[0]
        right_spec = pl.BlockSpec((per_step, tokens, BLOCK), lambda i: (i, 0, 0))
    elif kind == "columns":
        count = right.shape[1] // BLOCK
        right_spec = pl.BlockSpec((tokens, per_step * BLOCK), lambda i: (0, i))
    else:
        count = right.shape[0] // BLOCK
        right_spec = pl.BlockSpec((per_step * BLOCK, tokens), lambda i: (i, 0))
    first = start // (per_step * rows)
    operands, specs = [left, right], [pl.BlockSpec(left.shape, lambda i: (0, 0)), right_spec]
    if buffer is not None:
        operands.append(buffer)
        specs.append(pl.BlockSpec(memory_space=pl.ANY))
    return pl.pallas_call(
        functools.partial(weight_grad_kernel, rows=rows, kind=kind),
        grid=(count // per_step,),
        in_specs=specs,
        out_specs=pl.BlockSpec((groups, per_step * rows, BLOCK), lambda i: (0, first + i, 0)),
        out_shape=jax.ShapeDtypeStruct((groups, total_rows, BLOCK), LOW),
        input_output_aliases={} if buffer is None else {2: 0},
        cost_estimate=cost(2 * left.size * count * BLOCK, [left, left, right], []),
        compiler_params=pltpu.CompilerParams(vmem_limit_bytes=VMEM_LIMIT),
        name="weight_grad_" + kind,
    )(*operands)


def put_qkv(came_ref, place_ref, start, outs, layer, weights, gain_ref, gain_out_ref):
    for quarter in range(QUARTERS):
        part = came_ref[place_ref[quarter], :, start : start + 3 * QUARTER_HEADS * HD]
        part = part.astype(jnp.float32)
        for slot in range(QUARTER_HEADS):
            column = HD * (QUARTERS * slot + quarter)
            for which, out_ref in enumerate(outs):
                first = (3 * slot + which) * HD
                out_ref[layer, :, column : column + HD] = part[:, first : first + HD]
    gain_grad = 0.0
    for out_ref, weight_ref in zip(outs, weights):
        grad = out_ref[layer]
        gain_grad = gain_grad + jnp.sum(grad * weight_ref[layer], axis=1, keepdims=True)
        out_ref[layer] = grad * gain_ref[layer]
    gain_out_ref[layer] = jnp.broadcast_to(gain_grad, gain_out_ref.shape[1:])


def put_units(came_ref, place_ref, start, outs, layer, weights, gain_ref, gain_out_ref, d_rows, padded, planes):
    half = BLOCK // 2
    for quarter in range(QUARTERS):
        part = came_ref[place_ref[quarter], :, start : start + 4 * planes * padded]
        part = part.astype(jnp.float32)
        for plane in range(planes):
            for core in range(2):
                column = d_rows * (8 * plane + 2 * quarter + core)
                unit, end = (2 * plane + core) * padded, (2 * plane + core) * padded + d_rows
                while unit < end:
                    stop = min(end, (unit // half + 1) * half)
                    for which, out_ref in enumerate(outs):
                        first = unit // half * BLOCK + which * half + unit % half
                        out_ref[layer, :, column : column + stop - unit] = part[
                            :, first : first + stop - unit
                        ]
                    column, unit = column + stop - unit, stop
    gain_grad = 0.0
    for out_ref, weight_ref in zip(outs, weights):
        grad = out_ref[layer]
        gain_grad = gain_grad + jnp.sum(grad * weight_ref[layer], axis=1, keepdims=True)
        out_ref[layer] = grad * gain_ref[layer]
    gain_out_ref[layer] = jnp.broadcast_to(gain_grad, gain_out_ref.shape[1:])


def finish_kernel(place_ref, *refs, ends, w_rows, d_rows, padded, planes, with_out):
    came_ref, *sums = refs[: 1 + LAYERS]
    weights, gains = refs[1 + LAYERS : 6 + LAYERS], refs[6 + LAYERS : 8 + LAYERS]
    outs = refs[8 + LAYERS :]
    units_width = 4 * planes * padded
    for layer in range(LAYERS):
        put_units(
            came_ref, place_ref, layer * units_width, outs[4:6], layer, weights[3:], gains[1],
            outs[8], d_rows, padded, planes,
        )
        if layer > 0:
            start = LAYERS * units_width + (layer - 1) * 3 * QUARTER_HEADS * HD
            put_qkv(came_ref, place_ref, start, outs[:3], layer, weights[:3], gains[0], outs[7])
        for block in range(D // BLOCK):
            lanes = slice(block * BLOCK, (block + 1) * BLOCK)
            rows = sums[layer][ends[0] + block * padded : ends[0] + (block + 1) * padded, :]
            outs[6][layer, :, lanes] = rows.astype(jnp.float32)[:d_rows]
            if with_out:
                rows = sums[layer][ends[1] + block * w_rows : ends[1] + (block + 1) * w_rows, :]
                outs[3][layer, :, lanes] = rows.astype(jnp.float32)


def finish_first_kernel(place_ref, came_ref, *refs):
    weights, gain_ref, outs, gain_out_ref = refs[:3], refs[3], refs[8:11], refs[11]
    for layer in range(1, LAYERS):
        for have_ref, out_ref in zip(refs[4:8], refs[8:]):
            out_ref[layer] = have_ref[layer]
    put_qkv(came_ref, place_ref, 0, outs, 0, weights, gain_ref, gain_out_ref)


def in_vmem(count):
    return [pl.BlockSpec(memory_space=pltpu.VMEM)] * count


def finish_gradients(place, came, sums, weights, gains, d_shape, ends, planes, with_out):
    layers, w_rows, unused = weights[0].shape
    d_rows = d_shape[1]
    padded = -(-d_rows // 16) * 16
    shapes = [weights[0].shape] * 4 + [weights[3].shape] * 2 + [d_shape] + [(layers, w_rows, 128)] * 2
    return pl.pallas_call(
        functools.partial(
            finish_kernel, ends=ends, w_rows=w_rows, d_rows=d_rows, padded=padded, planes=planes,
            with_out=with_out,
        ),
        in_specs=[pl.BlockSpec(memory_space=pltpu.SMEM)] + in_vmem(8 + LAYERS),
        out_specs=in_vmem(9),
        out_shape=[jax.ShapeDtypeStruct(shape, jnp.float32) for shape in shapes],
        compiler_params=pltpu.CompilerParams(vmem_limit_bytes=VMEM_LIMIT),
        name="finish_gradients",
    )(place, came, *sums, *weights, *gains)


def finish_first(place, came, weights, gain, grads, gain_grad):
    results = [*grads, gain_grad]
    return pl.pallas_call(
        finish_first_kernel,
        in_specs=[pl.BlockSpec(memory_space=pltpu.SMEM)] + in_vmem(9),
        out_specs=in_vmem(4),
        out_shape=[jax.ShapeDtypeStruct(member.shape, jnp.float32) for member in results],
        compiler_params=pltpu.CompilerParams(vmem_limit_bytes=VMEM_LIMIT),
        name="finish_first",
    )(place, came, *weights, gain, *results)


def on_device(
    tokens,
    w_query,
    w_key,
    w_value,
    w_out,
    w_gate,
    w_up,
    w_down,
    gain_attn,
    gain_ffn,
    variate_bias,
    doc_starts,
    variate_ids,
    time_ids,
    cotangent,
):
    seq = lax.axis_size("seq")
    planes = seq // 2
    spread = planes // QUARTER_HEADS
    tiles = planes // spread
    tok_rows = tokens.shape[0]
    cols = 4 * tok_rows
    all_rows = variate_ids.shape[0]
    w_rows = w_query.shape[1]
    d_rows = w_down.shape[1]
    padded = -(-d_rows // 16) * 16
    quarter_ff = 2 * planes * padded
    quarter_width = QUARTER_HEADS * HD
    split_heads = 2 * w_rows == HD
    here_seq, here_head = lax.axis_index("seq"), lax.axis_index("head")
    here_plane, here_lo = here_seq // 2, here_seq % 2
    here_y, here_core = here_head // 2, here_head % 2
    my_quarter = 2 * here_lo + here_y
    my_head = QUARTERS * (here_plane // spread) + my_quarter
    first_tile = (here_plane % spread) * tiles
    devices = [
        (plane, lo, y, core)
        for plane in range(planes)
        for lo in range(2)
        for y in range(2)
        for core in range(2)
    ]

    def place_of(plane, lo, y, core):
        return 8 * plane + 4 * lo + 2 * y + core

    row_groups = [
        [place_of(plane, lo, y, core) for plane in range(planes) for core in range(2)]
        for lo in range(2)
        for y in range(2)
    ]
    plane_groups = [[2 * plane + lo for plane in range(planes)] for lo in range(2)]
    x_swap = [(place, place ^ 1) for place in range(seq)]
    corner_swap = [
        (place_of(plane, lo, y, core), place_of(plane, 1 - lo, 1 - y, core))
        for plane, lo, y, core in devices
    ]

    def neighbours(across_y, across_x, across_both):
        return (
            lax.ppermute(across_y, "head", Y_SWAP),
            lax.ppermute(across_x, "seq", x_swap),
            lax.ppermute(across_both, BOTH, corner_swap),
        )

    def beside(value):
        return jnp.concatenate([value, *neighbours(value, value, value)], axis=0)

    def fold(partial):
        low = partial[tok_rows:].astype(LOW).reshape(3, tok_rows, -1)
        parts = neighbours(low[0], low[1], low[2])
        return partial[:tok_rows] + sum(part.astype(jnp.float32) for part in parts)

    def flip(pair, bit):
        return jnp.where(bit == 0, pair[0], pair[1]), jnp.where(bit == 0, pair[1], pair[0])

    def xor_order(grid, high, low):
        rows = [flip(row, low) for row in grid]
        first, second = zip(*[flip(column, high) for column in zip(*rows)])
        return [list(first), list(second)]

    def cross_rows(parts):
        grid = xor_order([[parts[0], parts[1]], [parts[2], parts[3]]], here_y, here_core)
        came = [[None, None], [None, None]]
        for high in range(2):
            for low in range(2):
                hops = [
                    (place_of(plane, lo, y, core), place_of(plane, y ^ high, core ^ low, lo))
                    for plane, lo, y, core in devices
                ]
                came[high][low] = lax.ppermute(grid[high][low], BOTH, hops)
        came = xor_order(came, here_lo, here_y)
        return jnp.concatenate([*came[0], *came[1]], axis=0)

    def cross_back(rows):
        parts = [rows[place * w_rows : (place + 1) * w_rows] for place in range(4)]
        grid = xor_order([parts[:2], parts[2:]], here_lo, here_y)
        came = [[None, None], [None, None]]
        for high in range(2):
            for low in range(2):
                hops = [
                    (place_of(plane, lo, y, core), place_of(plane, core, lo ^ high, y ^ low))
                    for plane, lo, y, core in devices
                ]
                came[high][low] = lax.ppermute(grid[high][low], BOTH, hops)
        return jnp.stack([*came[0], *came[1]])

    device_groups = [[8 * plane + place for place in range(8)] for plane in range(planes)]

    def plane_exchange(value):
        return lax.all_to_all(
            value, BOTH, split_axis=0, concat_axis=0, tiled=True, axis_index_groups=device_groups
        )

    def cross_rows_at_once(parts):
        zeros = jnp.zeros_like(parts)
        sent = jnp.stack(
            [jnp.where(here_lo == core, parts, zeros) for core in range(2)], axis=1
        )
        came = plane_exchange(sent.reshape(8, *parts.shape[1:]))
        came = jnp.where(here_core == 0, came[:4], came[4:])
        return came.reshape(-1, parts.shape[-1])

    def cross_back_at_once(rows):
        parts = rows.reshape(4, w_rows, -1)
        zeros = jnp.zeros_like(parts)
        sent = [jnp.where(here_core == lo, parts, zeros) for lo in range(2)]
        return plane_exchange(jnp.concatenate(sent, axis=0))

    def gather(part):
        return lax.all_gather(part, BOTH, axis=0, tiled=True, axis_index_groups=row_groups)

    def blocks_of(matrix):
        rows, n = matrix.shape
        return matrix.reshape(rows, n // BLOCK, BLOCK).transpose(1, 0, 2).reshape(-1, BLOCK)

    def from_blocks(packed, rows):
        groups, count = packed.shape[0], packed.shape[1] // rows
        parts = packed.reshape(groups, count, rows, BLOCK).transpose(0, 2, 1, 3)
        return parts.reshape(groups * rows, count * BLOCK)

    def scatter(packed):
        part = lax.psum_scatter(
            packed.reshape(-1, packed.shape[-1]),
            BOTH,
            scatter_dimension=0,
            tiled=True,
            axis_index_groups=row_groups,
        )
        return part

    def split_qkv(query, key, value):
        stacked = jnp.stack([query, key, value], axis=0)
        stacked = stacked.reshape(3, w_rows, QUARTER_HEADS, QUARTERS, HD)
        return stacked.transpose(3, 1, 2, 0, 4).reshape(QUARTERS, w_rows, 3 * quarter_width)

    def join_qkv(parts):
        parts = parts.reshape(QUARTERS, w_rows, QUARTER_HEADS, 3, HD)
        return parts.transpose(3, 1, 2, 0, 4).reshape(3, w_rows, D)

    def split_units(gate, upward):
        def quarters(matrix):
            parts = matrix.reshape(w_rows, planes, QUARTERS, 2, d_rows).transpose(2, 0, 1, 3, 4)
            parts = jnp.pad(parts, ((0, 0),) * 4 + ((0, padded - d_rows),))
            return parts.reshape(QUARTERS, w_rows, -1, 1, BLOCK // 2)

        both = jnp.concatenate([quarters(gate), quarters(upward)], axis=3)
        return both.reshape(QUARTERS, w_rows, 2 * quarter_ff)

    def join_units(parts):
        parts = parts.reshape(QUARTERS, w_rows, -1, 2, BLOCK // 2)

        def joined(part):
            part = part.reshape(QUARTERS, w_rows, planes, 2, padded)[..., :d_rows]
            return part.transpose(1, 2, 0, 3, 4).reshape(w_rows, 4 * seq * d_rows)

        return joined(parts[:, :, :, 0]), joined(parts[:, :, :, 1])

    def whole_out(part):
        matrix = lax.all_gather(part, BOTH, axis=0, tiled=True).reshape(QUARTER_HEADS, QUARTERS, HD, D)
        return lax.dynamic_index_in_dim(matrix, my_quarter, 1, keepdims=False).reshape(quarter_width, D)

    def whole_out_back(grad):
        spaced = lax.dynamic_update_slice_in_dim(
            jnp.zeros((QUARTER_HEADS, QUARTERS, HD, D), LOW),
            grad.astype(LOW).reshape(QUARTER_HEADS, 1, HD, D),
            my_quarter,
            1,
        )
        return lax.psum_scatter(spaced.reshape(D, D), BOTH, scatter_dimension=0, tiled=True)

    def normalize(values):
        inverse = lax.rsqrt(jnp.mean(values * values, axis=-1, keepdims=True) + NORM_EPS)
        return values * inverse, inverse

    def normalize_back(scaled, inverse, inner):
        return inverse * (inner - scaled * jnp.mean(inner * scaled, axis=-1, keepdims=True))

    def scaled_qkv(layer):
        scale = gain_attn[layer][:, None]
        return split_qkv(
            *((member[layer] * scale).astype(LOW) for member in (w_query, w_key, w_value))
        )

    def attention_part(layer, qkv_rows):
        if not split_heads:
            return qkv_rows
        return jnp.concatenate([qkv_rows, blocks_of(w_out[layer].astype(LOW))], axis=1)

    def attention_matrices(layer, part):
        whole = gather(part)
        if split_heads:
            out_matrix = from_blocks(
                whole[:, 3 * quarter_width :].reshape(2 * planes, -1, BLOCK), w_rows
            )
        else:
            out_matrix = whole_out(w_out[layer].astype(LOW))
        return whole[:, : 3 * quarter_width], out_matrix

    first_part = attention_part(0, cross_rows_at_once(scaled_qkv(0)))
    first_part, tokens, cotangent, time_ids, w_query, w_key, w_value, w_gate, w_up = (
        lax.optimization_barrier(
            (first_part, tokens, cotangent, time_ids, w_query, w_key, w_value, w_gate, w_up)
        )
    )
    attention_weights = [attention_matrices(0, first_part)]
    start_scaled, start_inverse = normalize(tokens)
    start_normed = beside(start_scaled.astype(LOW))

    group_rows = 4 * w_rows
    unit_end = 2 * quarter_ff // BLOCK * group_rows
    ffn_end = unit_end + D // BLOCK * padded
    out_end = ffn_end + (D // BLOCK * w_rows if split_heads else 0)
    qkv_end = out_end + 3 * quarter_width // BLOCK * group_rows

    def units_parts(layer):
        scale = gain_ffn[layer][:, None]
        return split_units((w_gate[layer] * scale).astype(LOW), (w_up[layer] * scale).astype(LOW))

    def ffn_part(layer, units_rows):
        down_part = jnp.pad(w_down[layer].astype(LOW), ((0, padded - d_rows), (0, 0)))
        return jnp.concatenate([blocks_of(units_rows), blocks_of(down_part)], axis=0)

    later_weights = [units_parts(layer) for layer in range(LAYERS)]
    later_weights += [scaled_qkv(layer) for layer in range(1, LAYERS)]
    later_widths = [member.shape[-1] for member in later_weights]
    later_weights = jnp.concatenate(later_weights, axis=-1)

    def cut(whole):
        parts, start = [], 0
        for width in later_widths:
            parts.append(whole[..., start : start + width])
            start += width
        return parts

    ffn_weights = []

    def placed_ids(ids):
        ids = ids.reshape(planes, 2, 2, 2, tok_rows)
        ids = jnp.where(here_lo == 0, ids, ids[:, ::-1])
        ids = jnp.where(here_y == 0, ids, ids[:, :, ::-1])
        ids = jnp.where(here_core == 0, ids, ids[:, :, :, ::-1])
        return ids.transpose(3, 0, 1, 2, 4).reshape(2 * planes, cols)

    def my_tiles(value):
        if spread == 1:
            return value
        return lax.dynamic_slice_in_dim(value, first_tile, tiles, 0)

    positions = jnp.arange(all_rows, dtype=jnp.int32)
    doc_ids = jnp.sum((doc_starts[None, :] <= positions[:, None]).astype(jnp.int32), axis=1)
    docs = placed_ids(doc_ids)
    variates = placed_ids(variate_ids)
    q_docs, q_variates = my_tiles(docs[:planes]), my_tiles(variates[:planes])
    extra_row = jnp.arange(HD, dtype=jnp.int32)[None, :, None]

    def one_hot(ids):
        return ids[:, None, :] == extra_row % VARIATES

    def is_doc(ids):
        return ids[:, None, :] == extra_row - 24

    doc_row = (extra_row >= 24) & (extra_row < 32)
    ones_row = (extra_row == 16) | (extra_row == 17) | ((extra_row >= 32) & (extra_row < 35))
    k_hits = one_hot(variates) & (extra_row < 16) | is_doc(docs) & doc_row | ones_row
    k_aug = jnp.where(k_hits, 1.0, 0.0).astype(LOW)

    def query_extra(layer):
        same, other = variate_bias[layer, 0, my_head], variate_bias[layer, 1, my_head]
        gap = same - other
        gap_lead, other_lead = (part.astype(LOW).astype(jnp.float32) for part in (gap, other))
        gap_part = jnp.where(extra_row < VARIATES, gap_lead, gap - gap_lead)
        other_part = jnp.where(extra_row == 16, other_lead, other - other_lead)
        spread_gap = jnp.where(one_hot(q_variates), gap_part, 0.0)
        shut = jnp.where(doc_row & ~is_doc(q_docs), FLOOR_SCORE, 0.0)
        tail = jnp.where(extra_row < 18, other_part, shut)
        return jnp.where(extra_row < 16, spread_gap, tail).astype(LOW)

    q_augs = [query_extra(layer) for layer in range(LAYERS)]
    q_onehots = (q_variates[:, None, :] == jnp.arange(VARIATES, dtype=jnp.int32)[:, None]).astype(
        jnp.float32
    )

    half_dim = HD // 2
    frequency = jnp.exp(jnp.arange(half_dim).astype(jnp.float32) * (-2.0 * math.log(10000.0) / HD))
    times = beside(time_ids.astype(jnp.float32))
    angles = frequency[:, None] * times[None, :]
    cosines, sines = jnp.cos(angles), jnp.sin(angles)
    start_normed, later_weights, k_aug, cosines, sines, *q_augs = lax.optimization_barrier(
        (start_normed, later_weights, k_aug, cosines, sines, *q_augs)
    )

    def rotate(values, sines):
        former, latter = values[:, :half_dim], values[:, half_dim:]
        return jnp.concatenate(
            [former * cosines - latter * sines, latter * cosines + former * sines], axis=1
        )

    def to_heads(value):
        if spread > 1:
            value = jnp.repeat(value, spread, axis=0)
        return lax.all_to_all(
            value, "seq", split_axis=0, concat_axis=0, tiled=True, axis_index_groups=plane_groups
        )

    def all_blocks(value):
        if spread == 1:
            return value
        zeros = jnp.zeros((planes,) + value.shape[1:], value.dtype)
        return lax.dynamic_update_slice_in_dim(zeros, value, first_tile, 0)

    def from_heads(value):
        value = lax.all_to_all(
            value, "seq", split_axis=0, concat_axis=0, tiled=True, axis_index_groups=plane_groups
        )
        if spread > 1:
            value = value.reshape((QUARTER_HEADS, spread) + value.shape[1:])
            value = jnp.sum(value.astype(jnp.float32), axis=1).astype(LOW)
        return value

    stream = tokens
    saved = []
    for layer in range(LAYERS):
        qkv_matrix, out_matrix = attention_weights[layer]
        if layer == 0:
            scaled_one, inverse_one, normed = start_scaled, start_inverse, start_normed
        else:
            scaled_one, inverse_one = normalize(stream)
            normed = beside(scaled_one.astype(LOW))
        projected = dot(qkv_matrix, normed, TT).reshape(QUARTER_HEADS, 3 * HD, cols)
        query = rotate(projected[:, :HD], sines) * (1.0 / math.sqrt(HD))
        key = rotate(projected[:, HD : 2 * HD], sines)
        sent = jnp.concatenate([query, key, projected[:, 2 * HD :]], axis=1).astype(LOW)
        if layer == 0:
            sent, later_weights = lax.optimization_barrier((sent, later_weights))
            later_weights = cross_rows(later_weights)
        own = to_heads(sent)
        own, later_weights = lax.optimization_barrier((own, later_weights))
        packed = gather(ffn_part(layer, cut(later_weights)[layer])).reshape(2 * planes, -1, BLOCK)
        ffn_weights.append(packed)
        sib = lax.ppermute(own[:, HD:], "head", CORE_SWAP)
        queries = my_tiles(own)
        q_aug = q_augs[layer]
        out, lse = attention_forward(queries, q_aug, own, sib, k_aug)
        if layer == 0:
            out, cotangent = lax.optimization_barrier((out, cotangent))
            last_grad_low = beside(cotangent.astype(LOW))
        attended = from_heads(all_blocks(out)).reshape(quarter_width, cols)
        if layer == 0:
            attended, last_grad_low = lax.optimization_barrier((attended, last_grad_low))
        middle = stream + fold(dot(attended, out_matrix, TN))
        scaled_two, inverse_two = normalize(middle)
        normed_ffn = beside(scaled_two.astype(LOW))
        if layer < LAYERS - 1:
            next_part = attention_part(layer + 1, cut(later_weights)[LAYERS + layer])
            normed_ffn, next_part = lax.optimization_barrier((normed_ffn, next_part))
            attention_weights.append(attention_matrices(layer + 1, next_part))
        both, hidden, partial = ffn_forward(normed_ffn, packed, quarter_ff, group_rows, padded)
        saved.append(
            (
                scaled_one, inverse_one, normed, own, sib, queries, q_aug, out, lse, attended,
                scaled_two, inverse_two, normed_ffn, both, hidden,
            )
        )
        if layer < LAYERS - 1:
            stream = middle + fold(partial)
        else:
            last_middle, last_partial = middle, partial

    upstream = cotangent
    whole_grads, ffn_sums = [None] * LAYERS, [None] * LAYERS
    bias_parts = [None] * LAYERS
    buffer, sent_last = None, None
    qkv_grad = None

    for layer in reversed(range(LAYERS)):
        (qkv_matrix, out_matrix), packed = attention_weights[layer], ffn_weights[layer]
        (
            scaled_one, inverse_one, normed, own, sib, queries, q_aug, out, lse, attended,
            scaled_two, inverse_two, normed_ffn, both, hidden,
        ) = saved[layer]
        upstream_low = beside(upstream.astype(LOW)) if layer < LAYERS - 1 else last_grad_low
        grad_units, partial = ffn_backward(upstream_low, packed, both, quarter_ff, group_rows, padded)
        inner = fold(partial)
        total_rows = qkv_end if layer < LAYERS - 1 else out_end
        buffer = weight_grad(
            buffer, total_rows, normed_ffn.T, grad_units, "blocks", group_rows, 0, 4 * padded // group_rows
        )
        inner, buffer = lax.optimization_barrier((inner, buffer))
        buffer = weight_grad(
            buffer, total_rows, hidden.T, upstream_low, "columns", padded, unit_end, D // BLOCK
        )
        grad_middle = upstream + normalize_back(scaled_two, inverse_two, inner)
        middle_low = beside(grad_middle.astype(LOW))
        middle_low, buffer = lax.optimization_barrier((middle_low, buffer))
        grad_attended = dot(out_matrix, middle_low, NT).astype(LOW)
        if split_heads:
            buffer = weight_grad(
                buffer, total_rows, attended, middle_low, "columns", w_rows, ffn_end, D // BLOCK
            )
        else:
            whole_grads[layer] = whole_out_back(dot(attended, middle_low, NN))
        if sent_last is not None:
            buffer, sent_last = lax.optimization_barrier((buffer, sent_last))
            ffn_sums[layer + 1] = sent_last
        out_grad = my_tiles(to_heads(grad_attended.reshape(QUARTER_HEADS, HD, cols)))
        buffer, out_grad = lax.optimization_barrier((buffer, out_grad))
        if layer == 0:
            sent_last = scatter(buffer)
        grad_q, grad_kv = attention_backward(
            queries, q_aug, lse, out, out_grad, own, sib, k_aug
        )
        same_grad = jnp.sum(grad_q[:, HD : HD + VARIATES] * q_onehots)
        all_grad = jnp.sum(grad_q[:, HD + 16])
        crossed = lax.ppermute(grad_kv[planes:], "head", CORE_SWAP)
        grad_kv = (grad_kv[:planes].astype(jnp.float32) + crossed.astype(jnp.float32)).astype(LOW)
        grad_q = (grad_q[:, :HD] * (1.0 / math.sqrt(HD))).astype(LOW)
        if layer == LAYERS - 1:
            grad_kv, last_partial = lax.optimization_barrier((grad_kv, last_partial))
            stream = last_middle + fold(last_partial)
        grad_heads = from_heads(jnp.concatenate([all_blocks(grad_q), grad_kv], axis=1))
        if layer > 0:
            grad_heads, buffer, stream = lax.optimization_barrier((grad_heads, buffer, stream))
            sent_last = scatter(buffer)
        grad_heads = jnp.concatenate(
            [
                rotate(grad_heads[:, :HD].astype(jnp.float32), -sines).astype(LOW),
                rotate(grad_heads[:, HD : 2 * HD].astype(jnp.float32), -sines).astype(LOW),
                grad_heads[:, 2 * HD :],
            ],
            axis=1,
        ).reshape(3 * quarter_width, cols)
        bias_parts[layer] = jnp.stack([same_grad, all_grad - same_grad])
        if layer > 0:
            buffer = weight_grad(
                None, qkv_end, normed.T, grad_heads, "rows", group_rows, out_end, 1
            )
        else:
            qkv_grad = dot(normed, grad_heads, TT).astype(LOW)
            qkv_grad, grad_heads = lax.optimization_barrier((qkv_grad, grad_heads))
            qkv_grad, sent_last = lax.optimization_barrier((qkv_grad, sent_last))
            ffn_sums[0] = sent_last
            qkv_sum = scatter(qkv_grad)
        partial = dot(grad_heads, qkv_matrix, TT)
        if layer > 0:
            inner = fold(partial)
            inner, buffer = lax.optimization_barrier((inner, buffer))
        else:
            qkv_sum, partial = lax.optimization_barrier((qkv_sum, partial))
            inner = fold(partial)
        upstream = grad_middle + normalize_back(scaled_one, inverse_one, inner)

    bias_local = lax.dynamic_update_slice(
        jnp.zeros((LAYERS, 2, HEADS), jnp.float32), jnp.stack(bias_parts)[:, :, None], (0, 0, my_head)
    )
    bias_total = bias_local
    for axis, size in (("head", 4), ("seq", seq)):
        hop = 1
        while hop < size:
            swap = [(place, place ^ hop) for place in range(size)]
            bias_total = bias_total + lax.ppermute(bias_total, axis, swap)
            hop *= 2

    later_sums = [from_blocks(member[None, :unit_end], group_rows) for member in ffn_sums]
    later_sums += [from_blocks(member[None, out_end:], group_rows) for member in ffn_sums[:-1]]
    quarters = jnp.arange(QUARTERS, dtype=jnp.int32)
    weights = (w_query, w_key, w_value, w_gate, w_up)
    gains = (gain_attn[:, :, None], gain_ffn[:, :, None])
    *grads, gain_one, gain_two = finish_gradients(
        quarters ^ (2 * here_y + here_core), cross_back(jnp.concatenate(later_sums, axis=1)), ffn_sums,
        weights, gains, w_down.shape, (unit_end, ffn_end), planes, split_heads,
    )
    if not split_heads:
        grads[3] = jnp.stack(whole_grads).astype(jnp.float32)
    *grads[:3], gain_one = finish_first(
        2 * quarters + here_lo, cross_back_at_once(qkv_sum), weights[:3], gains[0], grads[:3], gain_one
    )
    return (stream, upstream, *grads, gain_one[:, :, 0], gain_two[:, :, 0], bias_total)


def solution(mesh):
    rows = P(BOTH, None)
    middle = P(None, BOTH, None)
    gains = P(None, BOTH)
    return jax.shard_map(
        on_device,
        mesh=mesh,
        in_specs=(rows,) + (middle,) * 7 + (gains,) * 2 + (P(),) * 3 + (P(BOTH), rows),
        out_specs=(rows, rows) + (middle,) * 7 + (gains,) * 2 + (P(),),
        check_vma=False,
    )
```

```python
import functools
import math

import jax
import jax.numpy as jnp
from jax import lax
from jax.experimental import pallas as pl
from jax.experimental.pallas import tpu as pltpu
from jax.sharding import PartitionSpec as P

D = 1024
HEADS = 16
HD = 64
LAYERS = 2
VARIATES = 8
BLOCK = 256

NORM_EPS = 1e-05
FLOOR_SCORE = -1e30
LOW = jnp.bfloat16
BOTH = ("seq", "head")

QUARTERS = 4
QUARTER_HEADS = HEADS // QUARTERS
Y_SWAP = [(place, place ^ 2) for place in range(4)]
CORE_SWAP = [(place, place ^ 1) for place in range(4)]

NN = (((1,), (0,)), ((), ()))
NT = (((1,), (1,)), ((), ()))
TN = (((0,), (0,)), ((), ()))
TT = (((0,), (1,)), ((), ()))
VMEM_LIMIT = 56 * 1024 * 1024


def cost(flops, operands, results, transcendentals=0):
    moved = sum(member.size * member.dtype.itemsize for member in [*operands, *results])
    return pl.CostEstimate(flops=flops, bytes_accessed=moved, transcendentals=transcendentals)


def dot(left, right, dims):
    return lax.dot_general(left, right, dims, preferred_element_type=jnp.float32)


def forward_kernel(flip_ref, q_ref, q_aug_ref, own_ref, sib_ref, k_aug_ref, out_ref, lse_ref):
    blocks = own_ref.shape[0]
    sources = ((own_ref, HD), (sib_ref, 0))
    spots = [(half, block) for half in range(2) for block in range(blocks)]
    cols = q_ref.shape[-1]
    q_side = jnp.concatenate([q_ref[0, :HD, :], q_aug_ref[0]], axis=0).T
    top = jnp.full((cols, 1), FLOOR_SCORE, jnp.float32)
    total = jnp.zeros((cols, 1), jnp.float32)
    acc = jnp.zeros((cols, HD), jnp.float32)

    def scores(half, block):
        ref, low_row = sources[half]
        extra = k_aug_ref[half * blocks + block]
        k_side = jnp.concatenate([ref[block, low_row : low_row + HD, :], extra], axis=0)
        return dot(q_side, k_side, NN)

    following = scores(*spots[0])
    for number, (half, block) in enumerate(spots):
        part = following
        if number + 1 < len(spots):
            following = scores(*spots[number + 1])
        fresh = jnp.maximum(top, jnp.max(part, axis=-1, keepdims=True))
        shrink = jnp.exp(top - fresh)
        prob = jnp.exp(part - fresh)
        total = total * shrink + jnp.sum(prob, axis=-1, keepdims=True)
        ref, low_row = sources[half]
        values = ref[block, low_row + HD : low_row + 2 * HD, :]
        acc = acc * shrink + dot(prob.astype(LOW), values, NT)
        top = fresh
    result = acc / total
    lse = jnp.broadcast_to(top + jnp.log(total), (cols, HD))
    both = jnp.concatenate([result, lse], axis=1).T
    piece = out_ref.shape[-1]
    for place in range(cols // piece):
        part = both[:HD, place * piece : (place + 1) * piece]
        out_ref[0, place ^ flip_ref[0]] = part.astype(LOW)
    lse_ref[0] = both[HD : HD + 8]


def split_rows(row, rows):
    one = row.astype(LOW).astype(jnp.float32)
    two = (row - one).astype(LOW).astype(jnp.float32)
    three = row - one - two
    pad = jnp.zeros((rows - 3, row.shape[-1]), jnp.float32)
    return jnp.concatenate([one, two, three, pad], axis=0).astype(LOW)


def backward_kernel(
    flip_ref, q_ref, q_aug_ref, lse_ref, out_ref, grad_ref, own_ref, sib_ref, k_aug_ref,
    dq_ref, dkv_ref, dkv_acc,
):
    step = pl.program_id(0)
    blocks = own_ref.shape[0]
    sources = ((own_ref, HD), (sib_ref, 0))
    cols, key_cols = q_ref.shape[-1], own_ref.shape[-1]

    @pl.when(step == 0)
    def _():
        dkv_acc[...] = jnp.zeros_like(dkv_acc)

    q_low = q_ref[0, :HD, :]
    places = range(grad_ref.shape[1])
    g_low = jnp.concatenate([grad_ref[0, place ^ flip_ref[0]] for place in places], axis=1)
    out = jnp.concatenate([out_ref[0, place ^ flip_ref[0]] for place in places], axis=1)
    row_dot = jnp.sum(g_low.astype(jnp.float32) * out.astype(jnp.float32), axis=0, keepdims=True)
    aug = jnp.concatenate(
        [q_aug_ref[0, :32, :], split_rows(-lse_ref[0, :1, :], 16), q_aug_ref[0, 48:, :]], axis=0
    )
    q_side = jnp.concatenate([q_low, aug], axis=0).T
    g_side = jnp.concatenate([g_low, split_rows(-row_dot, HD)], axis=0).T
    ones = jnp.concatenate(
        [jnp.ones((16, key_cols), LOW), jnp.zeros((HD - 16, key_cols), LOW)], axis=0
    )
    dq = jnp.zeros((cols, 2 * HD), jnp.float32)
    spots = [(half, block) for half in range(2) for block in range(blocks)]

    def products(half, block):
        ref, low_row = sources[half]
        k_side = jnp.concatenate(
            [ref[block, low_row : low_row + HD, :], k_aug_ref[half * blocks + block]], axis=0
        )
        v_side = jnp.concatenate([ref[block, low_row + HD : low_row + 2 * HD, :], ones], axis=0)
        return k_side, dot(q_side, k_side, NN), dot(g_side, v_side, NN)

    following = products(*spots[0])
    for spot in range(len(spots)):
        k_side, score, prob_grad = following
        if spot + 1 < len(spots):
            following = products(*spots[spot + 1])
        prob = jnp.exp(score)
        score_grad = (prob * prob_grad).astype(LOW)
        dq = dq + dot(score_grad, k_side, NT)
        dkv_acc[spot, :HD, :] += dot(q_low, score_grad, NN)
        dkv_acc[spot, HD:, :] += dot(g_low, prob.astype(LOW), NN)
    dq_ref[0] = dq.T

    @pl.when(step == pl.num_programs(0) - 1)
    def _():
        dkv_ref[...] = dkv_acc[...].astype(LOW)


def whole_spec(shape):
    rank = len(shape)
    return pl.BlockSpec(shape, lambda i, flip: (0,) * rank)


def tile_spec(rows, cols):
    return pl.BlockSpec((1, rows, cols), lambda i, flip: (i, 0, 0))


def owner_spec(shape):
    return pl.BlockSpec((1, *shape[1:]), lambda i, flip: (i, 0, 0, 0))


def attention_forward(flip, queries, q_aug, own, sib, k_aug):
    tiles, unused, cols = queries.shape
    pairs = 2 * tiles * own.shape[0] * cols * cols
    out_shape = (tiles, 4, HD, cols // 4)
    results = [
        jax.ShapeDtypeStruct(out_shape, LOW),
        jax.ShapeDtypeStruct((tiles, 8, cols), jnp.float32),
    ]
    return pl.pallas_call(
        forward_kernel,
        grid_spec=pltpu.PrefetchScalarGridSpec(
            num_scalar_prefetch=1,
            grid=(tiles,),
            in_specs=[tile_spec(3 * HD, cols), tile_spec(HD, cols)]
            + [whole_spec(member.shape) for member in (own, sib, k_aug)],
            out_specs=[owner_spec(out_shape), tile_spec(8, cols)],
        ),
        out_shape=results,
        cost_estimate=cost(16 * HD * pairs, [queries, own, sib], results, pairs),
        compiler_params=pltpu.CompilerParams(vmem_limit_bytes=VMEM_LIMIT),
        name="attention_forward",
    )(flip, queries, q_aug, own, sib, k_aug)


def attention_backward(flip, queries, q_aug, lse, out, grad, own, sib, k_aug):
    tiles, unused, cols = queries.shape
    dkv_shape = (2 * own.shape[0], 2 * HD, cols)
    pairs = 2 * tiles * own.shape[0] * cols * cols
    results = [
        jax.ShapeDtypeStruct((tiles, 2 * HD, cols), jnp.float32),
        jax.ShapeDtypeStruct(dkv_shape, LOW),
    ]
    return pl.pallas_call(
        backward_kernel,
        grid_spec=pltpu.PrefetchScalarGridSpec(
            num_scalar_prefetch=1,
            grid=(tiles,),
            in_specs=[tile_spec(3 * HD, cols), tile_spec(HD, cols), tile_spec(8, cols)]
            + [owner_spec(out.shape)] * 2
            + [whole_spec(member.shape) for member in (own, sib, k_aug)],
            out_specs=[tile_spec(2 * HD, cols), whole_spec(dkv_shape)],
            scratch_shapes=[pltpu.VMEM(dkv_shape, jnp.float32)],
        ),
        out_shape=results,
        cost_estimate=cost(32 * HD * pairs, [queries, own, sib], results, pairs),
        compiler_params=pltpu.CompilerParams(vmem_limit_bytes=VMEM_LIMIT),
        name="attention_backward",
    )(flip, queries, q_aug, lse, out, grad, own, sib, k_aug)


def silu_parts(gate):
    sigmoid = 1.0 / (1.0 + jnp.exp(-gate))
    return sigmoid, gate * sigmoid


def put_parts(values, lanes, own_ref, *low_refs):
    rows = own_ref.shape[0]
    own_ref[:, lanes] = values[:rows]
    for place, low_ref in enumerate(low_refs):
        low_ref[:, lanes] = values[(place + 1) * rows : (place + 2) * rows].astype(LOW)


def parts_of(tokens, lanes, index):
    shape = (tokens // 4, D)
    types = [jnp.float32, LOW, LOW, LOW]
    return (
        [jax.ShapeDtypeStruct(shape, kind) for kind in types],
        [pl.BlockSpec((tokens // 4, lanes), index) for unused in types],
    )


def ffn_forward_kernel(
    x_ref, unit_ref, down_ref, both_ref, hidden_ref, *out_refs, unit_rows, down_rows, unit_steps
):
    step = pl.program_id(0)
    half = BLOCK // 2

    @pl.when(step < unit_steps)
    def _():
        count = unit_ref.shape[1] // unit_rows
        for place in range(count):
            matrix = unit_ref[:, place * unit_rows : (place + 1) * unit_rows, :].reshape(-1, BLOCK)
            both = dot(x_ref[...], matrix, NN)
            both_ref[place] = both.astype(both_ref.dtype)
            hidden = silu_parts(both[:, :half])[1] * both[:, half:]
            spot = step * count + place
            hidden_ref[:, pl.ds(pl.multiple_of(spot * half, half), half)] = hidden.astype(LOW)

    @pl.when(step >= unit_steps)
    def _():
        for place in range(down_ref.shape[1] // down_rows):
            matrix = down_ref[:, place * down_rows : (place + 1) * down_rows, :].reshape(-1, BLOCK)
            lanes = slice(place * BLOCK, (place + 1) * BLOCK)
            put_parts(dot(hidden_ref[...], matrix, NN), lanes, *out_refs)


def ffn_backward_kernel(
    g_ref, unit_ref, down_ref, both_ref, grads_ref, *refs, unit_rows, down_rows, down_steps
):
    part_refs, inner_ref, hidden_grad = refs[:4], refs[4], refs[5]
    step = pl.program_id(0)
    half = BLOCK // 2

    @pl.when(step < down_steps)
    def _():
        total = 0.0
        for place in range(down_ref.shape[1] // down_rows):
            matrix = down_ref[:, place * down_rows : (place + 1) * down_rows, :].reshape(-1, BLOCK)
            part = g_ref[:, place * BLOCK : (place + 1) * BLOCK]
            total = total + dot(part, matrix, NT)

        @pl.when(step == 0)
        def _():
            hidden_grad[...] = total

        @pl.when(step > 0)
        def _():
            hidden_grad[...] += total

    @pl.when(step >= down_steps)
    def _():
        count = unit_ref.shape[1] // unit_rows
        total = 0.0
        for place in range(count):
            matrix = unit_ref[:, place * unit_rows : (place + 1) * unit_rows, :].reshape(-1, BLOCK)
            spot = (step - down_steps) * count + place
            gate = both_ref[place, :, :half].astype(jnp.float32)
            upward = both_ref[place, :, half:].astype(jnp.float32)
            above = hidden_grad[:, pl.ds(pl.multiple_of(spot * half, half), half)]
            sigmoid, silu = silu_parts(gate)
            grad_gate = above * upward * (sigmoid * (1.0 + gate * (1.0 - sigmoid)))
            grads = jnp.concatenate([grad_gate, above * silu], axis=1).astype(LOW)
            grads_ref[place] = grads
            total = total + dot(grads, matrix, NT)

        @pl.when(step == down_steps)
        def _():
            inner_ref[...] = total

        @pl.when(step > down_steps)
        def _():
            inner_ref[...] += total

    @pl.when(step == pl.num_programs(0) - 1)
    def _():
        put_parts(inner_ref[...], slice(0, D), *part_refs)


FFN_DOWNS = 4


def ffn_units(cols_ff):
    return max(count for count in (1, 2, 3) if 2 * cols_ff // BLOCK % count == 0)


def ffn_specs(cols_ff, unit_rows, down_rows, groups, unit_step, down_step):
    unit_blocks, down_blocks = 2 * cols_ff // BLOCK, D // BLOCK
    units, downs = ffn_units(cols_ff) * unit_rows, FFN_DOWNS * down_rows
    first_down = unit_blocks * unit_rows // downs
    return (
        unit_blocks // ffn_units(cols_ff),
        down_blocks // FFN_DOWNS,
        [
            pl.BlockSpec((groups, units, BLOCK), lambda i: (0, unit_step(i), 0)),
            pl.BlockSpec((groups, downs, BLOCK), lambda i: (0, first_down + down_step(i), 0)),
        ],
    )


def ffn_forward(x, packed, cols_ff, unit_rows, down_rows):
    tokens, unit_steps = x.shape[0], 2 * cols_ff // BLOCK // ffn_units(cols_ff)
    unit_step = lambda i: jnp.minimum(i, unit_steps - 1)
    down_step = lambda i: jnp.maximum(i - unit_steps, 0)
    unit_steps, down_steps, specs = ffn_specs(
        cols_ff, unit_rows, down_rows, packed.shape[0], unit_step, down_step
    )
    parts, part_specs = parts_of(tokens, FFN_DOWNS * BLOCK, lambda i: (0, down_step(i)))
    results = [
        jax.ShapeDtypeStruct((2 * cols_ff // BLOCK, tokens, BLOCK), LOW),
        jax.ShapeDtypeStruct((tokens, cols_ff), LOW),
        *parts,
    ]
    return pl.pallas_call(
        functools.partial(
            ffn_forward_kernel, unit_rows=unit_rows, down_rows=down_rows, unit_steps=unit_steps
        ),
        grid=(unit_steps + down_steps,),
        in_specs=[pl.BlockSpec(x.shape, lambda i: (0, 0)), *specs],
        out_specs=[
            pl.BlockSpec((ffn_units(cols_ff), tokens, BLOCK), lambda i: (unit_step(i), 0, 0)),
            pl.BlockSpec((tokens, cols_ff), lambda i: (0, 0)),
            *part_specs,
        ],
        out_shape=results,
        cost_estimate=cost(6 * tokens * D * cols_ff, [x, packed], results),
        compiler_params=pltpu.CompilerParams(vmem_limit_bytes=VMEM_LIMIT),
        name="ffn_forward",
    )(x, packed, packed)


def ffn_backward(grad, packed, both, cols_ff, unit_rows, down_rows):
    tokens, down_steps = grad.shape[0], D // BLOCK // FFN_DOWNS
    unit_step = lambda i: jnp.maximum(i - down_steps, 0)
    down_step = lambda i: jnp.minimum(i, down_steps - 1)
    unit_steps, down_steps, specs = ffn_specs(
        cols_ff, unit_rows, down_rows, packed.shape[0], unit_step, down_step
    )
    unit_spec = pl.BlockSpec((ffn_units(cols_ff), tokens, BLOCK), lambda i: (unit_step(i), 0, 0))
    parts, part_specs = parts_of(tokens, D, lambda i: (0, 0))
    results = [jax.ShapeDtypeStruct((2 * cols_ff // BLOCK, tokens, BLOCK), LOW), *parts]
    return pl.pallas_call(
        functools.partial(
            ffn_backward_kernel, unit_rows=unit_rows, down_rows=down_rows, down_steps=down_steps
        ),
        grid=(unit_steps + down_steps,),
        in_specs=[
            pl.BlockSpec((tokens, FFN_DOWNS * BLOCK), lambda i: (0, down_step(i))),
            *specs,
            unit_spec,
        ],
        out_specs=[unit_spec, *part_specs],
        out_shape=results,
        scratch_shapes=[pltpu.VMEM((tokens, D), jnp.float32), pltpu.VMEM((tokens, cols_ff), jnp.float32)],
        cost_estimate=cost(6 * tokens * D * cols_ff, [grad, packed, both], results),
        compiler_params=pltpu.CompilerParams(vmem_limit_bytes=VMEM_LIMIT),
        name="ffn_backward",
    )(grad, packed, packed, both)


def weight_grad_kernel(left_ref, right_ref, *refs, rows, kind):
    out_ref = refs[-1]
    for place in range(out_ref.shape[1] // rows):
        if kind == "blocks":
            grad = dot(left_ref[...], right_ref[place], NN)
        elif kind == "columns":
            grad = dot(left_ref[...], right_ref[:, place * BLOCK : (place + 1) * BLOCK], NN)
        else:
            grad = dot(left_ref[...], right_ref[place * BLOCK : (place + 1) * BLOCK, :], NT)
        out_ref[:, place * rows : (place + 1) * rows, :] = grad.reshape(-1, rows, BLOCK).astype(LOW)


def weight_grad(buffer, total_rows, left, right, kind, rows, start, per_step):
    tokens = left.shape[1]
    groups = left.shape[0] // rows
    if kind == "blocks":
        count = right.shape[0]
        right_spec = pl.BlockSpec((per_step, tokens, BLOCK), lambda i: (i, 0, 0))
    elif kind == "columns":
        count = right.shape[1] // BLOCK
        right_spec = pl.BlockSpec((tokens, per_step * BLOCK), lambda i: (0, i))
    else:
        count = right.shape[0] // BLOCK
        right_spec = pl.BlockSpec((per_step * BLOCK, tokens), lambda i: (i, 0))
    first = start // (per_step * rows)
    operands, specs = [left, right], [pl.BlockSpec(left.shape, lambda i: (0, 0)), right_spec]
    if buffer is not None:
        operands.append(buffer)
        specs.append(pl.BlockSpec(memory_space=pl.ANY))
    return pl.pallas_call(
        functools.partial(weight_grad_kernel, rows=rows, kind=kind),
        grid=(count // per_step,),
        in_specs=specs,
        out_specs=pl.BlockSpec((groups, per_step * rows, BLOCK), lambda i: (0, first + i, 0)),
        out_shape=jax.ShapeDtypeStruct((groups, total_rows, BLOCK), LOW),
        input_output_aliases={} if buffer is None else {2: 0},
        cost_estimate=cost(2 * left.size * count * BLOCK, [left, left, right], []),
        compiler_params=pltpu.CompilerParams(vmem_limit_bytes=VMEM_LIMIT),
        name="weight_grad_" + kind,
    )(*operands)


def put_qkv(came_ref, place_ref, start, outs, layer, weights, gain_ref, gain_out_ref):
    for quarter in range(QUARTERS):
        part = came_ref[place_ref[quarter], :, start : start + 3 * QUARTER_HEADS * HD]
        part = part.astype(jnp.float32)
        for slot in range(QUARTER_HEADS):
            column = HD * (QUARTERS * slot + quarter)
            for which, out_ref in enumerate(outs):
                first = (3 * slot + which) * HD
                out_ref[layer, :, column : column + HD] = part[:, first : first + HD]
    gain_grad = 0.0
    for out_ref, weight_ref in zip(outs, weights):
        grad = out_ref[layer]
        gain_grad = gain_grad + jnp.sum(grad * weight_ref[layer], axis=1, keepdims=True)
        out_ref[layer] = grad * gain_ref[layer]
    gain_out_ref[layer] = jnp.broadcast_to(gain_grad, gain_out_ref.shape[1:])


def put_units(came_ref, place_ref, start, outs, layer, weights, gain_ref, gain_out_ref, d_rows, padded, planes):
    half = BLOCK // 2
    for quarter in range(QUARTERS):
        part = came_ref[place_ref[quarter], :, start : start + 4 * planes * padded]
        part = part.astype(jnp.float32)
        for plane in range(planes):
            for core in range(2):
                column = d_rows * (8 * plane + 2 * quarter + core)
                unit, end = (2 * plane + core) * padded, (2 * plane + core) * padded + d_rows
                while unit < end:
                    stop = min(end, (unit // half + 1) * half)
                    for which, out_ref in enumerate(outs):
                        first = unit // half * BLOCK + which * half + unit % half
                        out_ref[layer, :, column : column + stop - unit] = part[
                            :, first : first + stop - unit
                        ]
                    column, unit = column + stop - unit, stop
    gain_grad = 0.0
    for out_ref, weight_ref in zip(outs, weights):
        grad = out_ref[layer]
        gain_grad = gain_grad + jnp.sum(grad * weight_ref[layer], axis=1, keepdims=True)
        out_ref[layer] = grad * gain_ref[layer]
    gain_out_ref[layer] = jnp.broadcast_to(gain_grad, gain_out_ref.shape[1:])


def finish_kernel(place_ref, *refs, unit_end, w_rows, d_rows, padded, planes, with_out):
    came_ref, *sums = refs[: 1 + LAYERS]
    out_sums, refs = refs[1 + LAYERS : 2 * LAYERS], refs[2 * LAYERS :]
    weights, gains, outs = refs[:5], refs[5:7], refs[7:]
    units_width = 4 * planes * padded
    for layer in range(LAYERS):
        put_units(
            came_ref, place_ref, layer * units_width, outs[4:6], layer, weights[3:], gains[1],
            outs[8], d_rows, padded, planes,
        )
        if layer > 0:
            start = LAYERS * units_width + (layer - 1) * 3 * QUARTER_HEADS * HD
            put_qkv(came_ref, place_ref, start, outs[:3], layer, weights[:3], gains[0], outs[7])
        for block in range(D // BLOCK):
            lanes = slice(block * BLOCK, (block + 1) * BLOCK)
            rows = sums[layer][unit_end + block * padded : unit_end + (block + 1) * padded, :]
            outs[6][layer, :, lanes] = rows.astype(jnp.float32)[:d_rows]
            if with_out and layer > 0:
                rows = out_sums[layer - 1][block * w_rows : (block + 1) * w_rows, :]
                outs[3][layer, :, lanes] = rows.astype(jnp.float32)


def finish_first_kernel(place_ref, came_ref, out_sum_ref, *refs, w_rows, with_out):
    weights, gain_ref, have, outs = refs[:3], refs[3], refs[4:9], refs[9:]
    for layer in range(1, LAYERS):
        for have_ref, out_ref in zip(have, outs):
            out_ref[layer] = have_ref[layer]
    put_qkv(came_ref, place_ref, 0, outs[:3], 0, weights, gain_ref, outs[3])
    if with_out:
        for block in range(D // BLOCK):
            rows = out_sum_ref[block * w_rows : (block + 1) * w_rows, :]
            outs[4][0, :, block * BLOCK : (block + 1) * BLOCK] = rows.astype(jnp.float32)


def in_vmem(count):
    return [pl.BlockSpec(memory_space=pltpu.VMEM)] * count


def finish_gradients(
    place, came, sums, out_sums, weights, gains, d_shape, unit_end, planes, with_out
):
    layers, w_rows, unused = weights[0].shape
    d_rows = d_shape[1]
    padded = -(-d_rows // 16) * 16
    shapes = [weights[0].shape] * 4 + [weights[3].shape] * 2 + [d_shape] + [(layers, w_rows, 128)] * 2
    return pl.pallas_call(
        functools.partial(
            finish_kernel, unit_end=unit_end, w_rows=w_rows, d_rows=d_rows, padded=padded, planes=planes,
            with_out=with_out,
        ),
        in_specs=[pl.BlockSpec(memory_space=pltpu.SMEM)] + in_vmem(7 + 2 * LAYERS),
        out_specs=in_vmem(9),
        out_shape=[jax.ShapeDtypeStruct(shape, jnp.float32) for shape in shapes],
        compiler_params=pltpu.CompilerParams(vmem_limit_bytes=VMEM_LIMIT),
        name="finish_gradients",
    )(place, came, *sums, *out_sums, *weights, *gains)


def finish_first(place, came, out_sum, weights, gain, grads, with_out):
    return pl.pallas_call(
        functools.partial(finish_first_kernel, w_rows=weights[0].shape[1], with_out=with_out),
        in_specs=[pl.BlockSpec(memory_space=pltpu.SMEM)] + in_vmem(11),
        out_specs=in_vmem(5),
        out_shape=[jax.ShapeDtypeStruct(member.shape, jnp.float32) for member in grads],
        compiler_params=pltpu.CompilerParams(vmem_limit_bytes=VMEM_LIMIT),
        name="finish_first",
    )(place, came, out_sum, *weights, gain, *grads)


def on_device(
    tokens,
    w_query,
    w_key,
    w_value,
    w_out,
    w_gate,
    w_up,
    w_down,
    gain_attn,
    gain_ffn,
    variate_bias,
    doc_starts,
    variate_ids,
    time_ids,
    cotangent,
):
    seq = lax.axis_size("seq")
    planes = seq // 2
    spread = planes // QUARTER_HEADS
    tiles = planes // spread
    tok_rows = tokens.shape[0]
    cols = 4 * tok_rows
    all_rows = variate_ids.shape[0]
    w_rows = w_query.shape[1]
    d_rows = w_down.shape[1]
    padded = -(-d_rows // 16) * 16
    quarter_ff = 2 * planes * padded
    quarter_width = QUARTER_HEADS * HD
    split_heads = 2 * w_rows == HD
    here_seq, here_head = lax.axis_index("seq"), lax.axis_index("head")
    here_plane, here_lo = here_seq // 2, here_seq % 2
    here_y, here_core = here_head // 2, here_head % 2
    my_quarter = 2 * here_lo + here_y
    my_head = QUARTERS * (here_plane // spread) + my_quarter
    first_tile = (here_plane % spread) * tiles
    devices = [
        (plane, lo, y, core)
        for plane in range(planes)
        for lo in range(2)
        for y in range(2)
        for core in range(2)
    ]

    def place_of(plane, lo, y, core):
        return 8 * plane + 4 * lo + 2 * y + core

    row_groups = [
        [place_of(plane, lo, y, core) for plane in range(planes) for core in range(2)]
        for lo in range(2)
        for y in range(2)
    ]
    plane_groups = [[2 * plane + lo for plane in range(planes)] for lo in range(2)]
    x_swap = [(place, place ^ 1) for place in range(seq)]
    corner_swap = [
        (place_of(plane, lo, y, core), place_of(plane, 1 - lo, 1 - y, core))
        for plane, lo, y, core in devices
    ]

    def neighbours(across_y, across_x, across_both):
        return (
            lax.ppermute(across_y, "head", Y_SWAP),
            lax.ppermute(across_x, "seq", x_swap),
            lax.ppermute(across_both, BOTH, corner_swap),
        )

    def beside(value):
        return jnp.concatenate([value, *neighbours(value, value, value)], axis=0)

    def fold(own, *others):
        return own + sum(part.astype(jnp.float32) for part in neighbours(*others))

    def fold_whole(partial):
        low = partial[tok_rows:].astype(LOW).reshape(3, tok_rows, -1)
        return fold(partial[:tok_rows], low[0], low[1], low[2])

    def flip(pair, bit):
        return jnp.where(bit == 0, pair[0], pair[1]), jnp.where(bit == 0, pair[1], pair[0])

    def xor_order(grid, high, low):
        rows = [flip(row, low) for row in grid]
        first, second = zip(*[flip(column, high) for column in zip(*rows)])
        return [list(first), list(second)]

    def cross_rows(parts):
        grid = xor_order([[parts[0], parts[1]], [parts[2], parts[3]]], here_y, here_core)
        came = [[None, None], [None, None]]
        for high in range(2):
            for low in range(2):
                hops = [
                    (place_of(plane, lo, y, core), place_of(plane, y ^ high, core ^ low, lo))
                    for plane, lo, y, core in devices
                ]
                came[high][low] = lax.ppermute(grid[high][low], BOTH, hops)
        came = xor_order(came, here_lo, here_y)
        return jnp.concatenate([*came[0], *came[1]], axis=0)

    def cross_back(rows):
        parts = [rows[place * w_rows : (place + 1) * w_rows] for place in range(4)]
        grid = xor_order([parts[:2], parts[2:]], here_lo, here_y)
        came = [[None, None], [None, None]]
        for high in range(2):
            for low in range(2):
                hops = [
                    (place_of(plane, lo, y, core), place_of(plane, core, lo ^ high, y ^ low))
                    for plane, lo, y, core in devices
                ]
                came[high][low] = lax.ppermute(grid[high][low], BOTH, hops)
        return jnp.stack([*came[0], *came[1]])

    device_groups = [[8 * plane + place for place in range(8)] for plane in range(planes)]

    def plane_exchange(value):
        return lax.all_to_all(
            value, BOTH, split_axis=0, concat_axis=0, tiled=True, axis_index_groups=device_groups
        )

    def cross_rows_at_once(parts):
        zeros = jnp.zeros_like(parts)
        sent = jnp.stack(
            [jnp.where(here_lo == core, parts, zeros) for core in range(2)], axis=1
        )
        came = plane_exchange(sent.reshape(8, *parts.shape[1:]))
        came = jnp.where(here_core == 0, came[:4], came[4:])
        return came.reshape(-1, parts.shape[-1])

    def cross_back_at_once(rows):
        parts = rows.reshape(4, w_rows, -1)
        zeros = jnp.zeros_like(parts)
        sent = [jnp.where(here_core == lo, parts, zeros) for lo in range(2)]
        return plane_exchange(jnp.concatenate(sent, axis=0))

    def gather(part):
        return lax.all_gather(part, BOTH, axis=0, tiled=True, axis_index_groups=row_groups)

    def blocks_of(matrix):
        rows, n = matrix.shape
        return matrix.reshape(rows, n // BLOCK, BLOCK).transpose(1, 0, 2).reshape(-1, BLOCK)

    def from_blocks(packed, rows):
        groups, count = packed.shape[0], packed.shape[1] // rows
        parts = packed.reshape(groups, count, rows, BLOCK).transpose(0, 2, 1, 3)
        return parts.reshape(groups * rows, count * BLOCK)

    def scatter(packed):
        part = lax.psum_scatter(
            packed.reshape(-1, packed.shape[-1]),
            BOTH,
            scatter_dimension=0,
            tiled=True,
            axis_index_groups=row_groups,
        )
        return part

    def split_qkv(query, key, value):
        stacked = jnp.stack([query, key, value], axis=0)
        stacked = stacked.reshape(3, w_rows, QUARTER_HEADS, QUARTERS, HD)
        return stacked.transpose(3, 1, 2, 0, 4).reshape(QUARTERS, w_rows, 3 * quarter_width)

    def join_qkv(parts):
        parts = parts.reshape(QUARTERS, w_rows, QUARTER_HEADS, 3, HD)
        return parts.transpose(3, 1, 2, 0, 4).reshape(3, w_rows, D)

    def split_units(gate, upward):
        def quarters(matrix):
            parts = matrix.reshape(w_rows, planes, QUARTERS, 2, d_rows).transpose(2, 0, 1, 3, 4)
            parts = jnp.pad(parts, ((0, 0),) * 4 + ((0, padded - d_rows),))
            return parts.reshape(QUARTERS, w_rows, -1, 1, BLOCK // 2)

        both = jnp.concatenate([quarters(gate), quarters(upward)], axis=3)
        return both.reshape(QUARTERS, w_rows, 2 * quarter_ff)

    def join_units(parts):
        parts = parts.reshape(QUARTERS, w_rows, -1, 2, BLOCK // 2)

        def joined(part):
            part = part.reshape(QUARTERS, w_rows, planes, 2, padded)[..., :d_rows]
            return part.transpose(1, 2, 0, 3, 4).reshape(w_rows, 4 * seq * d_rows)

        return joined(parts[:, :, :, 0]), joined(parts[:, :, :, 1])

    def whole_out_back(grad):
        spaced = lax.dynamic_update_slice_in_dim(
            jnp.zeros((QUARTER_HEADS, QUARTERS, HD, D), LOW),
            grad.astype(LOW).reshape(QUARTER_HEADS, 1, HD, D),
            my_quarter,
            1,
        )
        return lax.psum_scatter(spaced.reshape(D, D), BOTH, scatter_dimension=0, tiled=True)

    def normalize(values):
        inverse = lax.rsqrt(jnp.mean(values * values, axis=-1, keepdims=True) + NORM_EPS)
        return values * inverse, inverse

    def normalize_back(scaled, inverse, inner):
        return inverse * (inner - scaled * jnp.mean(inner * scaled, axis=-1, keepdims=True))

    def scaled_qkv(layer):
        scale = gain_attn[layer][:, None]
        return split_qkv(
            *((member[layer] * scale).astype(LOW) for member in (w_query, w_key, w_value))
        )

    def attention_part(layer, qkv_rows):
        blocks = blocks_of(w_out[layer].astype(LOW))
        return jnp.concatenate([qkv_rows, blocks], axis=1)

    def attention_matrices(part):
        whole = gather(part)
        blocks = whole[:, 3 * quarter_width :].reshape(2 * planes, -1, BLOCK)
        return whole[:, : 3 * quarter_width], from_blocks(blocks, w_rows)

    first_part = attention_part(0, cross_rows_at_once(scaled_qkv(0)))
    first_part, tokens, cotangent, time_ids, w_query, w_key, w_value, w_gate, w_up = (
        lax.optimization_barrier(
            (first_part, tokens, cotangent, time_ids, w_query, w_key, w_value, w_gate, w_up)
        )
    )
    attention_weights, out_weights = [attention_matrices(first_part)], []
    start_scaled, start_inverse = normalize(tokens)
    start_normed = beside(start_scaled.astype(LOW))

    group_rows = 4 * w_rows
    unit_end = 2 * quarter_ff // BLOCK * group_rows
    ffn_end = unit_end + D // BLOCK * padded
    out_end = ffn_end + (D // BLOCK * w_rows if split_heads else 0)

    def units_parts(layer):
        scale = gain_ffn[layer][:, None]
        return split_units((w_gate[layer] * scale).astype(LOW), (w_up[layer] * scale).astype(LOW))

    def ffn_part(layer, units_rows):
        down_part = jnp.pad(w_down[layer].astype(LOW), ((0, padded - d_rows), (0, 0)))
        return jnp.concatenate([blocks_of(units_rows), blocks_of(down_part)], axis=0)

    later_weights = [units_parts(layer) for layer in range(LAYERS)]
    later_weights += [scaled_qkv(layer) for layer in range(1, LAYERS)]
    later_widths = [member.shape[-1] for member in later_weights]
    later_weights = jnp.concatenate(later_weights, axis=-1)

    def cut(whole):
        parts, start = [], 0
        for width in later_widths:
            parts.append(whole[..., start : start + width])
            start += width
        return parts

    ffn_weights = []

    def placed_ids(ids):
        ids = ids.reshape(planes, 2, 2, 2, tok_rows)
        ids = jnp.where(here_lo == 0, ids, ids[:, ::-1])
        ids = jnp.where(here_y == 0, ids, ids[:, :, ::-1])
        ids = jnp.where(here_core == 0, ids, ids[:, :, :, ::-1])
        return ids.transpose(3, 0, 1, 2, 4).reshape(2 * planes, cols)

    def my_tiles(value):
        if spread == 1:
            return value
        return lax.dynamic_slice_in_dim(value, first_tile, tiles, 0)

    positions = jnp.arange(all_rows, dtype=jnp.int32)
    doc_ids = jnp.sum((doc_starts[None, :] <= positions[:, None]).astype(jnp.int32), axis=1)
    docs = placed_ids(doc_ids)
    variates = placed_ids(variate_ids)
    q_docs, q_variates = my_tiles(docs[:planes]), my_tiles(variates[:planes])
    extra_row = jnp.arange(HD, dtype=jnp.int32)[None, :, None]

    def one_hot(ids):
        return ids[:, None, :] == extra_row % VARIATES

    def is_doc(ids):
        return ids[:, None, :] == extra_row - 24

    doc_row = (extra_row >= 24) & (extra_row < 32)
    ones_row = (extra_row == 16) | (extra_row == 17) | ((extra_row >= 32) & (extra_row < 35))
    k_hits = one_hot(variates) & (extra_row < 16) | is_doc(docs) & doc_row | ones_row
    k_aug = jnp.where(k_hits, 1.0, 0.0).astype(LOW)

    def query_extra(layer):
        same, other = variate_bias[layer, 0, my_head], variate_bias[layer, 1, my_head]
        gap = same - other
        gap_lead, other_lead = (part.astype(LOW).astype(jnp.float32) for part in (gap, other))
        gap_part = jnp.where(extra_row < VARIATES, gap_lead, gap - gap_lead)
        other_part = jnp.where(extra_row == 16, other_lead, other - other_lead)
        spread_gap = jnp.where(one_hot(q_variates), gap_part, 0.0)
        shut = jnp.where(doc_row & ~is_doc(q_docs), FLOOR_SCORE, 0.0)
        tail = jnp.where(extra_row < 18, other_part, shut)
        return jnp.where(extra_row < 16, spread_gap, tail).astype(LOW)

    q_augs = [query_extra(layer) for layer in range(LAYERS)]
    q_onehots = (q_variates[:, None, :] == jnp.arange(VARIATES, dtype=jnp.int32)[:, None]).astype(
        jnp.float32
    )

    half_dim = HD // 2
    frequency = jnp.exp(jnp.arange(half_dim).astype(jnp.float32) * (-2.0 * math.log(10000.0) / HD))
    times = beside(time_ids.astype(jnp.float32))
    angles = frequency[:, None] * times[None, :]
    cosines, sines = jnp.cos(angles), jnp.sin(angles)
    start_normed, later_weights, k_aug, cosines, sines, *q_augs = lax.optimization_barrier(
        (start_normed, later_weights, k_aug, cosines, sines, *q_augs)
    )

    def rotate(values, sines):
        former, latter = values[:, :half_dim], values[:, half_dim:]
        return jnp.concatenate(
            [former * cosines - latter * sines, latter * cosines + former * sines], axis=1
        )

    def to_heads(value):
        if spread > 1:
            value = jnp.repeat(value, spread, axis=0)
        return lax.all_to_all(
            value, "seq", split_axis=0, concat_axis=0, tiled=True, axis_index_groups=plane_groups
        )

    def all_blocks(value):
        if spread == 1:
            return value
        zeros = jnp.zeros((planes,) + value.shape[1:], value.dtype)
        return lax.dynamic_update_slice_in_dim(zeros, value, first_tile, 0)

    def over_spread(value):
        if spread == 1:
            return value
        value = value.reshape((QUARTER_HEADS, spread) + value.shape[1:])
        return jnp.sum(value.astype(jnp.float32), axis=1).astype(LOW)

    def from_heads(value):
        return over_spread(
            lax.all_to_all(
                value, "seq", split_axis=0, concat_axis=0, tiled=True, axis_index_groups=plane_groups
            )
        )

    chip_groups = [
        [place_of(plane, lo, y, core) for plane in range(planes) for lo in range(2) for y in range(2)]
        for core in range(2)
    ]

    def over_chips(value):
        shape = value.shape
        value = value.reshape(-1, *shape[2:])
        value = lax.all_to_all(
            value, BOTH, split_axis=0, concat_axis=0, tiled=True, axis_index_groups=chip_groups
        )
        return value.reshape(shape)

    chip_flips = jnp.reshape(my_quarter, (1,)).astype(jnp.int32)

    def plane_order(value):
        grid = [[value[:, 2 * lo + y] for y in range(2)] for lo in range(2)]
        grid = xor_order(grid, here_lo, here_y)
        return jnp.stack([*grid[0], *grid[1]])

    def chip_order(value):
        grid = xor_order([[value[0], value[1]], [value[2], value[3]]], here_lo, here_y)
        return jnp.stack([*grid[0], *grid[1]], axis=1)

    def share_for_out(middle_low, attended):
        pieces = attended.reshape(4, quarter_width, tok_rows)
        cuts = quarter_width // tok_rows

        def joined(piece):
            parts = [piece[cut * tok_rows : (cut + 1) * tok_rows] for cut in range(cuts)]
            return jnp.concatenate([middle_low, *parts], axis=1)

        came = neighbours(*(joined(piece) for piece in pieces[1:]))
        tokens_low = jnp.concatenate([middle_low, *(part[:, :D] for part in came)], axis=0)

        def results(part):
            return jnp.concatenate(
                [part[:, D + cut * tok_rows : D + (cut + 1) * tok_rows] for cut in range(cuts)], axis=0
            )

        return tokens_low, jnp.concatenate([pieces[0], *(results(part) for part in came)], axis=1)

    stream = tokens
    saved = []
    for layer in range(LAYERS):
        qkv_matrix, out_quarter = attention_weights[layer]
        if layer == 0:
            scaled_one, inverse_one, normed = start_scaled, start_inverse, start_normed
        else:
            scaled_one, inverse_one = normalize(stream)
            normed = beside(scaled_one.astype(LOW))
        projected = dot(qkv_matrix, normed, TT).reshape(QUARTER_HEADS, 3 * HD, cols)
        query = rotate(projected[:, :HD], sines) * (1.0 / math.sqrt(HD))
        key = rotate(projected[:, HD : 2 * HD], sines)
        sent = jnp.concatenate([query, key, projected[:, 2 * HD :]], axis=1).astype(LOW)
        if layer == 0:
            sent, later_weights = lax.optimization_barrier((sent, later_weights))
            later_weights, cotangent = lax.optimization_barrier((cross_rows(later_weights), cotangent))
            last_grad_low = beside(cotangent.astype(LOW))
        own = to_heads(sent)
        next_part = ffn_part(layer, cut(later_weights)[layer])
        own, next_part, last_grad_low = lax.optimization_barrier((own, next_part, last_grad_low))
        packed = gather(next_part).reshape(2 * planes, -1, BLOCK)
        ffn_weights.append(packed)
        own, out_quarter = lax.optimization_barrier((own, out_quarter))
        out_parts = [out_quarter, *neighbours(out_quarter, out_quarter, out_quarter)]
        sib = lax.ppermute(own[:, HD:], "head", CORE_SWAP)
        queries = my_tiles(own)
        q_aug = q_augs[layer]
        out, lse = attention_forward(chip_flips, queries, q_aug, own, sib, k_aug)
        out, *out_parts = lax.optimization_barrier((out, *out_parts))
        out_matrix = jnp.concatenate(out_parts, axis=0)
        out_weights.append(out_matrix)
        attended = over_spread(over_chips(all_blocks(out))).reshape(QUARTER_HEADS, 4, HD, tok_rows)
        attended = plane_order(attended).reshape(D, tok_rows)
        middle = stream + dot(attended, out_matrix, TN)
        scaled_two, inverse_two = normalize(middle)
        normed_ffn = beside(scaled_two.astype(LOW))
        if layer < LAYERS - 1:
            next_part = attention_part(layer + 1, cut(later_weights)[LAYERS + layer])
            normed_ffn, next_part = lax.optimization_barrier((normed_ffn, next_part))
            attention_weights.append(attention_matrices(next_part))
        both, hidden, *parts = ffn_forward(normed_ffn, packed, quarter_ff, group_rows, padded)
        saved.append(
            (
                scaled_one, inverse_one, normed, own, sib, queries, q_aug, out, lse, attended,
                scaled_two, inverse_two, normed_ffn, both, hidden,
            )
        )
        if layer < LAYERS - 1:
            stream = middle + fold(*parts)
        else:
            last_middle, last_parts = middle, parts

    upstream = cotangent
    whole_grads, ffn_sums, qkv_sums = [None] * LAYERS, [None] * LAYERS, [None] * LAYERS
    bias_parts = [None] * LAYERS
    for layer in reversed(range(LAYERS)):
        qkv_matrix, unused = attention_weights[layer]
        out_matrix, packed = out_weights[layer], ffn_weights[layer]
        (
            scaled_one, inverse_one, normed, own, sib, queries, q_aug, out, lse, attended,
            scaled_two, inverse_two, normed_ffn, both, hidden,
        ) = saved[layer]
        upstream_low = beside(upstream.astype(LOW)) if layer < LAYERS - 1 else last_grad_low
        grad_units, *parts = ffn_backward(upstream_low, packed, both, quarter_ff, group_rows, padded)
        inner = fold(*parts)
        buffer = weight_grad(
            None, ffn_end, normed_ffn.T, grad_units, "blocks", group_rows, 0, 4 * padded // group_rows
        )
        inner, buffer = lax.optimization_barrier((inner, buffer))
        buffer = weight_grad(
            buffer, ffn_end, hidden.T, upstream_low, "columns", padded, unit_end, D // BLOCK
        )
        grad_middle = upstream + normalize_back(scaled_two, inverse_two, inner)
        middle_low = grad_middle.astype(LOW)
        grad_attended = dot(out_matrix, middle_low, NT).astype(LOW)
        grad_attended = chip_order(grad_attended.reshape(4, QUARTER_HEADS, HD, tok_rows))
        if spread > 1:
            grad_attended = jnp.repeat(grad_attended, spread, axis=0)
        out_grad = my_tiles(over_chips(grad_attended))
        buffer, out_grad, middle_low, attended = lax.optimization_barrier(
            (buffer, out_grad, middle_low, attended)
        )
        if layer < LAYERS - 1:
            buffer, qkv_sums[layer + 1] = lax.optimization_barrier((buffer, qkv_sums[layer + 1]))
        ffn_sums[layer] = scatter(buffer)
        middle_low, attended = share_for_out(middle_low, attended)
        grad_q, grad_kv = attention_backward(
            chip_flips, queries, q_aug, lse, out, out_grad, own, sib, k_aug
        )
        grad_kv, middle_low, attended = lax.optimization_barrier((grad_kv, middle_low, attended))
        if not split_heads:
            whole_grads[layer] = whole_out_back(dot(attended, middle_low, NN))
        else:
            out_blocks = weight_grad(
                None, out_end - ffn_end, attended, middle_low, "columns", w_rows, 0, D // BLOCK
            )
        same_grad = jnp.sum(grad_q[:, HD : HD + VARIATES] * q_onehots)
        all_grad = jnp.sum(grad_q[:, HD + 16])
        crossed = lax.ppermute(grad_kv[planes:], "head", CORE_SWAP)
        grad_kv = (grad_kv[:planes].astype(jnp.float32) + crossed.astype(jnp.float32)).astype(LOW)
        grad_q = (grad_q[:, :HD] * (1.0 / math.sqrt(HD))).astype(LOW)
        if layer == LAYERS - 1:
            grad_kv, *last_parts = lax.optimization_barrier((grad_kv, *last_parts))
            stream = last_middle + fold(*last_parts)
        grad_heads = from_heads(jnp.concatenate([all_blocks(grad_q), grad_kv], axis=1))
        if layer == LAYERS - 1:
            grad_heads, stream = lax.optimization_barrier((grad_heads, stream))
        grad_heads = jnp.concatenate(
            [
                rotate(grad_heads[:, :HD].astype(jnp.float32), -sines).astype(LOW),
                rotate(grad_heads[:, HD : 2 * HD].astype(jnp.float32), -sines).astype(LOW),
                grad_heads[:, 2 * HD :],
            ],
            axis=1,
        ).reshape(3 * quarter_width, cols)
        bias_parts[layer] = jnp.stack([same_grad, all_grad - same_grad])
        partial = dot(grad_heads, qkv_matrix, TT)
        qkv_grad = dot(normed, grad_heads, TT).astype(LOW)
        qkv_grad, ffn_sums[layer] = lax.optimization_barrier((qkv_grad, ffn_sums[layer]))
        if split_heads:
            qkv_grad = jnp.concatenate([qkv_grad, out_blocks.reshape(-1, BLOCK)], axis=1)
        if layer > 0:
            inner = fold_whole(partial)
            inner, qkv_grad = lax.optimization_barrier((inner, qkv_grad))
        qkv_sums[layer] = scatter(qkv_grad)
        if layer == 0:
            qkv_sums[0], partial, *bias_parts = lax.optimization_barrier(
                (qkv_sums[0], partial, *bias_parts)
            )
            inner = fold_whole(partial)
        upstream = grad_middle + normalize_back(scaled_one, inverse_one, inner)

    bias_local = lax.dynamic_update_slice(
        jnp.zeros((LAYERS, 2, HEADS), jnp.float32), jnp.stack(bias_parts)[:, :, None], (0, 0, my_head)
    )
    bias_total = bias_local
    for axis, size in (("head", 4), ("seq", seq)):
        hop = 1
        while hop < size:
            swap = [(place, place ^ hop) for place in range(size)]
            bias_total = bias_total + lax.ppermute(bias_total, axis, swap)
            hop *= 2

    later_sums = [from_blocks(member[None, :unit_end], group_rows) for member in ffn_sums]
    out_sums = [member[:, 3 * quarter_width :] for member in qkv_sums]
    qkv_sums = [member[:, : 3 * quarter_width] for member in qkv_sums]
    if not split_heads:
        out_sums = [member[:, :BLOCK] for member in qkv_sums]
    later_sums = jnp.concatenate([*later_sums, *qkv_sums[1:]], axis=1)
    quarters = jnp.arange(QUARTERS, dtype=jnp.int32)
    weights = (w_query, w_key, w_value, w_gate, w_up)
    gains = (gain_attn[:, :, None], gain_ffn[:, :, None])
    *grads, gain_one, gain_two = finish_gradients(
        quarters ^ (2 * here_y + here_core), cross_back(later_sums), ffn_sums,
        out_sums[1:], weights, gains, w_down.shape, unit_end, planes, split_heads,
    )
    *grads[:3], gain_one, grads[3] = finish_first(
        2 * quarters + here_lo, cross_back_at_once(qkv_sums[0]), out_sums[0], weights[:3], gains[0],
        [*grads[:3], gain_one, grads[3]], split_heads,
    )
    if not split_heads:
        grads[3] = jnp.stack(whole_grads).astype(jnp.float32)
    return (stream, upstream, *grads, gain_one[:, :, 0], gain_two[:, :, 0], bias_total)


def solution(mesh):
    rows = P(BOTH, None)
    middle = P(None, BOTH, None)
    gains = P(None, BOTH)
    return jax.shard_map(
        on_device,
        mesh=mesh,
        in_specs=(rows,) + (middle,) * 7 + (gains,) * 2 + (P(),) * 3 + (P(BOTH), rows),
        out_specs=(rows, rows) + (middle,) * 7 + (gains,) * 2 + (P(),),
        check_vma=False,
    )
```

```python
import functools
import math

import jax
import jax.numpy as jnp
from jax import lax
from jax.experimental import pallas as pl
from jax.experimental.pallas import tpu as pltpu
from jax.sharding import PartitionSpec as P

D = 1024
HEADS = 16
HD = 64
LAYERS = 2
VARIATES = 8
BLOCK = 256

NORM_EPS = 1e-05
FLOOR_SCORE = -1e30
LOW = jnp.bfloat16
BOTH = ("seq", "head")

QUARTERS = 4
QUARTER_HEADS = HEADS // QUARTERS
Y_SWAP = [(place, place ^ 2) for place in range(4)]
CORE_SWAP = [(place, place ^ 1) for place in range(4)]

NN = (((1,), (0,)), ((), ()))
NT = (((1,), (1,)), ((), ()))
TN = (((0,), (0,)), ((), ()))
TT = (((0,), (1,)), ((), ()))
VMEM_LIMIT = 56 * 1024 * 1024


def cost(flops, operands, results, transcendentals=0):
    moved = sum(member.size * member.dtype.itemsize for member in [*operands, *results])
    return pl.CostEstimate(flops=flops, bytes_accessed=moved, transcendentals=transcendentals)


def dot(left, right, dims):
    return lax.dot_general(left, right, dims, preferred_element_type=jnp.float32)


def forward_kernel(flip_ref, q_ref, q_aug_ref, own_ref, sib_ref, k_aug_ref, out_ref, lse_ref):
    blocks = own_ref.shape[0]
    sources = ((own_ref, HD), (sib_ref, 0))
    spots = [(half, block) for half in range(2) for block in range(blocks)]
    cols = q_ref.shape[-1]
    q_side = jnp.concatenate([q_ref[0, :HD, :], q_aug_ref[0]], axis=0).T
    top = jnp.full((cols, 1), FLOOR_SCORE, jnp.float32)
    total = jnp.zeros((cols, 1), jnp.float32)
    acc = jnp.zeros((cols, HD), jnp.float32)

    def scores(half, block):
        ref, low_row = sources[half]
        extra = k_aug_ref[half * blocks + block]
        k_side = jnp.concatenate([ref[block, low_row : low_row + HD, :], extra], axis=0)
        return dot(q_side, k_side, NN)

    following = scores(*spots[0])
    for number, (half, block) in enumerate(spots):
        part = following
        if number + 1 < len(spots):
            following = scores(*spots[number + 1])
        fresh = jnp.maximum(top, jnp.max(part, axis=-1, keepdims=True))
        shrink = jnp.exp(top - fresh)
        prob = jnp.exp(part - fresh)
        total = total * shrink + jnp.sum(prob, axis=-1, keepdims=True)
        ref, low_row = sources[half]
        values = ref[block, low_row + HD : low_row + 2 * HD, :]
        acc = acc * shrink + dot(prob.astype(LOW), values, NT)
        top = fresh
    result = acc / total
    lse = jnp.broadcast_to(top + jnp.log(total), (cols, HD))
    both = jnp.concatenate([result, lse], axis=1).T
    piece = out_ref.shape[-1]
    for place in range(cols // piece):
        part = both[:HD, place * piece : (place + 1) * piece]
        out_ref[0, place ^ flip_ref[0]] = part.astype(LOW)
    lse_ref[0] = both[HD : HD + 8]


def split_rows(row, rows):
    one = row.astype(LOW).astype(jnp.float32)
    two = (row - one).astype(LOW).astype(jnp.float32)
    three = row - one - two
    pad = jnp.zeros((rows - 3, row.shape[-1]), jnp.float32)
    return jnp.concatenate([one, two, three, pad], axis=0).astype(LOW)


def backward_kernel(
    flip_ref, q_ref, q_aug_ref, lse_ref, out_ref, grad_ref, own_ref, sib_ref, k_aug_ref,
    dq_ref, dkv_ref, dkv_acc,
):
    step = pl.program_id(0)
    blocks = own_ref.shape[0]
    sources = ((own_ref, HD), (sib_ref, 0))
    cols, key_cols = q_ref.shape[-1], own_ref.shape[-1]

    @pl.when(step == 0)
    def _():
        dkv_acc[...] = jnp.zeros_like(dkv_acc)

    q_low = q_ref[0, :HD, :]
    places = range(grad_ref.shape[1])
    g_low = jnp.concatenate([grad_ref[0, place ^ flip_ref[0]] for place in places], axis=1)
    out = jnp.concatenate([out_ref[0, place ^ flip_ref[0]] for place in places], axis=1)
    row_dot = jnp.sum(g_low.astype(jnp.float32) * out.astype(jnp.float32), axis=0, keepdims=True)
    aug = jnp.concatenate(
        [q_aug_ref[0, :32, :], split_rows(-lse_ref[0, :1, :], 16), q_aug_ref[0, 48:, :]], axis=0
    )
    q_side = jnp.concatenate([q_low, aug], axis=0).T
    g_side = jnp.concatenate([g_low, split_rows(-row_dot, HD)], axis=0).T
    ones = jnp.concatenate(
        [jnp.ones((16, key_cols), LOW), jnp.zeros((HD - 16, key_cols), LOW)], axis=0
    )
    dq = jnp.zeros((cols, 2 * HD), jnp.float32)
    spots = [(half, block) for half in range(2) for block in range(blocks)]

    def products(half, block):
        ref, low_row = sources[half]
        k_side = jnp.concatenate(
            [ref[block, low_row : low_row + HD, :], k_aug_ref[half * blocks + block]], axis=0
        )
        v_side = jnp.concatenate([ref[block, low_row + HD : low_row + 2 * HD, :], ones], axis=0)
        return k_side, dot(q_side, k_side, NN), dot(g_side, v_side, NN)

    following = products(*spots[0])
    for spot in range(len(spots)):
        k_side, score, prob_grad = following
        if spot + 1 < len(spots):
            following = products(*spots[spot + 1])
        prob = jnp.exp(score)
        score_grad = (prob * prob_grad).astype(LOW)
        dq = dq + dot(score_grad, k_side, NT)
        dkv_acc[spot, :HD, :] += dot(q_low, score_grad, NN)
        dkv_acc[spot, HD:, :] += dot(g_low, prob.astype(LOW), NN)
    dq_ref[0] = dq.T

    @pl.when(step == pl.num_programs(0) - 1)
    def _():
        dkv_ref[...] = dkv_acc[...].astype(LOW)


def whole_spec(shape):
    rank = len(shape)
    return pl.BlockSpec(shape, lambda i, flip: (0,) * rank)


def tile_spec(rows, cols):
    return pl.BlockSpec((1, rows, cols), lambda i, flip: (i, 0, 0))


def owner_spec(shape):
    return pl.BlockSpec((1, *shape[1:]), lambda i, flip: (i, 0, 0, 0))


def attention_forward(flip, queries, q_aug, own, sib, k_aug):
    tiles, unused, cols = queries.shape
    pairs = 2 * tiles * own.shape[0] * cols * cols
    out_shape = (tiles, 4, HD, cols // 4)
    results = [
        jax.ShapeDtypeStruct(out_shape, LOW),
        jax.ShapeDtypeStruct((tiles, 8, cols), jnp.float32),
    ]
    return pl.pallas_call(
        forward_kernel,
        grid_spec=pltpu.PrefetchScalarGridSpec(
            num_scalar_prefetch=1,
            grid=(tiles,),
            in_specs=[tile_spec(3 * HD, cols), tile_spec(HD, cols)]
            + [whole_spec(member.shape) for member in (own, sib, k_aug)],
            out_specs=[owner_spec(out_shape), tile_spec(8, cols)],
        ),
        out_shape=results,
        cost_estimate=cost(16 * HD * pairs, [queries, own, sib], results, pairs),
        compiler_params=pltpu.CompilerParams(vmem_limit_bytes=VMEM_LIMIT),
        name="attention_forward",
    )(flip, queries, q_aug, own, sib, k_aug)


def attention_backward(flip, queries, q_aug, lse, out, grad, own, sib, k_aug):
    tiles, unused, cols = queries.shape
    dkv_shape = (2 * own.shape[0], 2 * HD, cols)
    pairs = 2 * tiles * own.shape[0] * cols * cols
    results = [
        jax.ShapeDtypeStruct((tiles, 2 * HD, cols), jnp.float32),
        jax.ShapeDtypeStruct(dkv_shape, LOW),
    ]
    return pl.pallas_call(
        backward_kernel,
        grid_spec=pltpu.PrefetchScalarGridSpec(
            num_scalar_prefetch=1,
            grid=(tiles,),
            in_specs=[tile_spec(3 * HD, cols), tile_spec(HD, cols), tile_spec(8, cols)]
            + [owner_spec(out.shape)] * 2
            + [whole_spec(member.shape) for member in (own, sib, k_aug)],
            out_specs=[tile_spec(2 * HD, cols), whole_spec(dkv_shape)],
            scratch_shapes=[pltpu.VMEM(dkv_shape, jnp.float32)],
        ),
        out_shape=results,
        cost_estimate=cost(32 * HD * pairs, [queries, own, sib], results, pairs),
        compiler_params=pltpu.CompilerParams(vmem_limit_bytes=VMEM_LIMIT),
        name="attention_backward",
    )(flip, queries, q_aug, lse, out, grad, own, sib, k_aug)


def silu_parts(gate):
    sigmoid = 1.0 / (1.0 + jnp.exp(-gate))
    return sigmoid, gate * sigmoid


def put_parts(values, lanes, own_ref, *low_refs):
    rows = own_ref.shape[0]
    own_ref[:, lanes] = values[:rows]
    for place, low_ref in enumerate(low_refs):
        low_ref[:, lanes] = values[(place + 1) * rows : (place + 2) * rows].astype(LOW)


def parts_of(tokens, lanes, index):
    shape = (tokens // 4, D)
    types = [jnp.float32, LOW, LOW, LOW]
    return (
        [jax.ShapeDtypeStruct(shape, kind) for kind in types],
        [pl.BlockSpec((tokens // 4, lanes), index) for unused in types],
    )


def join_rows(x_ref, refs):
    @pl.when(pl.program_id(0) == 0)
    def _():
        rows = refs[0].shape[0]
        for place, ref in enumerate(refs):
            x_ref[place * rows : (place + 1) * rows, :] = ref[...]


def ffn_forward_kernel(*refs, unit_rows, down_rows, unit_steps):
    unit_ref, down_ref, both_ref, hidden_ref = refs[4:8]
    out_refs, x_ref = refs[8:12], refs[12]
    join_rows(x_ref, refs[:4])
    step = pl.program_id(0)
    half = BLOCK // 2

    @pl.when(step < unit_steps)
    def _():
        count = unit_ref.shape[1] // unit_rows
        for place in range(count):
            matrix = unit_ref[:, place * unit_rows : (place + 1) * unit_rows, :].reshape(-1, BLOCK)
            both = dot(x_ref[...], matrix, NN)
            both_ref[place] = both.astype(both_ref.dtype)
            hidden = silu_parts(both[:, :half])[1] * both[:, half:]
            spot = step * count + place
            hidden_ref[:, pl.ds(pl.multiple_of(spot * half, half), half)] = hidden.astype(LOW)

    @pl.when(step >= unit_steps)
    def _():
        for place in range(down_ref.shape[1] // down_rows):
            matrix = down_ref[:, place * down_rows : (place + 1) * down_rows, :].reshape(-1, BLOCK)
            lanes = slice(place * BLOCK, (place + 1) * BLOCK)
            put_parts(dot(hidden_ref[...], matrix, NN), lanes, *out_refs)


def ffn_backward_kernel(*refs, unit_rows, down_rows, down_steps):
    unit_ref, down_ref, both_ref, grads_ref = refs[4:8]
    part_refs, inner_ref, hidden_grad, g_ref = refs[8:12], refs[12], refs[13], refs[14]
    join_rows(g_ref, refs[:4])
    step = pl.program_id(0)
    half = BLOCK // 2

    @pl.when(step < down_steps)
    def _():
        total = 0.0
        for place in range(down_ref.shape[1] // down_rows):
            matrix = down_ref[:, place * down_rows : (place + 1) * down_rows, :].reshape(-1, BLOCK)
            lanes = pl.ds(pl.multiple_of((step * FFN_DOWNS + place) * BLOCK, BLOCK), BLOCK)
            total = total + dot(g_ref[:, lanes], matrix, NT)

        @pl.when(step == 0)
        def _():
            hidden_grad[...] = total

        @pl.when(step > 0)
        def _():
            hidden_grad[...] += total

    @pl.when(step >= down_steps)
    def _():
        count = unit_ref.shape[1] // unit_rows
        total = 0.0
        for place in range(count):
            matrix = unit_ref[:, place * unit_rows : (place + 1) * unit_rows, :].reshape(-1, BLOCK)
            spot = (step - down_steps) * count + place
            gate = both_ref[place, :, :half].astype(jnp.float32)
            upward = both_ref[place, :, half:].astype(jnp.float32)
            above = hidden_grad[:, pl.ds(pl.multiple_of(spot * half, half), half)]
            sigmoid, silu = silu_parts(gate)
            grad_gate = above * upward * (sigmoid * (1.0 + gate * (1.0 - sigmoid)))
            grads = jnp.concatenate([grad_gate, above * silu], axis=1).astype(LOW)
            grads_ref[place] = grads
            total = total + dot(grads, matrix, NT)

        @pl.when(step == down_steps)
        def _():
            inner_ref[...] = total

        @pl.when(step > down_steps)
        def _():
            inner_ref[...] += total

    @pl.when(step == pl.num_programs(0) - 1)
    def _():
        put_parts(inner_ref[...], slice(0, D), *part_refs)


FFN_DOWNS = 4


def ffn_units(cols_ff):
    return max(count for count in (1, 2, 3) if 2 * cols_ff // BLOCK % count == 0)


def ffn_specs(cols_ff, unit_rows, down_rows, groups, unit_step, down_step):
    unit_blocks, down_blocks = 2 * cols_ff // BLOCK, D // BLOCK
    units, downs = ffn_units(cols_ff) * unit_rows, FFN_DOWNS * down_rows
    first_down = unit_blocks * unit_rows // downs
    return (
        unit_blocks // ffn_units(cols_ff),
        down_blocks // FFN_DOWNS,
        [
            pl.BlockSpec((groups, units, BLOCK), lambda i: (0, unit_step(i), 0)),
            pl.BlockSpec((groups, downs, BLOCK), lambda i: (0, first_down + down_step(i), 0)),
        ],
    )


def ffn_forward(rows, packed, cols_ff, unit_rows, down_rows):
    tokens, unit_steps = 4 * rows[0].shape[0], 2 * cols_ff // BLOCK // ffn_units(cols_ff)
    unit_step = lambda i: jnp.minimum(i, unit_steps - 1)
    down_step = lambda i: jnp.maximum(i - unit_steps, 0)
    unit_steps, down_steps, specs = ffn_specs(
        cols_ff, unit_rows, down_rows, packed.shape[0], unit_step, down_step
    )
    parts, part_specs = parts_of(tokens, FFN_DOWNS * BLOCK, lambda i: (0, down_step(i)))
    results = [
        jax.ShapeDtypeStruct((2 * cols_ff // BLOCK, tokens, BLOCK), LOW),
        jax.ShapeDtypeStruct((tokens, cols_ff), LOW),
        *parts,
    ]
    return pl.pallas_call(
        functools.partial(
            ffn_forward_kernel, unit_rows=unit_rows, down_rows=down_rows, unit_steps=unit_steps
        ),
        grid=(unit_steps + down_steps,),
        in_specs=[pl.BlockSpec(rows[0].shape, lambda i: (0, 0))] * 4 + specs,
        out_specs=[
            pl.BlockSpec((ffn_units(cols_ff), tokens, BLOCK), lambda i: (unit_step(i), 0, 0)),
            pl.BlockSpec((tokens, cols_ff), lambda i: (0, 0)),
            *part_specs,
        ],
        out_shape=results,
        scratch_shapes=[pltpu.VMEM((tokens, D), LOW)],
        cost_estimate=cost(6 * tokens * D * cols_ff, [*rows, packed], results),
        compiler_params=pltpu.CompilerParams(vmem_limit_bytes=VMEM_LIMIT),
        name="ffn_forward",
    )(*rows, packed, packed)


def ffn_backward(rows, packed, both, cols_ff, unit_rows, down_rows):
    tokens, down_steps = 4 * rows[0].shape[0], D // BLOCK // FFN_DOWNS
    unit_step = lambda i: jnp.maximum(i - down_steps, 0)
    down_step = lambda i: jnp.minimum(i, down_steps - 1)
    unit_steps, down_steps, specs = ffn_specs(
        cols_ff, unit_rows, down_rows, packed.shape[0], unit_step, down_step
    )
    unit_spec = pl.BlockSpec((ffn_units(cols_ff), tokens, BLOCK), lambda i: (unit_step(i), 0, 0))
    parts, part_specs = parts_of(tokens, D, lambda i: (0, 0))
    results = [jax.ShapeDtypeStruct((2 * cols_ff // BLOCK, tokens, BLOCK), LOW), *parts]
    return pl.pallas_call(
        functools.partial(
            ffn_backward_kernel, unit_rows=unit_rows, down_rows=down_rows, down_steps=down_steps
        ),
        grid=(unit_steps + down_steps,),
        in_specs=[pl.BlockSpec(rows[0].shape, lambda i: (0, 0))] * 4 + [*specs, unit_spec],
        out_specs=[unit_spec, *part_specs],
        out_shape=results,
        scratch_shapes=[
            pltpu.VMEM((tokens, D), jnp.float32),
            pltpu.VMEM((tokens, cols_ff), jnp.float32),
            pltpu.VMEM((tokens, D), LOW),
        ],
        cost_estimate=cost(6 * tokens * D * cols_ff, [*rows, packed, both], results),
        compiler_params=pltpu.CompilerParams(vmem_limit_bytes=VMEM_LIMIT),
        name="ffn_backward",
    )(*rows, packed, packed, both)


def ffn_weight_grads_kernel(*refs, unit_rows, down_rows):
    unit_grads_ref, hidden_ref, g_refs, out_ref, x_ref = refs[4], refs[5], refs[6:10], refs[10], refs[11]
    step, last = pl.program_id(0), pl.num_programs(0) - 1

    @pl.when(step == 0)
    def _():
        rows = refs[0].shape[0]
        for place, ref in enumerate(refs[:4]):
            x_ref[:, place * rows : (place + 1) * rows] = ref[...].T

    @pl.when(step < last)
    def _():
        for place in range(out_ref.shape[1] // unit_rows):
            grad = dot(x_ref[...], unit_grads_ref[place], NN)
            grad = grad.reshape(-1, unit_rows, BLOCK).astype(LOW)
            out_ref[:, place * unit_rows : (place + 1) * unit_rows, :] = grad

    @pl.when(step == last)
    def _():
        hidden = hidden_ref[...].T
        for place in range(out_ref.shape[1] // down_rows):
            lanes = slice(place * BLOCK, (place + 1) * BLOCK)
            right = jnp.concatenate([ref[:, lanes] for ref in g_refs], axis=0)
            grad = dot(hidden, right, NN).reshape(-1, down_rows, BLOCK).astype(LOW)
            out_ref[:, place * down_rows : (place + 1) * down_rows, :] = grad


def ffn_weight_grads(rows, unit_grads, hidden, grad_rows, groups, unit_rows, down_rows):
    tokens, cols_ff = hidden.shape
    step_rows = D // BLOCK * down_rows
    per_step = step_rows // unit_rows
    steps = unit_grads.shape[0] // per_step
    last = steps - 1
    result = jax.ShapeDtypeStruct((groups, (steps + 1) * step_rows, BLOCK), LOW)
    part_spec = pl.BlockSpec(rows[0].shape, lambda i: (0, 0))
    return pl.pallas_call(
        functools.partial(ffn_weight_grads_kernel, unit_rows=unit_rows, down_rows=down_rows),
        grid=(steps + 1,),
        in_specs=[part_spec] * 4
        + [
            pl.BlockSpec((per_step, tokens, BLOCK), lambda i: (jnp.minimum(i, last), 0, 0)),
            pl.BlockSpec(hidden.shape, lambda i: (0, 0)),
        ]
        + [part_spec] * 4,
        out_specs=pl.BlockSpec((groups, step_rows, BLOCK), lambda i: (0, i, 0)),
        out_shape=result,
        scratch_shapes=[pltpu.VMEM((D, tokens), LOW)],
        cost_estimate=cost(6 * tokens * D * cols_ff, [*rows, unit_grads, hidden, *grad_rows], [result]),
        compiler_params=pltpu.CompilerParams(vmem_limit_bytes=VMEM_LIMIT),
        name="ffn_weight_grads",
    )(*rows, unit_grads, hidden, *grad_rows)


def out_grad_kernel(left_ref, right_ref, out_ref, *, rows):
    for place in range(D // BLOCK):
        grad = dot(left_ref[...], right_ref[:, place * BLOCK : (place + 1) * BLOCK], NN)
        out_ref[:, place * rows : (place + 1) * rows, :] = grad.reshape(-1, rows, BLOCK).astype(LOW)


def out_weight_grad(left, right, rows):
    result = jax.ShapeDtypeStruct((left.shape[0] // rows, D // BLOCK * rows, BLOCK), LOW)
    return pl.pallas_call(
        functools.partial(out_grad_kernel, rows=rows),
        in_specs=in_vmem(2),
        out_specs=in_vmem(1)[0],
        out_shape=result,
        cost_estimate=cost(2 * left.size * D, [left, right], [result]),
        compiler_params=pltpu.CompilerParams(vmem_limit_bytes=VMEM_LIMIT),
        name="out_weight_grad",
    )(left, right)


def put_qkv(came_ref, place_ref, start, outs, layer, weights, gain_ref, gain_out_ref):
    for quarter in range(QUARTERS):
        part = came_ref[place_ref[quarter], :, start : start + 3 * QUARTER_HEADS * HD]
        part = part.astype(jnp.float32)
        for slot in range(QUARTER_HEADS):
            column = HD * (QUARTERS * slot + quarter)
            for which, out_ref in enumerate(outs):
                first = (3 * slot + which) * HD
                out_ref[layer, :, column : column + HD] = part[:, first : first + HD]
    gain_grad = 0.0
    for out_ref, weight_ref in zip(outs, weights):
        grad = out_ref[layer]
        gain_grad = gain_grad + jnp.sum(grad * weight_ref[layer], axis=1, keepdims=True)
        out_ref[layer] = grad * gain_ref[layer]
    gain_out_ref[layer] = jnp.broadcast_to(gain_grad, gain_out_ref.shape[1:])


def put_units(came_ref, place_ref, start, outs, layer, weights, gain_ref, gain_out_ref, d_rows, padded, planes):
    half = BLOCK // 2
    for quarter in range(QUARTERS):
        part = came_ref[place_ref[quarter], :, start : start + 4 * planes * padded]
        part = part.astype(jnp.float32)
        for plane in range(planes):
            for core in range(2):
                column = d_rows * (8 * plane + 2 * quarter + core)
                unit, end = (2 * plane + core) * padded, (2 * plane + core) * padded + d_rows
                while unit < end:
                    stop = min(end, (unit // half + 1) * half)
                    for which, out_ref in enumerate(outs):
                        first = unit // half * BLOCK + which * half + unit % half
                        out_ref[layer, :, column : column + stop - unit] = part[
                            :, first : first + stop - unit
                        ]
                    column, unit = column + stop - unit, stop
    gain_grad = 0.0
    for out_ref, weight_ref in zip(outs, weights):
        grad = out_ref[layer]
        gain_grad = gain_grad + jnp.sum(grad * weight_ref[layer], axis=1, keepdims=True)
        out_ref[layer] = grad * gain_ref[layer]
    gain_out_ref[layer] = jnp.broadcast_to(gain_grad, gain_out_ref.shape[1:])


def finish_kernel(place_ref, *refs, unit_end, w_rows, d_rows, padded, planes, with_out):
    came_ref, *sums = refs[: 1 + LAYERS]
    out_sums, refs = refs[1 + LAYERS : 2 * LAYERS], refs[2 * LAYERS :]
    weights, gains, outs = refs[:5], refs[5:7], refs[7:]
    units_width = 4 * planes * padded
    for layer in range(LAYERS):
        put_units(
            came_ref, place_ref, layer * units_width, outs[4:6], layer, weights[3:], gains[1],
            outs[8], d_rows, padded, planes,
        )
        if layer > 0:
            start = LAYERS * units_width + (layer - 1) * 3 * QUARTER_HEADS * HD
            put_qkv(came_ref, place_ref, start, outs[:3], layer, weights[:3], gains[0], outs[7])
        for block in range(D // BLOCK):
            lanes = slice(block * BLOCK, (block + 1) * BLOCK)
            rows = sums[layer][unit_end + block * padded : unit_end + (block + 1) * padded, :]
            outs[6][layer, :, lanes] = rows.astype(jnp.float32)[:d_rows]
            if with_out and layer > 0:
                rows = out_sums[layer - 1][block * w_rows : (block + 1) * w_rows, :]
                outs[3][layer, :, lanes] = rows.astype(jnp.float32)


def finish_first_kernel(place_ref, came_ref, out_sum_ref, *refs, w_rows, with_out):
    weights, gain_ref, have, outs = refs[:3], refs[3], refs[4:9], refs[9:]
    for layer in range(1, LAYERS):
        for have_ref, out_ref in zip(have, outs):
            out_ref[layer] = have_ref[layer]
    put_qkv(came_ref, place_ref, 0, outs[:3], 0, weights, gain_ref, outs[3])
    if with_out:
        for block in range(D // BLOCK):
            rows = out_sum_ref[block * w_rows : (block + 1) * w_rows, :]
            outs[4][0, :, block * BLOCK : (block + 1) * BLOCK] = rows.astype(jnp.float32)


def in_vmem(count):
    return [pl.BlockSpec(memory_space=pltpu.VMEM)] * count


def finish_gradients(
    place, came, sums, out_sums, weights, gains, d_shape, unit_end, planes, with_out
):
    layers, w_rows, unused = weights[0].shape
    d_rows = d_shape[1]
    padded = -(-d_rows // 16) * 16
    shapes = [weights[0].shape] * 4 + [weights[3].shape] * 2 + [d_shape] + [(layers, w_rows, 128)] * 2
    return pl.pallas_call(
        functools.partial(
            finish_kernel, unit_end=unit_end, w_rows=w_rows, d_rows=d_rows, padded=padded, planes=planes,
            with_out=with_out,
        ),
        in_specs=[pl.BlockSpec(memory_space=pltpu.SMEM)] + in_vmem(7 + 2 * LAYERS),
        out_specs=in_vmem(9),
        out_shape=[jax.ShapeDtypeStruct(shape, jnp.float32) for shape in shapes],
        compiler_params=pltpu.CompilerParams(vmem_limit_bytes=VMEM_LIMIT),
        name="finish_gradients",
    )(place, came, *sums, *out_sums, *weights, *gains)


def finish_first(place, came, out_sum, weights, gain, grads, with_out):
    return pl.pallas_call(
        functools.partial(finish_first_kernel, w_rows=weights[0].shape[1], with_out=with_out),
        in_specs=[pl.BlockSpec(memory_space=pltpu.SMEM)] + in_vmem(11),
        out_specs=in_vmem(5),
        out_shape=[jax.ShapeDtypeStruct(member.shape, jnp.float32) for member in grads],
        compiler_params=pltpu.CompilerParams(vmem_limit_bytes=VMEM_LIMIT),
        name="finish_first",
    )(place, came, out_sum, *weights, gain, *grads)


def on_device(
    tokens,
    w_query,
    w_key,
    w_value,
    w_out,
    w_gate,
    w_up,
    w_down,
    gain_attn,
    gain_ffn,
    variate_bias,
    doc_starts,
    variate_ids,
    time_ids,
    cotangent,
):
    seq = lax.axis_size("seq")
    planes = seq // 2
    spread = planes // QUARTER_HEADS
    tiles = planes // spread
    tok_rows = tokens.shape[0]
    cols = 4 * tok_rows
    all_rows = variate_ids.shape[0]
    w_rows = w_query.shape[1]
    d_rows = w_down.shape[1]
    padded = -(-d_rows // 16) * 16
    quarter_ff = 2 * planes * padded
    quarter_width = QUARTER_HEADS * HD
    split_heads = 2 * w_rows == HD
    here_seq, here_head = lax.axis_index("seq"), lax.axis_index("head")
    here_plane, here_lo = here_seq // 2, here_seq % 2
    here_y, here_core = here_head // 2, here_head % 2
    my_quarter = 2 * here_lo + here_y
    my_head = QUARTERS * (here_plane // spread) + my_quarter
    first_tile = (here_plane % spread) * tiles
    devices = [
        (plane, lo, y, core)
        for plane in range(planes)
        for lo in range(2)
        for y in range(2)
        for core in range(2)
    ]

    def place_of(plane, lo, y, core):
        return 8 * plane + 4 * lo + 2 * y + core

    row_groups = [
        [place_of(plane, lo, y, core) for plane in range(planes) for core in range(2)]
        for lo in range(2)
        for y in range(2)
    ]
    plane_groups = [[2 * plane + lo for plane in range(planes)] for lo in range(2)]
    x_swap = [(place, place ^ 1) for place in range(seq)]
    corner_swap = [
        (place_of(plane, lo, y, core), place_of(plane, 1 - lo, 1 - y, core))
        for plane, lo, y, core in devices
    ]

    def neighbours(across_y, across_x, across_both):
        return (
            lax.ppermute(across_y, "head", Y_SWAP),
            lax.ppermute(across_x, "seq", x_swap),
            lax.ppermute(across_both, BOTH, corner_swap),
        )

    def beside_parts(value):
        return [value, *neighbours(value, value, value)]

    def beside(value):
        return jnp.concatenate(beside_parts(value), axis=0)

    def fold(own, *others):
        return own + sum(part.astype(jnp.float32) for part in neighbours(*others))

    def fold_whole(partial):
        low = partial[tok_rows:].astype(LOW).reshape(3, tok_rows, -1)
        return fold(partial[:tok_rows], low[0], low[1], low[2])

    def flip(pair, bit):
        return jnp.where(bit == 0, pair[0], pair[1]), jnp.where(bit == 0, pair[1], pair[0])

    def xor_order(grid, high, low):
        rows = [flip(row, low) for row in grid]
        first, second = zip(*[flip(column, high) for column in zip(*rows)])
        return [list(first), list(second)]

    def cross_rows(parts):
        grid = xor_order([[parts[0], parts[1]], [parts[2], parts[3]]], here_y, here_core)
        came = [[None, None], [None, None]]
        for high in range(2):
            for low in range(2):
                hops = [
                    (place_of(plane, lo, y, core), place_of(plane, y ^ high, core ^ low, lo))
                    for plane, lo, y, core in devices
                ]
                came[high][low] = lax.ppermute(grid[high][low], BOTH, hops)
        came = xor_order(came, here_lo, here_y)
        return jnp.concatenate([*came[0], *came[1]], axis=0)

    def cross_back(rows):
        parts = [rows[place * w_rows : (place + 1) * w_rows] for place in range(4)]
        grid = xor_order([parts[:2], parts[2:]], here_lo, here_y)
        came = [[None, None], [None, None]]
        for high in range(2):
            for low in range(2):
                hops = [
                    (place_of(plane, lo, y, core), place_of(plane, core, lo ^ high, y ^ low))
                    for plane, lo, y, core in devices
                ]
                came[high][low] = lax.ppermute(grid[high][low], BOTH, hops)
        return jnp.stack([*came[0], *came[1]])

    device_groups = [[8 * plane + place for place in range(8)] for plane in range(planes)]

    def plane_exchange(value):
        return lax.all_to_all(
            value, BOTH, split_axis=0, concat_axis=0, tiled=True, axis_index_groups=device_groups
        )

    def cross_rows_at_once(parts):
        zeros = jnp.zeros_like(parts)
        sent = jnp.stack(
            [jnp.where(here_lo == core, parts, zeros) for core in range(2)], axis=1
        )
        came = plane_exchange(sent.reshape(8, *parts.shape[1:]))
        came = jnp.where(here_core == 0, came[:4], came[4:])
        return came.reshape(-1, parts.shape[-1])

    def cross_back_at_once(rows):
        parts = rows.reshape(4, w_rows, -1)
        zeros = jnp.zeros_like(parts)
        sent = [jnp.where(here_core == lo, parts, zeros) for lo in range(2)]
        return plane_exchange(jnp.concatenate(sent, axis=0))

    def gather(part):
        return lax.all_gather(part, BOTH, axis=0, tiled=True, axis_index_groups=row_groups)

    def blocks_of(matrix):
        rows, n = matrix.shape
        return matrix.reshape(rows, n // BLOCK, BLOCK).transpose(1, 0, 2).reshape(-1, BLOCK)

    def from_blocks(packed, rows):
        groups, count = packed.shape[0], packed.shape[1] // rows
        parts = packed.reshape(groups, count, rows, BLOCK).transpose(0, 2, 1, 3)
        return parts.reshape(groups * rows, count * BLOCK)

    def scatter(packed):
        part = lax.psum_scatter(
            packed.reshape(-1, packed.shape[-1]),
            BOTH,
            scatter_dimension=0,
            tiled=True,
            axis_index_groups=row_groups,
        )
        return part

    def split_qkv(query, key, value):
        stacked = jnp.stack([query, key, value], axis=0)
        stacked = stacked.reshape(3, w_rows, QUARTER_HEADS, QUARTERS, HD)
        return stacked.transpose(3, 1, 2, 0, 4).reshape(QUARTERS, w_rows, 3 * quarter_width)

    def join_qkv(parts):
        parts = parts.reshape(QUARTERS, w_rows, QUARTER_HEADS, 3, HD)
        return parts.transpose(3, 1, 2, 0, 4).reshape(3, w_rows, D)

    def split_units(gate, upward):
        def quarters(matrix):
            parts = matrix.reshape(w_rows, planes, QUARTERS, 2, d_rows).transpose(2, 0, 1, 3, 4)
            parts = jnp.pad(parts, ((0, 0),) * 4 + ((0, padded - d_rows),))
            return parts.reshape(QUARTERS, w_rows, -1, 1, BLOCK // 2)

        both = jnp.concatenate([quarters(gate), quarters(upward)], axis=3)
        return both.reshape(QUARTERS, w_rows, 2 * quarter_ff)

    def join_units(parts):
        parts = parts.reshape(QUARTERS, w_rows, -1, 2, BLOCK // 2)

        def joined(part):
            part = part.reshape(QUARTERS, w_rows, planes, 2, padded)[..., :d_rows]
            return part.transpose(1, 2, 0, 3, 4).reshape(w_rows, 4 * seq * d_rows)

        return joined(parts[:, :, :, 0]), joined(parts[:, :, :, 1])

    def whole_out_back(grad):
        spaced = lax.dynamic_update_slice_in_dim(
            jnp.zeros((QUARTER_HEADS, QUARTERS, HD, D), LOW),
            grad.astype(LOW).reshape(QUARTER_HEADS, 1, HD, D),
            my_quarter,
            1,
        )
        return lax.psum_scatter(spaced.reshape(D, D), BOTH, scatter_dimension=0, tiled=True)

    def normalize(values):
        inverse = lax.rsqrt(jnp.mean(values * values, axis=-1, keepdims=True) + NORM_EPS)
        return values * inverse, inverse

    def normalize_back(scaled, inverse, inner):
        return inverse * (inner - scaled * jnp.mean(inner * scaled, axis=-1, keepdims=True))

    def scaled_qkv(layer):
        scale = gain_attn[layer][:, None]
        return split_qkv(
            *((member[layer] * scale).astype(LOW) for member in (w_query, w_key, w_value))
        )

    def attention_part(layer, qkv_rows):
        blocks = blocks_of(w_out[layer].astype(LOW))
        return jnp.concatenate([qkv_rows, blocks], axis=1)

    def attention_matrices(part):
        whole = gather(part)
        blocks = whole[:, 3 * quarter_width :].reshape(2 * planes, -1, BLOCK)
        return whole[:, : 3 * quarter_width], from_blocks(blocks, w_rows)

    first_part = attention_part(0, cross_rows_at_once(scaled_qkv(0)))
    first_part, tokens, cotangent, time_ids, w_query, w_key, w_value, w_gate, w_up = (
        lax.optimization_barrier(
            (first_part, tokens, cotangent, time_ids, w_query, w_key, w_value, w_gate, w_up)
        )
    )
    attention_weights, out_weights = [attention_matrices(first_part)], []
    start_scaled, start_inverse = normalize(tokens)
    start_normed = beside(start_scaled.astype(LOW))

    group_rows = 4 * w_rows
    unit_end = 2 * quarter_ff // BLOCK * group_rows
    ffn_end = unit_end + D // BLOCK * padded

    def units_parts(layer):
        scale = gain_ffn[layer][:, None]
        return split_units((w_gate[layer] * scale).astype(LOW), (w_up[layer] * scale).astype(LOW))

    def ffn_part(layer, units_rows):
        down_part = jnp.pad(w_down[layer].astype(LOW), ((0, padded - d_rows), (0, 0)))
        return jnp.concatenate([blocks_of(units_rows), blocks_of(down_part)], axis=0)

    later_weights = [units_parts(layer) for layer in range(LAYERS)]
    later_weights += [scaled_qkv(layer) for layer in range(1, LAYERS)]
    later_widths = [member.shape[-1] for member in later_weights]
    later_weights = jnp.concatenate(later_weights, axis=-1)

    def cut(whole):
        parts, start = [], 0
        for width in later_widths:
            parts.append(whole[..., start : start + width])
            start += width
        return parts

    ffn_weights = []

    def placed_ids(ids):
        ids = ids.reshape(planes, 2, 2, 2, tok_rows)
        ids = jnp.where(here_lo == 0, ids, ids[:, ::-1])
        ids = jnp.where(here_y == 0, ids, ids[:, :, ::-1])
        ids = jnp.where(here_core == 0, ids, ids[:, :, :, ::-1])
        return ids.transpose(3, 0, 1, 2, 4).reshape(2 * planes, cols)

    def my_tiles(value):
        if spread == 1:
            return value
        return lax.dynamic_slice_in_dim(value, first_tile, tiles, 0)

    positions = jnp.arange(all_rows, dtype=jnp.int32)
    doc_ids = jnp.sum((doc_starts[None, :] <= positions[:, None]).astype(jnp.int32), axis=1)
    docs = placed_ids(doc_ids)
    variates = placed_ids(variate_ids)
    q_docs, q_variates = my_tiles(docs[:planes]), my_tiles(variates[:planes])
    extra_row = jnp.arange(HD, dtype=jnp.int32)[None, :, None]

    def one_hot(ids):
        return ids[:, None, :] == extra_row % VARIATES

    def is_doc(ids):
        return ids[:, None, :] == extra_row - 24

    doc_row = (extra_row >= 24) & (extra_row < 32)
    ones_row = (extra_row == 16) | (extra_row == 17) | ((extra_row >= 32) & (extra_row < 35))
    k_hits = one_hot(variates) & (extra_row < 16) | is_doc(docs) & doc_row | ones_row
    k_aug = jnp.where(k_hits, 1.0, 0.0).astype(LOW)

    def query_extra(layer):
        same, other = variate_bias[layer, 0, my_head], variate_bias[layer, 1, my_head]
        gap = same - other
        gap_lead, other_lead = (part.astype(LOW).astype(jnp.float32) for part in (gap, other))
        gap_part = jnp.where(extra_row < VARIATES, gap_lead, gap - gap_lead)
        other_part = jnp.where(extra_row == 16, other_lead, other - other_lead)
        spread_gap = jnp.where(one_hot(q_variates), gap_part, 0.0)
        shut = jnp.where(doc_row & ~is_doc(q_docs), FLOOR_SCORE, 0.0)
        tail = jnp.where(extra_row < 18, other_part, shut)
        return jnp.where(extra_row < 16, spread_gap, tail).astype(LOW)

    q_augs = [query_extra(layer) for layer in range(LAYERS)]
    q_onehots = (q_variates[:, None, :] == jnp.arange(VARIATES, dtype=jnp.int32)[:, None]).astype(
        jnp.float32
    )

    half_dim = HD // 2
    frequency = jnp.exp(jnp.arange(half_dim).astype(jnp.float32) * (-2.0 * math.log(10000.0) / HD))
    times = beside(time_ids.astype(jnp.float32))
    angles = frequency[:, None] * times[None, :]
    cosines, sines = jnp.cos(angles), jnp.sin(angles)
    start_normed, later_weights, k_aug, cosines, sines, *q_augs = lax.optimization_barrier(
        (start_normed, later_weights, k_aug, cosines, sines, *q_augs)
    )

    def rotate(values, sines):
        former, latter = values[:, :half_dim], values[:, half_dim:]
        return jnp.concatenate(
            [former * cosines - latter * sines, latter * cosines + former * sines], axis=1
        )

    def to_heads(value):
        if spread > 1:
            value = jnp.repeat(value, spread, axis=0)
        return lax.all_to_all(
            value, "seq", split_axis=0, concat_axis=0, tiled=True, axis_index_groups=plane_groups
        )

    def all_blocks(value):
        if spread == 1:
            return value
        zeros = jnp.zeros((planes,) + value.shape[1:], value.dtype)
        return lax.dynamic_update_slice_in_dim(zeros, value, first_tile, 0)

    def over_spread(value):
        if spread == 1:
            return value
        value = value.reshape((QUARTER_HEADS, spread) + value.shape[1:])
        return jnp.sum(value.astype(jnp.float32), axis=1).astype(LOW)

    def from_heads(value):
        return over_spread(
            lax.all_to_all(
                value, "seq", split_axis=0, concat_axis=0, tiled=True, axis_index_groups=plane_groups
            )
        )

    chip_groups = [
        [place_of(plane, lo, y, core) for plane in range(planes) for lo in range(2) for y in range(2)]
        for core in range(2)
    ]

    def over_chips(value):
        shape = value.shape
        value = value.reshape(-1, *shape[2:])
        value = lax.all_to_all(
            value, BOTH, split_axis=0, concat_axis=0, tiled=True, axis_index_groups=chip_groups
        )
        return value.reshape(shape)

    chip_flips = jnp.reshape(my_quarter, (1,)).astype(jnp.int32)

    def plane_order(value):
        grid = [[value[:, 2 * lo + y] for y in range(2)] for lo in range(2)]
        grid = xor_order(grid, here_lo, here_y)
        return jnp.stack([*grid[0], *grid[1]])

    def chip_order(value):
        grid = xor_order([[value[0], value[1]], [value[2], value[3]]], here_lo, here_y)
        return jnp.stack([*grid[0], *grid[1]], axis=1)

    def share_for_out(middle_low, attended):
        pieces = attended.reshape(4, quarter_width, tok_rows)
        cuts = quarter_width // tok_rows

        def joined(piece):
            parts = [piece[cut * tok_rows : (cut + 1) * tok_rows] for cut in range(cuts)]
            return jnp.concatenate([middle_low, *parts], axis=1)

        came = neighbours(*(joined(piece) for piece in pieces[1:]))
        tokens_low = jnp.concatenate([middle_low, *(part[:, :D] for part in came)], axis=0)

        def results(part):
            return jnp.concatenate(
                [part[:, D + cut * tok_rows : D + (cut + 1) * tok_rows] for cut in range(cuts)], axis=0
            )

        return tokens_low, jnp.concatenate([pieces[0], *(results(part) for part in came)], axis=1)

    stream = tokens
    saved = []
    for layer in range(LAYERS):
        qkv_matrix, out_quarter = attention_weights[layer]
        if layer == 0:
            scaled_one, inverse_one, normed = start_scaled, start_inverse, start_normed
        else:
            scaled_one, inverse_one = normalize(stream)
            normed = beside(scaled_one.astype(LOW))
        projected = dot(qkv_matrix, normed, TT).reshape(QUARTER_HEADS, 3 * HD, cols)
        query = rotate(projected[:, :HD], sines) * (1.0 / math.sqrt(HD))
        key = rotate(projected[:, HD : 2 * HD], sines)
        sent = jnp.concatenate([query, key, projected[:, 2 * HD :]], axis=1).astype(LOW)
        sent, later_weights, cotangent = lax.optimization_barrier((sent, later_weights, cotangent))
        if layer == 0:
            later_weights, cotangent = lax.optimization_barrier(
                (cross_rows(later_weights), cotangent)
            )
            last_grad_parts = beside_parts(cotangent.astype(LOW))
        own = to_heads(sent)
        if layer == 0:
            own, last_grad_parts = lax.optimization_barrier((own, last_grad_parts))
        next_part = ffn_part(layer, cut(later_weights)[layer])
        own, next_part = lax.optimization_barrier((own, next_part))
        packed = gather(next_part).reshape(2 * planes, -1, BLOCK)
        ffn_weights.append(packed)
        own, out_quarter = lax.optimization_barrier((own, out_quarter))
        halves = out_quarter.reshape(2, quarter_width // 2, D)
        half = jnp.where(here_core == 0, halves[0], halves[1])
        out_parts = neighbours(half, half, half)
        sib = lax.ppermute(own[:, HD:], "head", CORE_SWAP)
        queries = my_tiles(own)
        q_aug = q_augs[layer]
        out, lse = attention_forward(chip_flips, queries, q_aug, own, sib, k_aug)
        out, *out_parts = lax.optimization_barrier((out, *out_parts))
        mine = jnp.stack(out_parts)
        other = lax.ppermute(mine, "head", CORE_SWAP)
        pairs = jnp.where(
            here_core == 0, jnp.stack([mine, other], axis=1), jnp.stack([other, mine], axis=1)
        )
        out_matrix = jnp.concatenate([out_quarter, pairs.reshape(3 * quarter_width, D)], axis=0)
        out_weights.append(out_matrix)
        attended = over_spread(over_chips(all_blocks(out))).reshape(QUARTER_HEADS, 4, HD, tok_rows)
        attended = plane_order(attended).reshape(D, tok_rows)
        attended, out_matrix = lax.optimization_barrier((attended, out_matrix))
        middle = stream + dot(attended, out_matrix, TN)
        scaled_two, inverse_two = normalize(middle)
        normed_parts = beside_parts(scaled_two.astype(LOW))
        if layer < LAYERS - 1:
            next_part = attention_part(layer + 1, cut(later_weights)[LAYERS + layer])
            normed_parts, next_part = lax.optimization_barrier((normed_parts, next_part))
            attention_weights.append(attention_matrices(next_part))
        both, hidden, *parts = ffn_forward(normed_parts, packed, quarter_ff, group_rows, padded)
        saved.append(
            (
                scaled_one, inverse_one, normed, own, sib, queries, q_aug, out, lse, attended,
                scaled_two, inverse_two, normed_parts, both, hidden,
            )
        )
        if layer < LAYERS - 1:
            stream = middle + fold(*parts)
        else:
            last_middle, last_parts = middle, parts

    upstream = cotangent
    whole_grads, ffn_sums, qkv_sums = [None] * LAYERS, [None] * LAYERS, [None] * LAYERS
    bias_parts = [None] * LAYERS
    for layer in reversed(range(LAYERS)):
        qkv_matrix, unused = attention_weights[layer]
        out_matrix, packed = out_weights[layer], ffn_weights[layer]
        (
            scaled_one, inverse_one, normed, own, sib, queries, q_aug, out, lse, attended,
            scaled_two, inverse_two, normed_parts, both, hidden,
        ) = saved[layer]
        if layer < LAYERS - 1:
            upstream_parts = beside_parts(upstream.astype(LOW))
        else:
            upstream_parts = last_grad_parts
        grad_units, *parts = ffn_backward(upstream_parts, packed, both, quarter_ff, group_rows, padded)
        inner = fold(*parts)
        buffer = ffn_weight_grads(
            normed_parts, grad_units, hidden, upstream_parts, 2 * planes, group_rows, padded
        )
        inner, buffer = lax.optimization_barrier((inner, buffer))
        if layer < LAYERS - 1:
            buffer, qkv_sums[layer + 1] = lax.optimization_barrier((buffer, qkv_sums[layer + 1]))
        ffn_sums[layer] = scatter(buffer)
        grad_middle = upstream + normalize_back(scaled_two, inverse_two, inner)
        middle_low = grad_middle.astype(LOW)
        grad_attended = dot(out_matrix, middle_low, NT).astype(LOW)
        grad_attended = chip_order(grad_attended.reshape(4, QUARTER_HEADS, HD, tok_rows))
        if spread > 1:
            grad_attended = jnp.repeat(grad_attended, spread, axis=0)
        out_grad = my_tiles(over_chips(grad_attended))
        out_grad, middle_low, attended = lax.optimization_barrier((out_grad, middle_low, attended))
        middle_low, attended = share_for_out(middle_low, attended)
        grad_q, grad_kv = attention_backward(
            chip_flips, queries, q_aug, lse, out, out_grad, own, sib, k_aug
        )
        grad_kv, middle_low, attended = lax.optimization_barrier((grad_kv, middle_low, attended))
        if not split_heads:
            whole_grads[layer] = whole_out_back(dot(attended, middle_low, NN))
        else:
            out_blocks = out_weight_grad(attended, middle_low, w_rows)
        same_grad = jnp.sum(grad_q[:, HD : HD + VARIATES] * q_onehots)
        all_grad = jnp.sum(grad_q[:, HD + 16])
        crossed = lax.ppermute(grad_kv[planes:], "head", CORE_SWAP)
        grad_kv = (grad_kv[:planes].astype(jnp.float32) + crossed.astype(jnp.float32)).astype(LOW)
        grad_q = (grad_q[:, :HD] * (1.0 / math.sqrt(HD))).astype(LOW)
        if layer == LAYERS - 1:
            grad_kv, *last_parts = lax.optimization_barrier((grad_kv, *last_parts))
            stream = last_middle + fold(*last_parts)
        grad_heads = from_heads(jnp.concatenate([all_blocks(grad_q), grad_kv], axis=1))
        if layer == LAYERS - 1:
            grad_heads, stream = lax.optimization_barrier((grad_heads, stream))
        grad_heads = jnp.concatenate(
            [
                rotate(grad_heads[:, :HD].astype(jnp.float32), -sines).astype(LOW),
                rotate(grad_heads[:, HD : 2 * HD].astype(jnp.float32), -sines).astype(LOW),
                grad_heads[:, 2 * HD :],
            ],
            axis=1,
        ).reshape(3 * quarter_width, cols)
        bias_parts[layer] = jnp.stack([same_grad, all_grad - same_grad])
        partial = dot(grad_heads, qkv_matrix, TT)
        qkv_grad = dot(normed, grad_heads, TT).astype(LOW)
        qkv_grad, ffn_sums[layer] = lax.optimization_barrier((qkv_grad, ffn_sums[layer]))
        if split_heads:
            qkv_grad = jnp.concatenate([qkv_grad, out_blocks.reshape(-1, BLOCK)], axis=1)
        if layer > 0:
            inner = fold_whole(partial)
            inner, qkv_grad = lax.optimization_barrier((inner, qkv_grad))
        qkv_sums[layer] = scatter(qkv_grad)
        if layer > 0:
            upstream = grad_middle + normalize_back(scaled_one, inverse_one, inner)

    later_sums = [from_blocks(member[None, :unit_end], group_rows) for member in ffn_sums]
    out_sums = [member[:, 3 * quarter_width :] for member in qkv_sums]
    qkv_sums = [member[:, : 3 * quarter_width] for member in qkv_sums]
    if not split_heads:
        out_sums = [member[:, :BLOCK] for member in qkv_sums]
    later_sums = jnp.concatenate([*later_sums, *qkv_sums[1:]], axis=1)
    came, *bias_parts = lax.optimization_barrier((cross_back(later_sums), *bias_parts))
    bias_local = lax.dynamic_update_slice(
        jnp.zeros((LAYERS, 2, HEADS), jnp.float32), jnp.stack(bias_parts)[:, :, None], (0, 0, my_head)
    )
    bias_total = bias_local
    for axis, size in (("head", 4), ("seq", seq)):
        hop = 1
        while hop < size:
            swap = [(place, place ^ hop) for place in range(size)]
            bias_total = bias_total + lax.ppermute(bias_total, axis, swap)
            hop *= 2
    quarters = jnp.arange(QUARTERS, dtype=jnp.int32)
    weights = (w_query, w_key, w_value, w_gate, w_up)
    gains = (gain_attn[:, :, None], gain_ffn[:, :, None])
    *grads, gain_one, gain_two = finish_gradients(
        quarters ^ (2 * here_y + here_core), came, ffn_sums,
        out_sums[1:], weights, gains, w_down.shape, unit_end, planes, split_heads,
    )
    qkv_sums[0], out_sums[0], partial = lax.optimization_barrier((qkv_sums[0], out_sums[0], partial))
    inner = fold_whole(partial)
    upstream = grad_middle + normalize_back(scaled_one, inverse_one, inner)
    *grads[:3], gain_one, grads[3] = finish_first(
        2 * quarters + here_lo, cross_back_at_once(qkv_sums[0]), out_sums[0], weights[:3], gains[0],
        [*grads[:3], gain_one, grads[3]], split_heads,
    )
    if not split_heads:
        grads[3] = jnp.stack(whole_grads).astype(jnp.float32)
    return (stream, upstream, *grads, gain_one[:, :, 0], gain_two[:, :, 0], bias_total)


def solution(mesh):
    rows = P(BOTH, None)
    middle = P(None, BOTH, None)
    gains = P(None, BOTH)
    return jax.shard_map(
        on_device,
        mesh=mesh,
        in_specs=(rows,) + (middle,) * 7 + (gains,) * 2 + (P(),) * 3 + (P(BOTH), rows),
        out_specs=(rows, rows) + (middle,) * 7 + (gains,) * 2 + (P(),),
        check_vma=False,
    )
```

```python
import functools
import math

import jax
import jax.numpy as jnp
from jax import lax
from jax.experimental import pallas as pl
from jax.experimental.pallas import tpu as pltpu
from jax.sharding import PartitionSpec as P

D = 1024
HEADS = 16
HD = 64
LAYERS = 2
VARIATES = 8
BLOCK = 256

NORM_EPS = 1e-05
FLOOR_SCORE = -1e30
LOW = jnp.bfloat16
BOTH = ("seq", "head")

QUARTERS = 4
QUARTER_HEADS = HEADS // QUARTERS
Y_SWAP = [(place, place ^ 2) for place in range(4)]
CORE_SWAP = [(place, place ^ 1) for place in range(4)]

NN = (((1,), (0,)), ((), ()))
NT = (((1,), (1,)), ((), ()))
TN = (((0,), (0,)), ((), ()))
TT = (((0,), (1,)), ((), ()))
VMEM_LIMIT = 56 * 1024 * 1024


def in_vmem(count):
    return [pl.BlockSpec(memory_space=pltpu.VMEM)] * count


def cost(flops, operands, results, transcendentals=0):
    moved = sum(member.size * member.dtype.itemsize for member in [*operands, *results])
    return pl.CostEstimate(flops=flops, bytes_accessed=moved, transcendentals=transcendentals)


def dot(left, right, dims):
    return lax.dot_general(left, right, dims, preferred_element_type=jnp.float32)


def forward_kernel(flip_ref, q_ref, q_aug_ref, own_ref, sib_ref, k_aug_ref, out_ref, lse_ref):
    blocks = own_ref.shape[0]
    sources = ((own_ref, HD), (sib_ref, 0))
    spots = [(half, block) for half in range(2) for block in range(blocks)]
    cols = q_ref.shape[-1]
    q_side = jnp.concatenate([q_ref[0, :HD, :], q_aug_ref[0]], axis=0).T
    top = jnp.full((cols, 1), FLOOR_SCORE, jnp.float32)
    total = jnp.zeros((cols, 1), jnp.float32)
    acc = jnp.zeros((cols, HD), jnp.float32)

    def scores(half, block):
        ref, low_row = sources[half]
        extra = k_aug_ref[half * blocks + block]
        k_side = jnp.concatenate([ref[block, low_row : low_row + HD, :], extra], axis=0)
        return dot(q_side, k_side, NN)

    following = scores(*spots[0])
    for number, (half, block) in enumerate(spots):
        part = following
        if number + 1 < len(spots):
            following = scores(*spots[number + 1])
        fresh = jnp.maximum(top, jnp.max(part, axis=-1, keepdims=True))
        shrink = jnp.exp(top - fresh)
        prob = jnp.exp(part - fresh)
        total = total * shrink + jnp.sum(prob, axis=-1, keepdims=True)
        ref, low_row = sources[half]
        values = ref[block, low_row + HD : low_row + 2 * HD, :]
        acc = acc * shrink + dot(prob.astype(LOW), values, NT)
        top = fresh
    result = acc / total
    lse = jnp.broadcast_to(top + jnp.log(total), (cols, HD))
    both = jnp.concatenate([result, lse], axis=1).T
    piece = out_ref.shape[-1]
    for place in range(cols // piece):
        part = both[:HD, place * piece : (place + 1) * piece]
        out_ref[0, place ^ flip_ref[0]] = part.astype(LOW)
    lse_ref[0] = both[HD : HD + 8]


def split_rows(row, rows):
    one = row.astype(LOW).astype(jnp.float32)
    two = (row - one).astype(LOW).astype(jnp.float32)
    three = row - one - two
    pad = jnp.zeros((rows - 3, row.shape[-1]), jnp.float32)
    return jnp.concatenate([one, two, three, pad], axis=0).astype(LOW)


def backward_kernel(
    flip_ref, q_ref, q_aug_ref, lse_ref, out_ref, grad_ref, own_ref, sib_ref, k_aug_ref,
    dq_ref, dkv_ref, dkv_acc,
):
    step = pl.program_id(0)
    blocks = own_ref.shape[0]
    sources = ((own_ref, HD), (sib_ref, 0))
    cols, key_cols = q_ref.shape[-1], own_ref.shape[-1]

    @pl.when(step == 0)
    def _():
        dkv_acc[...] = jnp.zeros_like(dkv_acc)

    q_low = q_ref[0, :HD, :]
    places = range(grad_ref.shape[1])
    g_low = jnp.concatenate([grad_ref[0, place ^ flip_ref[0]] for place in places], axis=1)
    out = jnp.concatenate([out_ref[0, place ^ flip_ref[0]] for place in places], axis=1)
    row_dot = jnp.sum(g_low.astype(jnp.float32) * out.astype(jnp.float32), axis=0, keepdims=True)
    aug = jnp.concatenate(
        [q_aug_ref[0, :32, :], split_rows(-lse_ref[0, :1, :], 16), q_aug_ref[0, 48:, :]], axis=0
    )
    q_side = jnp.concatenate([q_low, aug], axis=0).T
    g_side = jnp.concatenate([g_low, split_rows(-row_dot, HD)], axis=0).T
    ones = jnp.concatenate(
        [jnp.ones((16, key_cols), LOW), jnp.zeros((HD - 16, key_cols), LOW)], axis=0
    )
    dq = jnp.zeros((cols, 2 * HD), jnp.float32)
    spots = [(half, block) for half in range(2) for block in range(blocks)]

    def products(half, block):
        ref, low_row = sources[half]
        k_side = jnp.concatenate(
            [ref[block, low_row : low_row + HD, :], k_aug_ref[half * blocks + block]], axis=0
        )
        v_side = jnp.concatenate([ref[block, low_row + HD : low_row + 2 * HD, :], ones], axis=0)
        return k_side, dot(q_side, k_side, NN), dot(g_side, v_side, NN)

    following = products(*spots[0])
    for spot in range(len(spots)):
        k_side, score, prob_grad = following
        if spot + 1 < len(spots):
            following = products(*spots[spot + 1])
        prob = jnp.exp(score)
        score_grad = (prob * prob_grad).astype(LOW)
        dq = dq + dot(score_grad, k_side, NT)
        dkv_acc[spot, :HD, :] += dot(q_low, score_grad, NN)
        dkv_acc[spot, HD:, :] += dot(g_low, prob.astype(LOW), NN)
    dq_ref[0] = dq.T

    @pl.when(step == pl.num_programs(0) - 1)
    def _():
        dkv_ref[...] = dkv_acc[...].astype(LOW)


def whole_spec(shape):
    rank = len(shape)
    return pl.BlockSpec(shape, lambda i, flip: (0,) * rank)


def tile_spec(rows, cols):
    return pl.BlockSpec((1, rows, cols), lambda i, flip: (i, 0, 0))


def owner_spec(shape):
    return pl.BlockSpec((1, *shape[1:]), lambda i, flip: (i, 0, 0, 0))


def attention_forward(flip, queries, q_aug, own, sib, k_aug):
    tiles, unused, cols = queries.shape
    pairs = 2 * tiles * own.shape[0] * cols * cols
    out_shape = (tiles, 4, HD, cols // 4)
    results = [
        jax.ShapeDtypeStruct(out_shape, LOW),
        jax.ShapeDtypeStruct((tiles, 8, cols), jnp.float32),
    ]
    return pl.pallas_call(
        forward_kernel,
        grid_spec=pltpu.PrefetchScalarGridSpec(
            num_scalar_prefetch=1,
            grid=(tiles,),
            in_specs=[tile_spec(3 * HD, cols), tile_spec(HD, cols)]
            + [whole_spec(member.shape) for member in (own, sib, k_aug)],
            out_specs=[owner_spec(out_shape), tile_spec(8, cols)],
        ),
        out_shape=results,
        cost_estimate=cost(16 * HD * pairs, [queries, own, sib], results, pairs),
        compiler_params=pltpu.CompilerParams(vmem_limit_bytes=VMEM_LIMIT),
        name="attention_forward",
    )(flip, queries, q_aug, own, sib, k_aug)


def attention_backward(flip, queries, q_aug, lse, out, grad, own, sib, k_aug):
    tiles, unused, cols = queries.shape
    dkv_shape = (2 * own.shape[0], 2 * HD, cols)
    pairs = 2 * tiles * own.shape[0] * cols * cols
    results = [
        jax.ShapeDtypeStruct((tiles, 2 * HD, cols), jnp.float32),
        jax.ShapeDtypeStruct(dkv_shape, LOW),
    ]
    return pl.pallas_call(
        backward_kernel,
        grid_spec=pltpu.PrefetchScalarGridSpec(
            num_scalar_prefetch=1,
            grid=(tiles,),
            in_specs=[tile_spec(3 * HD, cols), tile_spec(HD, cols), tile_spec(8, cols)]
            + [owner_spec(out.shape)] * 2
            + [whole_spec(member.shape) for member in (own, sib, k_aug)],
            out_specs=[tile_spec(2 * HD, cols), whole_spec(dkv_shape)],
            scratch_shapes=[pltpu.VMEM(dkv_shape, jnp.float32)],
        ),
        out_shape=results,
        cost_estimate=cost(32 * HD * pairs, [queries, own, sib], results, pairs),
        compiler_params=pltpu.CompilerParams(vmem_limit_bytes=VMEM_LIMIT),
        name="attention_backward",
    )(flip, queries, q_aug, lse, out, grad, own, sib, k_aug)


def silu_parts(gate):
    sigmoid = 1.0 / (1.0 + jnp.exp(-gate))
    return sigmoid, gate * sigmoid


def put_parts(values, lanes, own_ref, *low_refs):
    rows = own_ref.shape[0]
    own_ref[:, lanes] = values[:rows]
    for place, low_ref in enumerate(low_refs):
        low_ref[:, lanes] = values[(place + 1) * rows : (place + 2) * rows].astype(LOW)


def parts_of(tokens, lanes, index):
    shape = (tokens // 4, D)
    types = [jnp.float32, LOW, LOW, LOW]
    return (
        [jax.ShapeDtypeStruct(shape, kind) for kind in types],
        [pl.BlockSpec((tokens // 4, lanes), index) for unused in types],
    )


def join_rows(x_ref, refs):
    @pl.when(pl.program_id(0) == 0)
    def _():
        rows = refs[0].shape[0]
        for place, ref in enumerate(refs):
            x_ref[place * rows : (place + 1) * rows, :] = ref[...]


def ffn_forward_kernel(*refs, unit_rows, down_rows, unit_steps):
    unit_ref, down_ref, both_ref, hidden_ref = refs[4:8]
    out_refs, x_ref = refs[8:12], refs[12]
    join_rows(x_ref, refs[:4])
    step = pl.program_id(0)
    half = BLOCK // 2

    @pl.when(step < unit_steps)
    def _():
        count = unit_ref.shape[1] // unit_rows
        for place in range(count):
            matrix = unit_ref[:, place * unit_rows : (place + 1) * unit_rows, :].reshape(-1, BLOCK)
            both = dot(x_ref[...], matrix, NN)
            both_ref[place] = both.astype(both_ref.dtype)
            hidden = silu_parts(both[:, :half])[1] * both[:, half:]
            spot = step * count + place
            hidden_ref[:, pl.ds(pl.multiple_of(spot * half, half), half)] = hidden.astype(LOW)

    @pl.when(step >= unit_steps)
    def _():
        for place in range(down_ref.shape[1] // down_rows):
            matrix = down_ref[:, place * down_rows : (place + 1) * down_rows, :].reshape(-1, BLOCK)
            lanes = slice(place * BLOCK, (place + 1) * BLOCK)
            put_parts(dot(hidden_ref[...], matrix, NN), lanes, *out_refs)


def ffn_backward_kernel(*refs, unit_rows, down_rows, down_steps):
    unit_ref, down_ref, both_ref, grads_ref = refs[4:8]
    part_refs, inner_ref, hidden_grad, g_ref = refs[8:12], refs[12], refs[13], refs[14]
    join_rows(g_ref, refs[:4])
    step = pl.program_id(0)
    half = BLOCK // 2

    @pl.when(step < down_steps)
    def _():
        total = 0.0
        for place in range(down_ref.shape[1] // down_rows):
            matrix = down_ref[:, place * down_rows : (place + 1) * down_rows, :].reshape(-1, BLOCK)
            lanes = pl.ds(pl.multiple_of((step * FFN_DOWNS + place) * BLOCK, BLOCK), BLOCK)
            total = total + dot(g_ref[:, lanes], matrix, NT)

        @pl.when(step == 0)
        def _():
            hidden_grad[...] = total

        @pl.when(step > 0)
        def _():
            hidden_grad[...] += total

    @pl.when(step >= down_steps)
    def _():
        count = unit_ref.shape[1] // unit_rows
        total = 0.0
        for place in range(count):
            matrix = unit_ref[:, place * unit_rows : (place + 1) * unit_rows, :].reshape(-1, BLOCK)
            spot = (step - down_steps) * count + place
            gate = both_ref[place, :, :half].astype(jnp.float32)
            upward = both_ref[place, :, half:].astype(jnp.float32)
            above = hidden_grad[:, pl.ds(pl.multiple_of(spot * half, half), half)]
            sigmoid, silu = silu_parts(gate)
            grad_gate = above * upward * (sigmoid * (1.0 + gate * (1.0 - sigmoid)))
            grads = jnp.concatenate([grad_gate, above * silu], axis=1).astype(LOW)
            grads_ref[place] = grads
            total = total + dot(grads, matrix, NT)

        @pl.when(step == down_steps)
        def _():
            inner_ref[...] = total

        @pl.when(step > down_steps)
        def _():
            inner_ref[...] += total

    @pl.when(step == pl.num_programs(0) - 1)
    def _():
        put_parts(inner_ref[...], slice(0, D), *part_refs)


FFN_DOWNS = 4


def ffn_units(cols_ff):
    return max(count for count in (1, 2, 3) if 2 * cols_ff // BLOCK % count == 0)


def ffn_specs(cols_ff, unit_rows, down_rows, groups, unit_step, down_step):
    unit_blocks, down_blocks = 2 * cols_ff // BLOCK, D // BLOCK
    units, downs = ffn_units(cols_ff) * unit_rows, FFN_DOWNS * down_rows
    first_down = unit_blocks * unit_rows // downs
    return (
        unit_blocks // ffn_units(cols_ff),
        down_blocks // FFN_DOWNS,
        [
            pl.BlockSpec((groups, units, BLOCK), lambda i: (0, unit_step(i), 0)),
            pl.BlockSpec((groups, downs, BLOCK), lambda i: (0, first_down + down_step(i), 0)),
        ],
    )


def ffn_forward(rows, packed, cols_ff, unit_rows, down_rows):
    tokens, unit_steps = 4 * rows[0].shape[0], 2 * cols_ff // BLOCK // ffn_units(cols_ff)
    unit_step = lambda i: jnp.minimum(i, unit_steps - 1)
    down_step = lambda i: jnp.maximum(i - unit_steps, 0)
    unit_steps, down_steps, specs = ffn_specs(
        cols_ff, unit_rows, down_rows, packed.shape[0], unit_step, down_step
    )
    parts, part_specs = parts_of(tokens, FFN_DOWNS * BLOCK, lambda i: (0, down_step(i)))
    results = [
        jax.ShapeDtypeStruct((2 * cols_ff // BLOCK, tokens, BLOCK), LOW),
        jax.ShapeDtypeStruct((tokens, cols_ff), LOW),
        *parts,
    ]
    return pl.pallas_call(
        functools.partial(
            ffn_forward_kernel, unit_rows=unit_rows, down_rows=down_rows, unit_steps=unit_steps
        ),
        grid=(unit_steps + down_steps,),
        in_specs=[pl.BlockSpec(rows[0].shape, lambda i: (0, 0))] * 4 + specs,
        out_specs=[
            pl.BlockSpec((ffn_units(cols_ff), tokens, BLOCK), lambda i: (unit_step(i), 0, 0)),
            pl.BlockSpec((tokens, cols_ff), lambda i: (0, 0)),
            *part_specs,
        ],
        out_shape=results,
        scratch_shapes=[pltpu.VMEM((tokens, D), LOW)],
        cost_estimate=cost(6 * tokens * D * cols_ff, [*rows, packed], results),
        compiler_params=pltpu.CompilerParams(vmem_limit_bytes=VMEM_LIMIT),
        name="ffn_forward",
    )(*rows, packed, packed)


def ffn_backward(rows, packed, both, cols_ff, unit_rows, down_rows):
    tokens, down_steps = 4 * rows[0].shape[0], D // BLOCK // FFN_DOWNS
    unit_step = lambda i: jnp.maximum(i - down_steps, 0)
    down_step = lambda i: jnp.minimum(i, down_steps - 1)
    unit_steps, down_steps, specs = ffn_specs(
        cols_ff, unit_rows, down_rows, packed.shape[0], unit_step, down_step
    )
    unit_spec = pl.BlockSpec((ffn_units(cols_ff), tokens, BLOCK), lambda i: (unit_step(i), 0, 0))
    parts, part_specs = parts_of(tokens, D, lambda i: (0, 0))
    results = [jax.ShapeDtypeStruct((2 * cols_ff // BLOCK, tokens, BLOCK), LOW), *parts]
    return pl.pallas_call(
        functools.partial(
            ffn_backward_kernel, unit_rows=unit_rows, down_rows=down_rows, down_steps=down_steps
        ),
        grid=(unit_steps + down_steps,),
        in_specs=[pl.BlockSpec(rows[0].shape, lambda i: (0, 0))] * 4 + [*specs, unit_spec],
        out_specs=[unit_spec, *part_specs],
        out_shape=results,
        scratch_shapes=[
            pltpu.VMEM((tokens, D), jnp.float32),
            pltpu.VMEM((tokens, cols_ff), jnp.float32),
            pltpu.VMEM((tokens, D), LOW),
        ],
        cost_estimate=cost(6 * tokens * D * cols_ff, [*rows, packed, both], results),
        compiler_params=pltpu.CompilerParams(vmem_limit_bytes=VMEM_LIMIT),
        name="ffn_backward",
    )(*rows, packed, packed, both)


def ffn_weight_grads_kernel(*refs, unit_rows, down_rows):
    unit_grads_ref, hidden_ref, g_refs, out_ref, x_ref = refs[4], refs[5], refs[6:10], refs[10], refs[11]
    step, last = pl.program_id(0), pl.num_programs(0) - 1

    @pl.when(step == 0)
    def _():
        rows = refs[0].shape[0]
        for place, ref in enumerate(refs[:4]):
            x_ref[:, place * rows : (place + 1) * rows] = ref[...].T

    @pl.when(step < last)
    def _():
        for place in range(out_ref.shape[1] // unit_rows):
            grad = dot(x_ref[...], unit_grads_ref[place], NN)
            grad = grad.reshape(-1, unit_rows, BLOCK).astype(LOW)
            out_ref[:, place * unit_rows : (place + 1) * unit_rows, :] = grad

    @pl.when(step == last)
    def _():
        hidden = hidden_ref[...].T
        for place in range(out_ref.shape[1] // down_rows):
            lanes = slice(place * BLOCK, (place + 1) * BLOCK)
            right = jnp.concatenate([ref[:, lanes] for ref in g_refs], axis=0)
            grad = dot(hidden, right, NN).reshape(-1, down_rows, BLOCK).astype(LOW)
            out_ref[:, place * down_rows : (place + 1) * down_rows, :] = grad


def ffn_weight_grads(rows, unit_grads, hidden, grad_rows, groups, unit_rows, down_rows):
    tokens, cols_ff = hidden.shape
    step_rows = D // BLOCK * down_rows
    per_step = step_rows // unit_rows
    steps = unit_grads.shape[0] // per_step
    last = steps - 1
    result = jax.ShapeDtypeStruct((groups, (steps + 1) * step_rows, BLOCK), LOW)
    part_spec = pl.BlockSpec(rows[0].shape, lambda i: (0, 0))
    return pl.pallas_call(
        functools.partial(ffn_weight_grads_kernel, unit_rows=unit_rows, down_rows=down_rows),
        grid=(steps + 1,),
        in_specs=[part_spec] * 4
        + [
            pl.BlockSpec((per_step, tokens, BLOCK), lambda i: (jnp.minimum(i, last), 0, 0)),
            pl.BlockSpec(hidden.shape, lambda i: (0, 0)),
        ]
        + [part_spec] * 4,
        out_specs=pl.BlockSpec((groups, step_rows, BLOCK), lambda i: (0, i, 0)),
        out_shape=result,
        scratch_shapes=[pltpu.VMEM((D, tokens), LOW)],
        cost_estimate=cost(6 * tokens * D * cols_ff, [*rows, unit_grads, hidden, *grad_rows], [result]),
        compiler_params=pltpu.CompilerParams(vmem_limit_bytes=VMEM_LIMIT),
        name="ffn_weight_grads",
    )(*rows, unit_grads, hidden, *grad_rows)


def out_grad_kernel(left_ref, right_ref, out_ref, *, rows):
    for place in range(D // BLOCK):
        grad = dot(left_ref[...], right_ref[:, place * BLOCK : (place + 1) * BLOCK], NN)
        out_ref[:, place * rows : (place + 1) * rows, :] = grad.reshape(-1, rows, BLOCK).astype(LOW)


def out_weight_grad(left, right, rows):
    result = jax.ShapeDtypeStruct((left.shape[0] // rows, D // BLOCK * rows, BLOCK), LOW)
    return pl.pallas_call(
        functools.partial(out_grad_kernel, rows=rows),
        in_specs=in_vmem(2),
        out_specs=in_vmem(1)[0],
        out_shape=result,
        cost_estimate=cost(2 * left.size * D, [left, right], [result]),
        compiler_params=pltpu.CompilerParams(vmem_limit_bytes=VMEM_LIMIT),
        name="out_weight_grad",
    )(left, right)


def take_qkv(room_ref, layer, quarter, weights, gain_ref):
    for slot in range(QUARTER_HEADS):
        column = HD * (QUARTERS * slot + quarter)
        for which, weight_ref in enumerate(weights):
            first = (3 * slot + which) * HD
            part = weight_ref[layer, :, column : column + HD] * gain_ref[layer]
            room_ref[:, first : first + HD] = part


def first_parts_kernel(lo_ref, *refs):
    weights, gain_ref, out_ref, room_ref = refs[:3], refs[3], refs[4], refs[5]
    for quarter in range(QUARTERS):
        take_qkv(room_ref, 0, quarter, weights, gain_ref)
        out_ref[2 * quarter + lo_ref[0]] = room_ref[...].astype(LOW)
        out_ref[2 * quarter + 1 - lo_ref[0]] = jnp.zeros(room_ref.shape, LOW)


def first_parts(lo, weights, gain):
    w_rows, width = weights[0].shape[1], 3 * QUARTER_HEADS * HD
    return pl.pallas_call(
        first_parts_kernel,
        in_specs=[pl.BlockSpec(memory_space=pltpu.SMEM)] + in_vmem(4),
        out_specs=in_vmem(1)[0],
        out_shape=jax.ShapeDtypeStruct((2 * QUARTERS, w_rows, width), LOW),
        scratch_shapes=[pltpu.VMEM((w_rows, width), jnp.float32)],
        compiler_params=pltpu.CompilerParams(vmem_limit_bytes=VMEM_LIMIT),
        name="first_parts",
    )(lo, *weights, gain)


def unit_places(d_rows, padded, planes):
    width = 2 * planes // 2 * padded
    column = lax.broadcasted_iota(jnp.int32, (1, QUARTERS * width), 1)
    quarter, rest = column // width, column % width
    group, unit = rest // padded, rest % padded
    source = d_rows * (8 * (group // 2) + 2 * quarter + group % 2) + unit
    source = jnp.where(unit < d_rows, source, -1)
    rows = lax.broadcasted_iota(jnp.int32, (4 * planes * d_rows, 1), 0)
    return jnp.where(rows == source, 1.0, 0.0).astype(LOW)


def later_parts_kernel(place_ref, *refs, d_rows, padded, planes):
    weights, gains = refs[:5], refs[5:7]
    outs, rows_ref, qkv_ref, all_ref = refs[7:11], refs[11], refs[12], refs[13]
    half, cols_ff = BLOCK // 2, 2 * planes * padded
    w_rows, width = weights[0].shape[1], cols_ff // 2
    taken = 4 * planes * d_rows
    pieces = [(layer, which, part) for layer in range(LAYERS) for which in range(2) for part in range(2)]
    for number, (layer, which, part) in enumerate(pieces):
        rows = weights[3 + which][layer, :, part * taken : (part + 1) * taken] * gains[1][layer]
        rows_ref[number * w_rows : (number + 1) * w_rows, :] = rows
    placed = dot(rows_ref[...].astype(LOW), unit_places(d_rows, padded, planes), NN)
    for number, (layer, which, part) in enumerate(pieces):
        rows = placed[number * w_rows : (number + 1) * w_rows].astype(LOW)
        for quarter in range(QUARTERS):
            for block in range(width // half):
                first = layer * 2 * cols_ff + (part * (width // half) + block) * BLOCK + which * half
                lane = quarter * width + block * half
                all_ref[quarter, :, first : first + half] = rows[:, lane : lane + half]
    for quarter in range(QUARTERS):
        for layer in range(1, LAYERS):
            take_qkv(qkv_ref, layer, quarter, weights[:3], gains[0])
            first = LAYERS * 2 * cols_ff + (layer - 1) * qkv_ref.shape[1]
            all_ref[quarter, :, first : first + qkv_ref.shape[1]] = qkv_ref[...].astype(LOW)
    for place, out_ref in enumerate(outs):
        out_ref[...] = all_ref[place ^ place_ref[0]]


def later_parts(place, weights, gains, d_rows, planes):
    w_rows = weights[0].shape[1]
    padded = -(-d_rows // 16) * 16
    cols_ff, width = 2 * planes * padded, 3 * QUARTER_HEADS * HD
    whole = LAYERS * 2 * cols_ff + (LAYERS - 1) * width
    return pl.pallas_call(
        functools.partial(later_parts_kernel, d_rows=d_rows, padded=padded, planes=planes),
        in_specs=[pl.BlockSpec(memory_space=pltpu.SMEM)] + in_vmem(7),
        out_specs=in_vmem(4),
        out_shape=[jax.ShapeDtypeStruct((w_rows, whole), LOW)] * QUARTERS,
        scratch_shapes=[
            pltpu.VMEM((4 * LAYERS * w_rows, 4 * planes * d_rows), jnp.float32),
            pltpu.VMEM((w_rows, width), jnp.float32),
            pltpu.VMEM((QUARTERS, w_rows, whole), LOW),
        ],
        compiler_params=pltpu.CompilerParams(vmem_limit_bytes=VMEM_LIMIT),
        name="later_parts",
    )(place, *weights, *gains)


def put_qkv(came_ref, place_ref, start, outs, layer, weights, gain_ref, gain_out_ref):
    for quarter in range(QUARTERS):
        part = came_ref[place_ref[quarter], :, start : start + 3 * QUARTER_HEADS * HD]
        part = part.astype(jnp.float32)
        for slot in range(QUARTER_HEADS):
            column = HD * (QUARTERS * slot + quarter)
            for which, out_ref in enumerate(outs):
                first = (3 * slot + which) * HD
                out_ref[layer, :, column : column + HD] = part[:, first : first + HD]
    gain_grad = 0.0
    for out_ref, weight_ref in zip(outs, weights):
        grad = out_ref[layer]
        gain_grad = gain_grad + jnp.sum(grad * weight_ref[layer], axis=1, keepdims=True)
        out_ref[layer] = grad * gain_ref[layer]
    gain_out_ref[layer : layer + 1, :] = jnp.broadcast_to(gain_grad, (gain_grad.shape[0], 128)).T[:1]


def put_units(came_ref, place_ref, start, outs, layer, weights, gain_ref, gain_out_ref, d_rows, padded, planes):
    half = BLOCK // 2
    for quarter in range(QUARTERS):
        part = came_ref[place_ref[quarter], :, start : start + 4 * planes * padded]
        part = part.astype(jnp.float32)
        for plane in range(planes):
            for core in range(2):
                column = d_rows * (8 * plane + 2 * quarter + core)
                unit, end = (2 * plane + core) * padded, (2 * plane + core) * padded + d_rows
                while unit < end:
                    stop = min(end, (unit // half + 1) * half)
                    for which, out_ref in enumerate(outs):
                        first = unit // half * BLOCK + which * half + unit % half
                        out_ref[layer, :, column : column + stop - unit] = part[
                            :, first : first + stop - unit
                        ]
                    column, unit = column + stop - unit, stop
    gain_grad = 0.0
    for out_ref, weight_ref in zip(outs, weights):
        grad = out_ref[layer]
        gain_grad = gain_grad + jnp.sum(grad * weight_ref[layer], axis=1, keepdims=True)
        out_ref[layer] = grad * gain_ref[layer]
    gain_out_ref[layer : layer + 1, :] = jnp.broadcast_to(gain_grad, (gain_grad.shape[0], 128)).T[:1]


def finish_kernel(place_ref, *refs, unit_end, w_rows, d_rows, padded, planes, with_out):
    came_ref, *sums = refs[: 1 + LAYERS]
    out_sums, refs = refs[1 + LAYERS : 2 * LAYERS], refs[2 * LAYERS :]
    weights, gains, outs = refs[:5], refs[5:7], refs[7:]
    units_width = 4 * planes * padded
    for layer in range(LAYERS):
        put_units(
            came_ref, place_ref, layer * units_width, outs[4:6], layer, weights[3:], gains[1],
            outs[8], d_rows, padded, planes,
        )
        if layer > 0:
            start = LAYERS * units_width + (layer - 1) * 3 * QUARTER_HEADS * HD
            put_qkv(came_ref, place_ref, start, outs[:3], layer, weights[:3], gains[0], outs[7])
        for block in range(D // BLOCK):
            lanes = slice(block * BLOCK, (block + 1) * BLOCK)
            rows = sums[layer][unit_end + block * padded : unit_end + (block + 1) * padded, :]
            outs[6][layer, :, lanes] = rows.astype(jnp.float32)[:d_rows]
            if with_out and layer > 0:
                rows = out_sums[layer - 1][block * w_rows : (block + 1) * w_rows, :]
                outs[3][layer, :, lanes] = rows.astype(jnp.float32)


def finish_first_kernel(place_ref, came_ref, out_sum_ref, *refs, w_rows, with_out):
    weights, gain_ref, have, outs = refs[:3], refs[3], refs[4:9], refs[9:]
    for layer in range(1, LAYERS):
        for have_ref, out_ref in zip(have, outs):
            out_ref[layer : layer + 1] = have_ref[layer : layer + 1]
    put_qkv(came_ref, place_ref, 0, outs[:3], 0, weights, gain_ref, outs[3])
    if with_out:
        for block in range(D // BLOCK):
            rows = out_sum_ref[block * w_rows : (block + 1) * w_rows, :]
            outs[4][0, :, block * BLOCK : (block + 1) * BLOCK] = rows.astype(jnp.float32)


def finish_gradients(
    place, came, sums, out_sums, weights, gains, d_shape, unit_end, planes, with_out
):
    layers, w_rows, unused = weights[0].shape
    d_rows = d_shape[1]
    padded = -(-d_rows // 16) * 16
    shapes = [weights[0].shape] * 4 + [weights[3].shape] * 2 + [d_shape] + [(layers, w_rows)] * 2
    return pl.pallas_call(
        functools.partial(
            finish_kernel, unit_end=unit_end, w_rows=w_rows, d_rows=d_rows, padded=padded, planes=planes,
            with_out=with_out,
        ),
        in_specs=[pl.BlockSpec(memory_space=pltpu.SMEM)] + in_vmem(7 + 2 * LAYERS),
        out_specs=in_vmem(9),
        out_shape=[jax.ShapeDtypeStruct(shape, jnp.float32) for shape in shapes],
        compiler_params=pltpu.CompilerParams(vmem_limit_bytes=VMEM_LIMIT),
        name="finish_gradients",
    )(place, came, *sums, *out_sums, *weights, *gains)


def finish_first(place, came, out_sum, weights, gain, grads, with_out):
    return pl.pallas_call(
        functools.partial(finish_first_kernel, w_rows=weights[0].shape[1], with_out=with_out),
        in_specs=[pl.BlockSpec(memory_space=pltpu.SMEM)] + in_vmem(11),
        out_specs=in_vmem(5),
        out_shape=[jax.ShapeDtypeStruct(member.shape, jnp.float32) for member in grads],
        compiler_params=pltpu.CompilerParams(vmem_limit_bytes=VMEM_LIMIT),
        name="finish_first",
    )(place, came, out_sum, *weights, gain, *grads)


def on_device(
    tokens,
    w_query,
    w_key,
    w_value,
    w_out,
    w_gate,
    w_up,
    w_down,
    gain_attn,
    gain_ffn,
    variate_bias,
    doc_starts,
    variate_ids,
    time_ids,
    cotangent,
):
    seq = lax.axis_size("seq")
    planes = seq // 2
    spread = planes // QUARTER_HEADS
    tiles = planes // spread
    tok_rows = tokens.shape[0]
    cols = 4 * tok_rows
    all_rows = variate_ids.shape[0]
    w_rows = w_query.shape[1]
    d_rows = w_down.shape[1]
    padded = -(-d_rows // 16) * 16
    quarter_ff = 2 * planes * padded
    quarter_width = QUARTER_HEADS * HD
    split_heads = 2 * w_rows == HD
    here_seq, here_head = lax.axis_index("seq"), lax.axis_index("head")
    here_plane, here_lo = here_seq // 2, here_seq % 2
    here_y, here_core = here_head // 2, here_head % 2
    my_quarter = 2 * here_lo + here_y
    my_head = QUARTERS * (here_plane // spread) + my_quarter
    first_tile = (here_plane % spread) * tiles
    devices = [
        (plane, lo, y, core)
        for plane in range(planes)
        for lo in range(2)
        for y in range(2)
        for core in range(2)
    ]

    def place_of(plane, lo, y, core):
        return 8 * plane + 4 * lo + 2 * y + core

    row_groups = [
        [place_of(plane, lo, y, core) for plane in range(planes) for core in range(2)]
        for lo in range(2)
        for y in range(2)
    ]
    plane_groups = [[2 * plane + lo for plane in range(planes)] for lo in range(2)]
    x_swap = [(place, place ^ 1) for place in range(seq)]
    corner_swap = [
        (place_of(plane, lo, y, core), place_of(plane, 1 - lo, 1 - y, core))
        for plane, lo, y, core in devices
    ]

    def neighbours(across_y, across_x, across_both):
        return (
            lax.ppermute(across_y, "head", Y_SWAP),
            lax.ppermute(across_x, "seq", x_swap),
            lax.ppermute(across_both, BOTH, corner_swap),
        )

    def beside_parts(value):
        return [value, *neighbours(value, value, value)]

    def beside(value):
        return jnp.concatenate(beside_parts(value), axis=0)

    def fold(own, *others):
        return own + sum(part.astype(jnp.float32) for part in neighbours(*others))

    def four_parts(partial):
        low = partial[tok_rows:].astype(LOW).reshape(3, tok_rows, -1)
        return partial[:tok_rows], low[0], low[1], low[2]

    def flip(pair, bit):
        return jnp.where(bit == 0, pair[0], pair[1]), jnp.where(bit == 0, pair[1], pair[0])

    def xor_order(grid, high, low):
        rows = [flip(row, low) for row in grid]
        first, second = zip(*[flip(column, high) for column in zip(*rows)])
        return [list(first), list(second)]

    def cross_rows(parts):
        came = [[None, None], [None, None]]
        for high in range(2):
            for low in range(2):
                hops = [
                    (place_of(plane, lo, y, core), place_of(plane, y ^ high, core ^ low, lo))
                    for plane, lo, y, core in devices
                ]
                came[high][low] = lax.ppermute(parts[2 * high + low], BOTH, hops)
        came = xor_order(came, here_lo, here_y)
        return jnp.concatenate([*came[0], *came[1]], axis=0)

    def cross_back(rows):
        parts = [rows[place * w_rows : (place + 1) * w_rows] for place in range(4)]
        grid = xor_order([parts[:2], parts[2:]], here_lo, here_y)
        came = [[None, None], [None, None]]
        for high in range(2):
            for low in range(2):
                hops = [
                    (place_of(plane, lo, y, core), place_of(plane, core, lo ^ high, y ^ low))
                    for plane, lo, y, core in devices
                ]
                came[high][low] = lax.ppermute(grid[high][low], BOTH, hops)
        return jnp.stack([*came[0], *came[1]])

    device_groups = [[8 * plane + place for place in range(8)] for plane in range(planes)]

    def plane_exchange(value):
        return lax.all_to_all(
            value, BOTH, split_axis=0, concat_axis=0, tiled=True, axis_index_groups=device_groups
        )

    def cross_rows_at_once(sent):
        came = plane_exchange(sent)
        came = jnp.where(here_core == 0, came[:4], came[4:])
        return came.reshape(-1, sent.shape[-1])

    def cross_back_at_once(rows):
        parts = rows.reshape(4, w_rows, -1)
        zeros = jnp.zeros_like(parts)
        sent = [jnp.where(here_core == lo, parts, zeros) for lo in range(2)]
        return plane_exchange(jnp.concatenate(sent, axis=0))

    def gather(part):
        return lax.all_gather(part, BOTH, axis=0, tiled=True, axis_index_groups=row_groups)

    def blocks_of(matrix):
        rows, n = matrix.shape
        return matrix.reshape(rows, n // BLOCK, BLOCK).transpose(1, 0, 2).reshape(-1, BLOCK)

    def from_blocks(packed, rows):
        groups, count = packed.shape[0], packed.shape[1] // rows
        parts = packed.reshape(groups, count, rows, BLOCK).transpose(0, 2, 1, 3)
        return parts.reshape(groups * rows, count * BLOCK)

    def scatter(packed):
        part = lax.psum_scatter(
            packed.reshape(-1, packed.shape[-1]),
            BOTH,
            scatter_dimension=0,
            tiled=True,
            axis_index_groups=row_groups,
        )
        return part

    def whole_out_back(grad):
        spaced = lax.dynamic_update_slice_in_dim(
            jnp.zeros((QUARTER_HEADS, QUARTERS, HD, D), LOW),
            grad.astype(LOW).reshape(QUARTER_HEADS, 1, HD, D),
            my_quarter,
            1,
        )
        return lax.psum_scatter(spaced.reshape(D, D), BOTH, scatter_dimension=0, tiled=True)

    def normalize(values):
        inverse = lax.rsqrt(jnp.mean(values * values, axis=-1, keepdims=True) + NORM_EPS)
        return values * inverse, inverse

    def normalize_back(scaled, inverse, inner):
        return inverse * (inner - scaled * jnp.mean(inner * scaled, axis=-1, keepdims=True))

    def attention_part(layer, qkv_rows):
        blocks = blocks_of(w_out[layer].astype(LOW))
        return jnp.concatenate([qkv_rows, blocks], axis=1)

    def attention_matrices(part):
        whole = gather(part)
        blocks = whole[:, 3 * quarter_width :].reshape(2 * planes, -1, BLOCK)
        return whole[:, : 3 * quarter_width], from_blocks(blocks, w_rows)

    gains = (gain_attn[:, :, None], gain_ffn[:, :, None])
    first_sent = first_parts(
        jnp.reshape(here_lo, (1,)).astype(jnp.int32), (w_query, w_key, w_value), gains[0]
    )
    first_part = attention_part(0, cross_rows_at_once(first_sent))
    first_part, time_ids, w_gate, w_up = lax.optimization_barrier((first_part, time_ids, w_gate, w_up))
    attention_weights, out_weights = [attention_matrices(first_part)], []
    start_scaled, start_inverse = normalize(tokens)
    start_normed = beside(start_scaled.astype(LOW))

    group_rows = 4 * w_rows
    unit_end = 2 * quarter_ff // BLOCK * group_rows
    ffn_end = unit_end + D // BLOCK * padded

    def ffn_part(layer, units_rows):
        down_part = jnp.pad(w_down[layer].astype(LOW), ((0, padded - d_rows), (0, 0)))
        return jnp.concatenate([blocks_of(units_rows), blocks_of(down_part)], axis=0)

    later_sent = later_parts(
        jnp.reshape(2 * here_y + here_core, (1,)).astype(jnp.int32),
        (w_query, w_key, w_value, w_gate, w_up), gains, d_rows, planes,
    )
    later_widths = [2 * quarter_ff] * LAYERS + [3 * quarter_width] * (LAYERS - 1)

    def cut(whole):
        parts, start = [], 0
        for width in later_widths:
            parts.append(whole[..., start : start + width])
            start += width
        return parts

    ffn_weights = []

    def placed_ids(ids):
        ids = ids.reshape(planes, 2, 2, 2, tok_rows)
        ids = jnp.where(here_lo == 0, ids, ids[:, ::-1])
        ids = jnp.where(here_y == 0, ids, ids[:, :, ::-1])
        ids = jnp.where(here_core == 0, ids, ids[:, :, :, ::-1])
        return ids.transpose(3, 0, 1, 2, 4).reshape(2 * planes, cols)

    def my_tiles(value):
        if spread == 1:
            return value
        return lax.dynamic_slice_in_dim(value, first_tile, tiles, 0)

    positions = jnp.arange(all_rows, dtype=jnp.int32)
    doc_ids = jnp.sum((doc_starts[None, :] <= positions[:, None]).astype(jnp.int32), axis=1)
    docs = placed_ids(doc_ids)
    variates = placed_ids(variate_ids)
    q_docs, q_variates = my_tiles(docs[:planes]), my_tiles(variates[:planes])
    extra_row = jnp.arange(HD, dtype=jnp.int32)[None, :, None]

    def one_hot(ids):
        return ids[:, None, :] == extra_row % VARIATES

    def is_doc(ids):
        return ids[:, None, :] == extra_row - 24

    doc_row = (extra_row >= 24) & (extra_row < 32)
    ones_row = (extra_row == 16) | (extra_row == 17) | ((extra_row >= 32) & (extra_row < 35))
    k_hits = one_hot(variates) & (extra_row < 16) | is_doc(docs) & doc_row | ones_row
    k_aug = jnp.where(k_hits, 1.0, 0.0).astype(LOW)

    def query_extra(layer):
        same, other = variate_bias[layer, 0, my_head], variate_bias[layer, 1, my_head]
        gap = same - other
        gap_lead, other_lead = (part.astype(LOW).astype(jnp.float32) for part in (gap, other))
        gap_part = jnp.where(extra_row < VARIATES, gap_lead, gap - gap_lead)
        other_part = jnp.where(extra_row == 16, other_lead, other - other_lead)
        spread_gap = jnp.where(one_hot(q_variates), gap_part, 0.0)
        shut = jnp.where(doc_row & ~is_doc(q_docs), FLOOR_SCORE, 0.0)
        tail = jnp.where(extra_row < 18, other_part, shut)
        return jnp.where(extra_row < 16, spread_gap, tail).astype(LOW)

    q_augs = [query_extra(layer) for layer in range(LAYERS)]
    q_onehots = (q_variates[:, None, :] == jnp.arange(VARIATES, dtype=jnp.int32)[:, None]).astype(
        jnp.float32
    )

    half_dim = HD // 2
    frequency = jnp.exp(jnp.arange(half_dim).astype(jnp.float32) * (-2.0 * math.log(10000.0) / HD))
    times = beside(time_ids.astype(jnp.float32))
    angles = frequency[:, None] * times[None, :]
    cosines, sines = jnp.cos(angles), jnp.sin(angles)
    start_normed, later_sent, k_aug, cosines, sines, *q_augs = lax.optimization_barrier(
        (start_normed, later_sent, k_aug, cosines, sines, *q_augs)
    )

    def rotate(values, sines):
        former, latter = values[:, :half_dim], values[:, half_dim:]
        return jnp.concatenate(
            [former * cosines - latter * sines, latter * cosines + former * sines], axis=1
        )

    def to_heads(value):
        if spread > 1:
            value = jnp.repeat(value, spread, axis=0)
        return lax.all_to_all(
            value, "seq", split_axis=0, concat_axis=0, tiled=True, axis_index_groups=plane_groups
        )

    def all_blocks(value):
        if spread == 1:
            return value
        zeros = jnp.zeros((planes,) + value.shape[1:], value.dtype)
        return lax.dynamic_update_slice_in_dim(zeros, value, first_tile, 0)

    def over_spread(value):
        if spread == 1:
            return value
        value = value.reshape((QUARTER_HEADS, spread) + value.shape[1:])
        return jnp.sum(value.astype(jnp.float32), axis=1).astype(LOW)

    def from_heads(value):
        return over_spread(
            lax.all_to_all(
                value, "seq", split_axis=0, concat_axis=0, tiled=True, axis_index_groups=plane_groups
            )
        )

    chip_groups = [
        [place_of(plane, lo, y, core) for plane in range(planes) for lo in range(2) for y in range(2)]
        for core in range(2)
    ]

    def over_chips(value):
        shape = value.shape
        value = value.reshape(-1, *shape[2:])
        value = lax.all_to_all(
            value, BOTH, split_axis=0, concat_axis=0, tiled=True, axis_index_groups=chip_groups
        )
        return value.reshape(shape)

    chip_flips = jnp.reshape(my_quarter, (1,)).astype(jnp.int32)

    def plane_order(value):
        grid = [[value[:, 2 * lo + y] for y in range(2)] for lo in range(2)]
        grid = xor_order(grid, here_lo, here_y)
        return jnp.stack([*grid[0], *grid[1]])

    def chip_order(value):
        grid = xor_order([[value[0], value[1]], [value[2], value[3]]], here_lo, here_y)
        return jnp.stack([*grid[0], *grid[1]], axis=1)

    def sum_everywhere(value):
        for axis, size in (("head", 4), ("seq", seq)):
            hop = 1
            while hop < size:
                swap = [(place, place ^ hop) for place in range(size)]
                value = value + lax.ppermute(value, axis, swap)
                hop *= 2
        return value

    def share_for_out(middle_low, attended):
        pieces = attended.reshape(4, quarter_width, tok_rows)
        cuts = quarter_width // tok_rows

        def joined(piece):
            parts = [piece[cut * tok_rows : (cut + 1) * tok_rows] for cut in range(cuts)]
            return jnp.concatenate([middle_low, *parts], axis=1)

        came = neighbours(*(joined(piece) for piece in pieces[1:]))
        tokens_low = jnp.concatenate([middle_low, *(part[:, :D] for part in came)], axis=0)

        def results(part):
            return jnp.concatenate(
                [part[:, D + cut * tok_rows : D + (cut + 1) * tok_rows] for cut in range(cuts)], axis=0
            )

        return tokens_low, jnp.concatenate([pieces[0], *(results(part) for part in came)], axis=1)

    stream = tokens
    saved = []
    for layer in range(LAYERS):
        qkv_matrix, out_quarter = attention_weights[layer]
        if layer == 0:
            scaled_one, inverse_one, normed = start_scaled, start_inverse, start_normed
        else:
            scaled_one, inverse_one = normalize(stream)
            normed = beside(scaled_one.astype(LOW))
        projected = dot(qkv_matrix, normed, TT).reshape(QUARTER_HEADS, 3 * HD, cols)
        query = rotate(projected[:, :HD], sines) * (1.0 / math.sqrt(HD))
        key = rotate(projected[:, HD : 2 * HD], sines)
        sent = jnp.concatenate([query, key, projected[:, 2 * HD :]], axis=1).astype(LOW)
        if layer == 0:
            later_weights = cross_rows(later_sent)
            sent, cotangent = lax.optimization_barrier((sent, cotangent))
            last_grad_parts = beside_parts(cotangent.astype(LOW))
        own = to_heads(sent)
        if layer == 0:
            own, last_grad_parts = lax.optimization_barrier((own, last_grad_parts))
        next_part = ffn_part(layer, cut(later_weights)[layer])
        own, next_part = lax.optimization_barrier((own, next_part))
        packed = gather(next_part).reshape(2 * planes, -1, BLOCK)
        ffn_weights.append(packed)
        own, out_quarter = lax.optimization_barrier((own, out_quarter))
        halves = out_quarter.reshape(2, quarter_width // 2, D)
        half = jnp.where(here_core == 0, halves[0], halves[1])
        out_parts = neighbours(half, half, half)
        sib = lax.ppermute(own[:, HD:], "head", CORE_SWAP)
        queries = my_tiles(own)
        q_aug = q_augs[layer]
        out, lse = attention_forward(chip_flips, queries, q_aug, own, sib, k_aug)
        out, *out_parts = lax.optimization_barrier((out, *out_parts))
        mine = jnp.stack(out_parts)
        other = lax.ppermute(mine, "head", CORE_SWAP)
        pairs = jnp.where(
            here_core == 0, jnp.stack([mine, other], axis=1), jnp.stack([other, mine], axis=1)
        )
        out_matrix = jnp.concatenate([out_quarter, pairs.reshape(3 * quarter_width, D)], axis=0)
        out_weights.append(out_matrix)
        attended = over_spread(over_chips(all_blocks(out))).reshape(QUARTER_HEADS, 4, HD, tok_rows)
        attended = plane_order(attended).reshape(D, tok_rows)
        attended, out_matrix = lax.optimization_barrier((attended, out_matrix))
        middle = stream + dot(attended, out_matrix, TN)
        scaled_two, inverse_two = normalize(middle)
        normed_parts = beside_parts(scaled_two.astype(LOW))
        if layer < LAYERS - 1:
            next_part = attention_part(layer + 1, cut(later_weights)[LAYERS + layer])
            normed_parts, next_part = lax.optimization_barrier((normed_parts, next_part))
            attention_weights.append(attention_matrices(next_part))
        both, hidden, *parts = ffn_forward(normed_parts, packed, quarter_ff, group_rows, padded)
        saved.append(
            (
                scaled_one, inverse_one, normed, own, sib, queries, q_aug, out, lse, attended,
                scaled_two, inverse_two, normed_parts, both, hidden,
            )
        )
        if layer < LAYERS - 1:
            stream = middle + fold(*parts)
        else:
            last_middle, last_parts = middle, parts

    upstream = cotangent
    whole_grads, ffn_sums, qkv_sums = [None] * LAYERS, [None] * LAYERS, [None] * LAYERS
    bias_parts = [None] * LAYERS
    for layer in reversed(range(LAYERS)):
        qkv_matrix, unused = attention_weights[layer]
        out_matrix, packed = out_weights[layer], ffn_weights[layer]
        (
            scaled_one, inverse_one, normed, own, sib, queries, q_aug, out, lse, attended,
            scaled_two, inverse_two, normed_parts, both, hidden,
        ) = saved[layer]
        if layer < LAYERS - 1:
            upstream_parts = beside_parts(upstream.astype(LOW))
        else:
            upstream_parts = last_grad_parts
        grad_units, *parts = ffn_backward(upstream_parts, packed, both, quarter_ff, group_rows, padded)
        inner = fold(*parts)
        buffer = ffn_weight_grads(
            normed_parts, grad_units, hidden, upstream_parts, 2 * planes, group_rows, padded
        )
        inner, buffer = lax.optimization_barrier((inner, buffer))
        if layer < LAYERS - 1:
            buffer, qkv_sums[layer + 1] = lax.optimization_barrier((buffer, qkv_sums[layer + 1]))
        ffn_sums[layer] = scatter(buffer)
        grad_middle = upstream + normalize_back(scaled_two, inverse_two, inner)
        middle_low = grad_middle.astype(LOW)
        grad_attended = dot(out_matrix, middle_low, NT).astype(LOW)
        grad_attended = chip_order(grad_attended.reshape(4, QUARTER_HEADS, HD, tok_rows))
        if spread > 1:
            grad_attended = jnp.repeat(grad_attended, spread, axis=0)
        out_grad = my_tiles(over_chips(grad_attended))
        out_grad, middle_low, attended = lax.optimization_barrier((out_grad, middle_low, attended))
        middle_low, attended = share_for_out(middle_low, attended)
        grad_q, grad_kv = attention_backward(
            chip_flips, queries, q_aug, lse, out, out_grad, own, sib, k_aug
        )
        grad_kv, middle_low, attended = lax.optimization_barrier((grad_kv, middle_low, attended))
        if not split_heads:
            whole_grads[layer] = whole_out_back(dot(attended, middle_low, NN))
        else:
            out_blocks = out_weight_grad(attended, middle_low, w_rows)
        same_grad = jnp.sum(grad_q[:, HD : HD + VARIATES] * q_onehots)
        all_grad = jnp.sum(grad_q[:, HD + 16])
        crossed = lax.ppermute(grad_kv[planes:], "head", CORE_SWAP)
        grad_kv = (grad_kv[:planes].astype(jnp.float32) + crossed.astype(jnp.float32)).astype(LOW)
        grad_q = (grad_q[:, :HD] * (1.0 / math.sqrt(HD))).astype(LOW)
        if layer == LAYERS - 1:
            grad_kv, *last_parts = lax.optimization_barrier((grad_kv, *last_parts))
            stream = last_middle + fold(*last_parts)
        grad_heads = from_heads(jnp.concatenate([all_blocks(grad_q), grad_kv], axis=1))
        bias_parts[layer] = jnp.stack([same_grad, all_grad - same_grad])
        if layer == LAYERS - 1:
            grad_heads, stream, bias_parts[layer] = lax.optimization_barrier(
                (grad_heads, stream, bias_parts[layer])
            )
        if layer == 0:
            later_sums = [from_blocks(member[None, :unit_end], group_rows) for member in ffn_sums]
            later_sums += [member[:, : 3 * quarter_width] for member in qkv_sums[1:]]
            came = cross_back(jnp.concatenate(later_sums, axis=1))
            grad_heads, came = lax.optimization_barrier((grad_heads, came))
        grad_heads = jnp.concatenate(
            [
                rotate(grad_heads[:, :HD].astype(jnp.float32), -sines).astype(LOW),
                rotate(grad_heads[:, HD : 2 * HD].astype(jnp.float32), -sines).astype(LOW),
                grad_heads[:, 2 * HD :],
            ],
            axis=1,
        ).reshape(3 * quarter_width, cols)
        partial = dot(grad_heads, qkv_matrix, TT)
        qkv_grad = dot(normed, grad_heads, TT).astype(LOW)
        if split_heads:
            qkv_grad = jnp.concatenate([qkv_grad, out_blocks.reshape(-1, BLOCK)], axis=1)
        if layer > 0:
            inner = fold(*four_parts(partial))
            inner, qkv_grad = lax.optimization_barrier((inner, qkv_grad))
        qkv_grad, ffn_sums[layer] = lax.optimization_barrier((qkv_grad, ffn_sums[layer]))
        qkv_sums[layer] = scatter(qkv_grad)
        if layer > 0:
            upstream = grad_middle + normalize_back(scaled_one, inverse_one, inner)

    later_sums = [from_blocks(member[None, :unit_end], group_rows) for member in ffn_sums]
    out_sums = [member[:, 3 * quarter_width :] for member in qkv_sums]
    qkv_sums = [member[:, : 3 * quarter_width] for member in qkv_sums]
    if not split_heads:
        out_sums = [member[:, :BLOCK] for member in qkv_sums]
    bias_local = lax.dynamic_update_slice(
        jnp.zeros((LAYERS, 2, HEADS), jnp.float32), jnp.stack(bias_parts)[:, :, None], (0, 0, my_head)
    )
    bias_total = sum_everywhere(bias_local)
    quarters = jnp.arange(QUARTERS, dtype=jnp.int32)
    weights = (w_query, w_key, w_value, w_gate, w_up)
    *grads, gain_one, gain_two = finish_gradients(
        quarters ^ (2 * here_y + here_core), came, ffn_sums,
        out_sums[1:], weights, gains, w_down.shape, unit_end, planes, split_heads,
    )
    qkv_sums[0], out_sums[0], gain_two, parts, grads = lax.optimization_barrier(
        (qkv_sums[0], out_sums[0], gain_two, four_parts(partial), grads)
    )
    inner = fold(*parts)
    upstream = grad_middle + normalize_back(scaled_one, inverse_one, inner)
    *grads[:3], gain_one, grads[3] = finish_first(
        2 * quarters + here_lo, cross_back_at_once(qkv_sums[0]), out_sums[0], weights[:3], gains[0],
        [*grads[:3], gain_one, grads[3]], split_heads,
    )
    if not split_heads:
        grads[3] = jnp.stack(whole_grads).astype(jnp.float32)
    return (stream, upstream, *grads, gain_one, gain_two, bias_total)


def solution(mesh):
    rows = P(BOTH, None)
    middle = P(None, BOTH, None)
    gains = P(None, BOTH)
    return jax.shard_map(
        on_device,
        mesh=mesh,
        in_specs=(rows,) + (middle,) * 7 + (gains,) * 2 + (P(),) * 3 + (P(BOTH), rows),
        out_specs=(rows, rows) + (middle,) * 7 + (gains,) * 2 + (P(),),
        check_vma=False,
    )
```

```python
import functools
import math

import jax
import jax.numpy as jnp
from jax import lax
from jax.experimental import pallas as pl
from jax.experimental.pallas import tpu as pltpu
from jax.sharding import PartitionSpec as P

D = 1024
HEADS = 16
HD = 64
LAYERS = 2
VARIATES = 8
BLOCK = 256

NORM_EPS = 1e-05
FLOOR_SCORE = -1e30
LOW = jnp.bfloat16
BOTH = ("seq", "head")

QUARTERS = 4
QUARTER_HEADS = HEADS // QUARTERS
Y_SWAP = [(place, place ^ 2) for place in range(4)]
CORE_SWAP = [(place, place ^ 1) for place in range(4)]

NN = (((1,), (0,)), ((), ()))
NT = (((1,), (1,)), ((), ()))
TN = (((0,), (0,)), ((), ()))
TT = (((0,), (1,)), ((), ()))
VMEM_LIMIT = 56 * 1024 * 1024


def in_vmem(count):
    return [pl.BlockSpec(memory_space=pltpu.VMEM)] * count


def cost(flops, operands, results, transcendentals=0):
    moved = sum(member.size * member.dtype.itemsize for member in [*operands, *results])
    return pl.CostEstimate(flops=flops, bytes_accessed=moved, transcendentals=transcendentals)


def dot(left, right, dims):
    return lax.dot_general(left, right, dims, preferred_element_type=jnp.float32)


def forward_kernel(flip_ref, q_ref, q_aug_ref, own_ref, sib_ref, k_aug_ref, out_ref, lse_ref):
    blocks = own_ref.shape[0]
    sources = ((own_ref, HD), (sib_ref, 0))
    spots = [(half, block) for half in range(2) for block in range(blocks)]
    cols = q_ref.shape[-1]
    q_side = jnp.concatenate([q_ref[0, :HD, :], q_aug_ref[0]], axis=0).T
    top = jnp.full((cols, 1), FLOOR_SCORE, jnp.float32)
    total = jnp.zeros((cols, 1), jnp.float32)
    acc = jnp.zeros((cols, HD), jnp.float32)

    def scores(half, block):
        ref, low_row = sources[half]
        extra = k_aug_ref[half * blocks + block]
        k_side = jnp.concatenate([ref[block, low_row : low_row + HD, :], extra], axis=0)
        return dot(q_side, k_side, NN)

    following = scores(*spots[0])
    for number, (half, block) in enumerate(spots):
        part = following
        if number + 1 < len(spots):
            following = scores(*spots[number + 1])
        fresh = jnp.maximum(top, jnp.max(part, axis=-1, keepdims=True))
        shrink = jnp.exp(top - fresh)
        prob = jnp.exp(part - fresh)
        total = total * shrink + jnp.sum(prob, axis=-1, keepdims=True)
        ref, low_row = sources[half]
        values = ref[block, low_row + HD : low_row + 2 * HD, :]
        acc = acc * shrink + dot(prob.astype(LOW), values, NT)
        top = fresh
    result = acc / total
    lse = jnp.broadcast_to(top + jnp.log(total), (cols, HD))
    both = jnp.concatenate([result, lse], axis=1).T
    piece = out_ref.shape[-1]
    for place in range(cols // piece):
        part = both[:HD, place * piece : (place + 1) * piece]
        out_ref[0, place ^ flip_ref[0]] = part.astype(LOW)
    lse_ref[0] = both[HD : HD + 8]


def split_rows(row, rows):
    one = row.astype(LOW).astype(jnp.float32)
    two = (row - one).astype(LOW).astype(jnp.float32)
    three = row - one - two
    pad = jnp.zeros((rows - 3, row.shape[-1]), jnp.float32)
    return jnp.concatenate([one, two, three, pad], axis=0).astype(LOW)


def backward_kernel(
    flip_ref, q_ref, q_aug_ref, lse_ref, out_ref, grad_ref, own_ref, sib_ref, k_aug_ref,
    dq_ref, dkv_ref, dkv_acc,
):
    step = pl.program_id(0)
    blocks = own_ref.shape[0]
    sources = ((own_ref, HD), (sib_ref, 0))
    cols, key_cols = q_ref.shape[-1], own_ref.shape[-1]

    @pl.when(step == 0)
    def _():
        dkv_acc[...] = jnp.zeros_like(dkv_acc)

    q_low = q_ref[0, :HD, :]
    places = range(grad_ref.shape[1])
    g_low = jnp.concatenate([grad_ref[0, place ^ flip_ref[0]] for place in places], axis=1)
    out = jnp.concatenate([out_ref[0, place ^ flip_ref[0]] for place in places], axis=1)
    row_dot = jnp.sum(g_low.astype(jnp.float32) * out.astype(jnp.float32), axis=0, keepdims=True)
    aug = jnp.concatenate(
        [q_aug_ref[0, :32, :], split_rows(-lse_ref[0, :1, :], 16), q_aug_ref[0, 48:, :]], axis=0
    )
    q_side = jnp.concatenate([q_low, aug], axis=0).T
    g_side = jnp.concatenate([g_low, split_rows(-row_dot, HD)], axis=0).T
    ones = jnp.concatenate(
        [jnp.ones((16, key_cols), LOW), jnp.zeros((HD - 16, key_cols), LOW)], axis=0
    )
    dq = jnp.zeros((cols, 2 * HD), jnp.float32)
    spots = [(half, block) for half in range(2) for block in range(blocks)]

    def products(half, block):
        ref, low_row = sources[half]
        k_side = jnp.concatenate(
            [ref[block, low_row : low_row + HD, :], k_aug_ref[half * blocks + block]], axis=0
        )
        v_side = jnp.concatenate([ref[block, low_row + HD : low_row + 2 * HD, :], ones], axis=0)
        return k_side, dot(q_side, k_side, NN), dot(g_side, v_side, NN)

    following = products(*spots[0])
    for spot in range(len(spots)):
        k_side, score, prob_grad = following
        if spot + 1 < len(spots):
            following = products(*spots[spot + 1])
        prob = jnp.exp(score)
        score_grad = (prob * prob_grad).astype(LOW)
        dq = dq + dot(score_grad, k_side, NT)
        dkv_acc[spot, :HD, :] += dot(q_low, score_grad, NN)
        dkv_acc[spot, HD:, :] += dot(g_low, prob.astype(LOW), NN)
    dq_ref[0] = dq.T

    @pl.when(step == pl.num_programs(0) - 1)
    def _():
        dkv_ref[...] = dkv_acc[...].astype(LOW)


def whole_spec(shape):
    rank = len(shape)
    return pl.BlockSpec(shape, lambda i, flip: (0,) * rank)


def tile_spec(rows, cols):
    return pl.BlockSpec((1, rows, cols), lambda i, flip: (i, 0, 0))


def owner_spec(shape):
    return pl.BlockSpec((1, *shape[1:]), lambda i, flip: (i, 0, 0, 0))


def attention_forward(flip, queries, q_aug, own, sib, k_aug):
    tiles, unused, cols = queries.shape
    pairs = 2 * tiles * own.shape[0] * cols * cols
    out_shape = (tiles, 4, HD, cols // 4)
    results = [
        jax.ShapeDtypeStruct(out_shape, LOW),
        jax.ShapeDtypeStruct((tiles, 8, cols), jnp.float32),
    ]
    return pl.pallas_call(
        forward_kernel,
        grid_spec=pltpu.PrefetchScalarGridSpec(
            num_scalar_prefetch=1,
            grid=(tiles,),
            in_specs=[tile_spec(3 * HD, cols), tile_spec(HD, cols)]
            + [whole_spec(member.shape) for member in (own, sib, k_aug)],
            out_specs=[owner_spec(out_shape), tile_spec(8, cols)],
        ),
        out_shape=results,
        cost_estimate=cost(16 * HD * pairs, [queries, own, sib], results, pairs),
        compiler_params=pltpu.CompilerParams(vmem_limit_bytes=VMEM_LIMIT),
        name="attention_forward",
    )(flip, queries, q_aug, own, sib, k_aug)


def attention_backward(flip, queries, q_aug, lse, out, grad, own, sib, k_aug):
    tiles, unused, cols = queries.shape
    dkv_shape = (2 * own.shape[0], 2 * HD, cols)
    pairs = 2 * tiles * own.shape[0] * cols * cols
    results = [
        jax.ShapeDtypeStruct((tiles, 2 * HD, cols), jnp.float32),
        jax.ShapeDtypeStruct(dkv_shape, LOW),
    ]
    return pl.pallas_call(
        backward_kernel,
        grid_spec=pltpu.PrefetchScalarGridSpec(
            num_scalar_prefetch=1,
            grid=(tiles,),
            in_specs=[tile_spec(3 * HD, cols), tile_spec(HD, cols), tile_spec(8, cols)]
            + [owner_spec(out.shape)] * 2
            + [whole_spec(member.shape) for member in (own, sib, k_aug)],
            out_specs=[tile_spec(2 * HD, cols), whole_spec(dkv_shape)],
            scratch_shapes=[pltpu.VMEM(dkv_shape, jnp.float32)],
        ),
        out_shape=results,
        cost_estimate=cost(32 * HD * pairs, [queries, own, sib], results, pairs),
        compiler_params=pltpu.CompilerParams(vmem_limit_bytes=VMEM_LIMIT),
        name="attention_backward",
    )(flip, queries, q_aug, lse, out, grad, own, sib, k_aug)


def silu_parts(gate):
    sigmoid = 1.0 / (1.0 + jnp.exp(-gate))
    return sigmoid, gate * sigmoid


def put_parts(values, lanes, own_ref, *low_refs):
    rows = own_ref.shape[0]
    own_ref[:, lanes] = values[:rows]
    for place, low_ref in enumerate(low_refs):
        low_ref[:, lanes] = values[(place + 1) * rows : (place + 2) * rows].astype(LOW)


def parts_of(tokens, lanes, index):
    shape = (tokens // 4, D)
    types = [jnp.float32, LOW, LOW, LOW]
    return (
        [jax.ShapeDtypeStruct(shape, kind) for kind in types],
        [pl.BlockSpec((tokens // 4, lanes), index) for unused in types],
    )


def join_rows(x_ref, refs):
    @pl.when(pl.program_id(0) == 0)
    def _():
        rows = refs[0].shape[0]
        for place, ref in enumerate(refs):
            x_ref[place * rows : (place + 1) * rows, :] = ref[...]


def ffn_forward_kernel(*refs, unit_rows, down_rows, unit_steps):
    unit_ref, down_ref, both_ref, hidden_ref = refs[4:8]
    out_refs, x_ref = refs[8:12], refs[12]
    join_rows(x_ref, refs[:4])
    step = pl.program_id(0)
    half = BLOCK // 2

    @pl.when(step < unit_steps)
    def _():
        count = unit_ref.shape[1] // unit_rows
        for place in range(count):
            matrix = unit_ref[:, place * unit_rows : (place + 1) * unit_rows, :].reshape(-1, BLOCK)
            both = dot(x_ref[...], matrix, NN)
            both_ref[place] = both.astype(both_ref.dtype)
            hidden = silu_parts(both[:, :half])[1] * both[:, half:]
            spot = step * count + place
            hidden_ref[:, pl.ds(pl.multiple_of(spot * half, half), half)] = hidden.astype(LOW)

    @pl.when(step >= unit_steps)
    def _():
        for place in range(down_ref.shape[1] // down_rows):
            matrix = down_ref[:, place * down_rows : (place + 1) * down_rows, :].reshape(-1, BLOCK)
            lanes = slice(place * BLOCK, (place + 1) * BLOCK)
            put_parts(dot(hidden_ref[...], matrix, NN), lanes, *out_refs)


def ffn_backward_kernel(*refs, unit_rows, down_rows, down_steps):
    unit_ref, down_ref, both_ref, grads_ref = refs[4:8]
    part_refs, inner_ref, hidden_grad, g_ref = refs[8:12], refs[12], refs[13], refs[14]
    join_rows(g_ref, refs[:4])
    step = pl.program_id(0)
    half = BLOCK // 2

    @pl.when(step < down_steps)
    def _():
        total = 0.0
        for place in range(down_ref.shape[1] // down_rows):
            matrix = down_ref[:, place * down_rows : (place + 1) * down_rows, :].reshape(-1, BLOCK)
            lanes = pl.ds(pl.multiple_of((step * FFN_DOWNS + place) * BLOCK, BLOCK), BLOCK)
            total = total + dot(g_ref[:, lanes], matrix, NT)

        @pl.when(step == 0)
        def _():
            hidden_grad[...] = total

        @pl.when(step > 0)
        def _():
            hidden_grad[...] += total

    @pl.when(step >= down_steps)
    def _():
        count = unit_ref.shape[1] // unit_rows
        total = 0.0
        for place in range(count):
            matrix = unit_ref[:, place * unit_rows : (place + 1) * unit_rows, :].reshape(-1, BLOCK)
            spot = (step - down_steps) * count + place
            gate = both_ref[place, :, :half].astype(jnp.float32)
            upward = both_ref[place, :, half:].astype(jnp.float32)
            above = hidden_grad[:, pl.ds(pl.multiple_of(spot * half, half), half)]
            sigmoid, silu = silu_parts(gate)
            grad_gate = above * upward * (sigmoid * (1.0 + gate * (1.0 - sigmoid)))
            grads = jnp.concatenate([grad_gate, above * silu], axis=1).astype(LOW)
            grads_ref[place] = grads
            total = total + dot(grads, matrix, NT)

        @pl.when(step == down_steps)
        def _():
            inner_ref[...] = total

        @pl.when(step > down_steps)
        def _():
            inner_ref[...] += total

    @pl.when(step == pl.num_programs(0) - 1)
    def _():
        put_parts(inner_ref[...], slice(0, D), *part_refs)


def ffn_turn_kernel(*refs, unit_rows, down_rows, down_steps):
    unit_ref, down_ref, grads_ref, hidden_ref = refs[8:12]
    part_refs, inner_ref, hidden_grad, x_ref, g_ref = refs[12:16], *refs[16:20]
    join_rows(x_ref, refs[:4])
    join_rows(g_ref, refs[4:8])
    step = pl.program_id(0)
    half = BLOCK // 2

    @pl.when(step < down_steps)
    def _():
        total = 0.0
        for place in range(down_ref.shape[1] // down_rows):
            matrix = down_ref[:, place * down_rows : (place + 1) * down_rows, :].reshape(-1, BLOCK)
            lanes = pl.ds(pl.multiple_of((step * FFN_DOWNS + place) * BLOCK, BLOCK), BLOCK)
            total = total + dot(g_ref[:, lanes], matrix, NT)

        @pl.when(step == 0)
        def _():
            hidden_grad[...] = total

        @pl.when(step > 0)
        def _():
            hidden_grad[...] += total

    @pl.when(step >= down_steps)
    def _():
        count = unit_ref.shape[1] // unit_rows
        total = 0.0
        for place in range(count):
            matrix = unit_ref[:, place * unit_rows : (place + 1) * unit_rows, :].reshape(-1, BLOCK)
            both = dot(x_ref[...], matrix, NN)
            gate, upward = both[:, :half], both[:, half:]
            spot = (step - down_steps) * count + place
            lanes = pl.ds(pl.multiple_of(spot * half, half), half)
            above = hidden_grad[:, lanes]
            sigmoid, silu = silu_parts(gate)
            hidden_ref[:, lanes] = (silu * upward).astype(LOW)
            grad_gate = above * upward * (sigmoid * (1.0 + gate * (1.0 - sigmoid)))
            grads = jnp.concatenate([grad_gate, above * silu], axis=1).astype(LOW)
            grads_ref[place] = grads
            total = total + dot(grads, matrix, NT)

        @pl.when(step == down_steps)
        def _():
            inner_ref[...] = total

        @pl.when(step > down_steps)
        def _():
            inner_ref[...] += total

    @pl.when(step == pl.num_programs(0) - 1)
    def _():
        put_parts(inner_ref[...], slice(0, D), *part_refs)


def ffn_down_kernel(hidden_ref, down_ref, *out_refs, down_rows):
    for place in range(down_ref.shape[1] // down_rows):
        matrix = down_ref[:, place * down_rows : (place + 1) * down_rows, :].reshape(-1, BLOCK)
        lanes = slice(place * BLOCK, (place + 1) * BLOCK)
        put_parts(dot(hidden_ref[...], matrix, NN), lanes, *out_refs)


FFN_DOWNS = 4


def ffn_units(cols_ff):
    return max(count for count in (1, 2, 3) if 2 * cols_ff // BLOCK % count == 0)


def ffn_specs(cols_ff, unit_rows, down_rows, groups, unit_step, down_step):
    unit_blocks, down_blocks = 2 * cols_ff // BLOCK, D // BLOCK
    units, downs = ffn_units(cols_ff) * unit_rows, FFN_DOWNS * down_rows
    first_down = unit_blocks * unit_rows // downs
    return (
        unit_blocks // ffn_units(cols_ff),
        down_blocks // FFN_DOWNS,
        [
            pl.BlockSpec((groups, units, BLOCK), lambda i: (0, unit_step(i), 0)),
            pl.BlockSpec((groups, downs, BLOCK), lambda i: (0, first_down + down_step(i), 0)),
        ],
    )


def ffn_forward(rows, packed, cols_ff, unit_rows, down_rows):
    tokens, unit_steps = 4 * rows[0].shape[0], 2 * cols_ff // BLOCK // ffn_units(cols_ff)
    unit_step = lambda i: jnp.minimum(i, unit_steps - 1)
    down_step = lambda i: jnp.maximum(i - unit_steps, 0)
    unit_steps, down_steps, specs = ffn_specs(
        cols_ff, unit_rows, down_rows, packed.shape[0], unit_step, down_step
    )
    parts, part_specs = parts_of(tokens, FFN_DOWNS * BLOCK, lambda i: (0, down_step(i)))
    results = [
        jax.ShapeDtypeStruct((2 * cols_ff // BLOCK, tokens, BLOCK), LOW),
        jax.ShapeDtypeStruct((tokens, cols_ff), LOW),
        *parts,
    ]
    return pl.pallas_call(
        functools.partial(
            ffn_forward_kernel, unit_rows=unit_rows, down_rows=down_rows, unit_steps=unit_steps
        ),
        grid=(unit_steps + down_steps,),
        in_specs=[pl.BlockSpec(rows[0].shape, lambda i: (0, 0))] * 4 + specs,
        out_specs=[
            pl.BlockSpec((ffn_units(cols_ff), tokens, BLOCK), lambda i: (unit_step(i), 0, 0)),
            pl.BlockSpec((tokens, cols_ff), lambda i: (0, 0)),
            *part_specs,
        ],
        out_shape=results,
        scratch_shapes=[pltpu.VMEM((tokens, D), LOW)],
        cost_estimate=cost(6 * tokens * D * cols_ff, [*rows, packed], results),
        compiler_params=pltpu.CompilerParams(vmem_limit_bytes=VMEM_LIMIT),
        name="ffn_forward",
    )(*rows, packed, packed)


def ffn_backward(rows, packed, both, cols_ff, unit_rows, down_rows):
    tokens, down_steps = 4 * rows[0].shape[0], D // BLOCK // FFN_DOWNS
    unit_step = lambda i: jnp.maximum(i - down_steps, 0)
    down_step = lambda i: jnp.minimum(i, down_steps - 1)
    unit_steps, down_steps, specs = ffn_specs(
        cols_ff, unit_rows, down_rows, packed.shape[0], unit_step, down_step
    )
    unit_spec = pl.BlockSpec((ffn_units(cols_ff), tokens, BLOCK), lambda i: (unit_step(i), 0, 0))
    parts, part_specs = parts_of(tokens, D, lambda i: (0, 0))
    results = [jax.ShapeDtypeStruct((2 * cols_ff // BLOCK, tokens, BLOCK), LOW), *parts]
    return pl.pallas_call(
        functools.partial(
            ffn_backward_kernel, unit_rows=unit_rows, down_rows=down_rows, down_steps=down_steps
        ),
        grid=(unit_steps + down_steps,),
        in_specs=[pl.BlockSpec(rows[0].shape, lambda i: (0, 0))] * 4 + [*specs, unit_spec],
        out_specs=[unit_spec, *part_specs],
        out_shape=results,
        scratch_shapes=[
            pltpu.VMEM((tokens, D), jnp.float32),
            pltpu.VMEM((tokens, cols_ff), jnp.float32),
            pltpu.VMEM((tokens, D), LOW),
        ],
        cost_estimate=cost(6 * tokens * D * cols_ff, [*rows, packed, both], results),
        compiler_params=pltpu.CompilerParams(vmem_limit_bytes=VMEM_LIMIT),
        name="ffn_backward",
    )(*rows, packed, packed, both)


def ffn_turn(rows, grad_rows, packed, cols_ff, unit_rows, down_rows):
    tokens, down_steps = 4 * rows[0].shape[0], D // BLOCK // FFN_DOWNS
    unit_step = lambda i: jnp.maximum(i - down_steps, 0)
    down_step = lambda i: jnp.minimum(i, down_steps - 1)
    unit_steps, down_steps, specs = ffn_specs(
        cols_ff, unit_rows, down_rows, packed.shape[0], unit_step, down_step
    )
    parts, part_specs = parts_of(tokens, D, lambda i: (0, 0))
    results = [
        jax.ShapeDtypeStruct((2 * cols_ff // BLOCK, tokens, BLOCK), LOW),
        jax.ShapeDtypeStruct((tokens, cols_ff), LOW),
        *parts,
    ]
    return pl.pallas_call(
        functools.partial(
            ffn_turn_kernel, unit_rows=unit_rows, down_rows=down_rows, down_steps=down_steps
        ),
        grid=(unit_steps + down_steps,),
        in_specs=[pl.BlockSpec(rows[0].shape, lambda i: (0, 0))] * 8 + specs,
        out_specs=[
            pl.BlockSpec((ffn_units(cols_ff), tokens, BLOCK), lambda i: (unit_step(i), 0, 0)),
            pl.BlockSpec((tokens, cols_ff), lambda i: (0, 0)),
            *part_specs,
        ],
        out_shape=results,
        scratch_shapes=[
            pltpu.VMEM((tokens, D), jnp.float32),
            pltpu.VMEM((tokens, cols_ff), jnp.float32),
            pltpu.VMEM((tokens, D), LOW),
            pltpu.VMEM((tokens, D), LOW),
        ],
        cost_estimate=cost(10 * tokens * D * cols_ff, [*rows, *grad_rows, packed], results),
        compiler_params=pltpu.CompilerParams(vmem_limit_bytes=VMEM_LIMIT),
        name="ffn_turn",
    )(*rows, *grad_rows, packed, packed)


def ffn_down(hidden, packed, unit_rows, down_rows):
    tokens, cols_ff = hidden.shape
    specs = ffn_specs(
        cols_ff, unit_rows, down_rows, packed.shape[0], lambda i: 0, lambda i: i
    )[2]
    results, part_specs = parts_of(tokens, FFN_DOWNS * BLOCK, lambda i: (0, i))
    return pl.pallas_call(
        functools.partial(ffn_down_kernel, down_rows=down_rows),
        grid=(D // BLOCK // FFN_DOWNS,),
        in_specs=[pl.BlockSpec(hidden.shape, lambda i: (0, 0)), specs[1]],
        out_specs=part_specs,
        out_shape=results,
        cost_estimate=cost(2 * tokens * D * cols_ff, [hidden], results),
        compiler_params=pltpu.CompilerParams(vmem_limit_bytes=VMEM_LIMIT),
        name="ffn_down",
    )(hidden, packed)


def ffn_weight_grads_kernel(*refs, unit_rows, down_rows):
    unit_grads_ref, hidden_ref, g_refs, out_ref, x_ref = refs[4], refs[5], refs[6:10], refs[10], refs[11]
    step, last = pl.program_id(0), pl.num_programs(0) - 1

    @pl.when(step == 0)
    def _():
        rows = refs[0].shape[0]
        for place, ref in enumerate(refs[:4]):
            x_ref[:, place * rows : (place + 1) * rows] = ref[...].T

    @pl.when(step < last)
    def _():
        for place in range(out_ref.shape[1] // unit_rows):
            grad = dot(x_ref[...], unit_grads_ref[place], NN)
            grad = grad.reshape(-1, unit_rows, BLOCK).astype(LOW)
            out_ref[:, place * unit_rows : (place + 1) * unit_rows, :] = grad

    @pl.when(step == last)
    def _():
        hidden = hidden_ref[...].T
        for place in range(out_ref.shape[1] // down_rows):
            lanes = slice(place * BLOCK, (place + 1) * BLOCK)
            right = jnp.concatenate([ref[:, lanes] for ref in g_refs], axis=0)
            grad = dot(hidden, right, NN).reshape(-1, down_rows, BLOCK).astype(LOW)
            out_ref[:, place * down_rows : (place + 1) * down_rows, :] = grad


def ffn_weight_grads(rows, unit_grads, hidden, grad_rows, groups, unit_rows, down_rows):
    tokens, cols_ff = hidden.shape
    step_rows = D // BLOCK * down_rows
    per_step = step_rows // unit_rows
    steps = unit_grads.shape[0] // per_step
    last = steps - 1
    result = jax.ShapeDtypeStruct((groups, (steps + 1) * step_rows, BLOCK), LOW)
    part_spec = pl.BlockSpec(rows[0].shape, lambda i: (0, 0))
    return pl.pallas_call(
        functools.partial(ffn_weight_grads_kernel, unit_rows=unit_rows, down_rows=down_rows),
        grid=(steps + 1,),
        in_specs=[part_spec] * 4
        + [
            pl.BlockSpec((per_step, tokens, BLOCK), lambda i: (jnp.minimum(i, last), 0, 0)),
            pl.BlockSpec(hidden.shape, lambda i: (0, 0)),
        ]
        + [part_spec] * 4,
        out_specs=pl.BlockSpec((groups, step_rows, BLOCK), lambda i: (0, i, 0)),
        out_shape=result,
        scratch_shapes=[pltpu.VMEM((D, tokens), LOW)],
        cost_estimate=cost(6 * tokens * D * cols_ff, [*rows, unit_grads, hidden, *grad_rows], [result]),
        compiler_params=pltpu.CompilerParams(vmem_limit_bytes=VMEM_LIMIT),
        name="ffn_weight_grads",
    )(*rows, unit_grads, hidden, *grad_rows)


def out_grad_kernel(left_ref, right_ref, out_ref, *, rows):
    for place in range(D // BLOCK):
        grad = dot(left_ref[...], right_ref[:, place * BLOCK : (place + 1) * BLOCK], NN)
        out_ref[:, place * rows : (place + 1) * rows, :] = grad.reshape(-1, rows, BLOCK).astype(LOW)


def out_weight_grad(left, right, rows):
    result = jax.ShapeDtypeStruct((left.shape[0] // rows, D // BLOCK * rows, BLOCK), LOW)
    return pl.pallas_call(
        functools.partial(out_grad_kernel, rows=rows),
        in_specs=in_vmem(2),
        out_specs=in_vmem(1)[0],
        out_shape=result,
        cost_estimate=cost(2 * left.size * D, [left, right], [result]),
        compiler_params=pltpu.CompilerParams(vmem_limit_bytes=VMEM_LIMIT),
        name="out_weight_grad",
    )(left, right)


def gain_column(gain_ref, layer):
    return jnp.broadcast_to(gain_ref[layer : layer + 1, :], (128, gain_ref.shape[1])).T[:, :1]


def take_qkv(room_ref, layer, quarter, weights, gain_ref):
    gain = gain_column(gain_ref, layer)
    for slot in range(QUARTER_HEADS):
        column = HD * (QUARTERS * slot + quarter)
        for which, weight_ref in enumerate(weights):
            first = (3 * slot + which) * HD
            part = weight_ref[layer, :, column : column + HD] * gain
            room_ref[:, first : first + HD] = part


def first_parts_kernel(lo_ref, *refs):
    weights, gain_ref, out_ref, room_ref = refs[:3], refs[3], refs[4], refs[5]
    for quarter in range(QUARTERS):
        take_qkv(room_ref, 0, quarter, weights, gain_ref)
        out_ref[2 * quarter + lo_ref[0]] = room_ref[...].astype(LOW)
        out_ref[2 * quarter + 1 - lo_ref[0]] = jnp.zeros(room_ref.shape, LOW)


def first_parts(lo, weights, gain):
    w_rows, width = weights[0].shape[1], 3 * QUARTER_HEADS * HD
    return pl.pallas_call(
        first_parts_kernel,
        in_specs=[pl.BlockSpec(memory_space=pltpu.SMEM)] + in_vmem(4),
        out_specs=in_vmem(1)[0],
        out_shape=jax.ShapeDtypeStruct((2 * QUARTERS, w_rows, width), LOW),
        scratch_shapes=[pltpu.VMEM((w_rows, width), jnp.float32)],
        compiler_params=pltpu.CompilerParams(vmem_limit_bytes=VMEM_LIMIT),
        name="first_parts",
    )(lo, *weights, gain)


def unit_places(d_rows, padded, planes):
    width = 2 * planes // 2 * padded
    column = lax.broadcasted_iota(jnp.int32, (1, QUARTERS * width), 1)
    quarter, rest = column // width, column % width
    group, unit = rest // padded, rest % padded
    source = d_rows * (8 * (group // 2) + 2 * quarter + group % 2) + unit
    source = jnp.where(unit < d_rows, source, -1)
    rows = lax.broadcasted_iota(jnp.int32, (4 * planes * d_rows, 1), 0)
    return jnp.where(rows == source, 1.0, 0.0).astype(LOW)


def later_parts_kernel(place_ref, *refs, d_rows, padded, planes):
    weights, gains = refs[:5], refs[5:7]
    outs, rows_ref, qkv_ref, all_ref = refs[7:11], refs[11], refs[12], refs[13]
    half, cols_ff = BLOCK // 2, 2 * planes * padded
    w_rows, width = weights[0].shape[1], cols_ff // 2
    taken = 4 * planes * d_rows
    pieces = [(layer, which, part) for layer in range(LAYERS) for which in range(2) for part in range(2)]
    for number, (layer, which, part) in enumerate(pieces):
        rows = weights[3 + which][layer, :, part * taken : (part + 1) * taken] * gain_column(gains[1], layer)
        rows_ref[number * w_rows : (number + 1) * w_rows, :] = rows
    placed = dot(rows_ref[...].astype(LOW), unit_places(d_rows, padded, planes), NN)
    for number, (layer, which, part) in enumerate(pieces):
        rows = placed[number * w_rows : (number + 1) * w_rows].astype(LOW)
        for quarter in range(QUARTERS):
            for block in range(width // half):
                first = layer * 2 * cols_ff + (part * (width // half) + block) * BLOCK + which * half
                lane = quarter * width + block * half
                all_ref[quarter, :, first : first + half] = rows[:, lane : lane + half]
    for quarter in range(QUARTERS):
        for layer in range(1, LAYERS):
            take_qkv(qkv_ref, layer, quarter, weights[:3], gains[0])
            first = LAYERS * 2 * cols_ff + (layer - 1) * qkv_ref.shape[1]
            all_ref[quarter, :, first : first + qkv_ref.shape[1]] = qkv_ref[...].astype(LOW)
    for place, out_ref in enumerate(outs):
        out_ref[...] = all_ref[place ^ place_ref[0]]


def later_parts(place, weights, gains, d_rows, planes):
    w_rows = weights[0].shape[1]
    padded = -(-d_rows // 16) * 16
    cols_ff, width = 2 * planes * padded, 3 * QUARTER_HEADS * HD
    whole = LAYERS * 2 * cols_ff + (LAYERS - 1) * width
    return pl.pallas_call(
        functools.partial(later_parts_kernel, d_rows=d_rows, padded=padded, planes=planes),
        in_specs=[pl.BlockSpec(memory_space=pltpu.SMEM)] + in_vmem(7),
        out_specs=in_vmem(4),
        out_shape=[jax.ShapeDtypeStruct((w_rows, whole), LOW)] * QUARTERS,
        scratch_shapes=[
            pltpu.VMEM((4 * LAYERS * w_rows, 4 * planes * d_rows), jnp.float32),
            pltpu.VMEM((w_rows, width), jnp.float32),
            pltpu.VMEM((QUARTERS, w_rows, whole), LOW),
        ],
        compiler_params=pltpu.CompilerParams(vmem_limit_bytes=VMEM_LIMIT),
        name="later_parts",
    )(place, *weights, *gains)


def put_qkv(came_ref, place_ref, start, outs, layer, weights, gain_ref, gain_out_ref):
    for quarter in range(QUARTERS):
        part = came_ref[place_ref[quarter], :, start : start + 3 * QUARTER_HEADS * HD]
        part = part.astype(jnp.float32)
        for slot in range(QUARTER_HEADS):
            column = HD * (QUARTERS * slot + quarter)
            for which, out_ref in enumerate(outs):
                first = (3 * slot + which) * HD
                out_ref[layer, :, column : column + HD] = part[:, first : first + HD]
    gain_grad = 0.0
    for out_ref, weight_ref in zip(outs, weights):
        grad = out_ref[layer]
        gain_grad = gain_grad + jnp.sum(grad * weight_ref[layer], axis=1, keepdims=True)
        out_ref[layer] = grad * gain_column(gain_ref, layer)
    gain_out_ref[layer : layer + 1, :] = jnp.broadcast_to(gain_grad, (gain_grad.shape[0], 128)).T[:1]


def put_units(came_ref, place_ref, start, outs, layer, weights, gain_ref, gain_out_ref, d_rows, padded, planes):
    half = BLOCK // 2
    for quarter in range(QUARTERS):
        part = came_ref[place_ref[quarter], :, start : start + 4 * planes * padded]
        part = part.astype(jnp.float32)
        for plane in range(planes):
            for core in range(2):
                column = d_rows * (8 * plane + 2 * quarter + core)
                unit, end = (2 * plane + core) * padded, (2 * plane + core) * padded + d_rows
                while unit < end:
                    stop = min(end, (unit // half + 1) * half)
                    for which, out_ref in enumerate(outs):
                        first = unit // half * BLOCK + which * half + unit % half
                        out_ref[layer, :, column : column + stop - unit] = part[
                            :, first : first + stop - unit
                        ]
                    column, unit = column + stop - unit, stop
    gain_grad = 0.0
    for out_ref, weight_ref in zip(outs, weights):
        grad = out_ref[layer]
        gain_grad = gain_grad + jnp.sum(grad * weight_ref[layer], axis=1, keepdims=True)
        out_ref[layer] = grad * gain_column(gain_ref, layer)
    gain_out_ref[layer : layer + 1, :] = jnp.broadcast_to(gain_grad, (gain_grad.shape[0], 128)).T[:1]


def finish_kernel(place_ref, *refs, unit_end, w_rows, d_rows, padded, planes, with_out):
    out_lanes = slice(3 * QUARTER_HEADS * HD, 3 * QUARTER_HEADS * HD + BLOCK)
    came_ref, *sums = refs[: 1 + LAYERS]
    out_sums, refs = refs[1 + LAYERS : 2 * LAYERS], refs[2 * LAYERS :]
    weights, gains, outs = refs[:5], refs[5:7], refs[7:]
    units_width = 4 * planes * padded
    for layer in range(LAYERS):
        put_units(
            came_ref, place_ref, layer * units_width, outs[4:6], layer, weights[3:], gains[1],
            outs[8], d_rows, padded, planes,
        )
        if layer > 0:
            start = LAYERS * units_width + (layer - 1) * 3 * QUARTER_HEADS * HD
            put_qkv(came_ref, place_ref, start, outs[:3], layer, weights[:3], gains[0], outs[7])
        for block in range(D // BLOCK):
            lanes = slice(block * BLOCK, (block + 1) * BLOCK)
            rows = sums[layer][unit_end + block * padded : unit_end + (block + 1) * padded, :]
            outs[6][layer, :, lanes] = rows.astype(jnp.float32)[:d_rows]
            if with_out and layer > 0:
                rows = out_sums[layer - 1][block * w_rows : (block + 1) * w_rows, out_lanes]
                outs[3][layer, :, lanes] = rows.astype(jnp.float32)


def finish_first_kernel(place_ref, came_ref, out_sum_ref, *refs, w_rows, with_out):
    out_lanes = slice(3 * QUARTER_HEADS * HD, 3 * QUARTER_HEADS * HD + BLOCK)
    weights, gain_ref, have, outs = refs[:3], refs[3], refs[4:9], refs[9:]
    for layer in range(1, LAYERS):
        for have_ref, out_ref in zip(have, outs):
            out_ref[layer : layer + 1] = have_ref[layer : layer + 1]
    put_qkv(came_ref, place_ref, 0, outs[:3], 0, weights, gain_ref, outs[3])
    if with_out:
        for block in range(D // BLOCK):
            rows = out_sum_ref[block * w_rows : (block + 1) * w_rows, out_lanes]
            outs[4][0, :, block * BLOCK : (block + 1) * BLOCK] = rows.astype(jnp.float32)


def finish_gradients(
    place, came, sums, out_sums, weights, gains, d_shape, unit_end, planes, with_out
):
    layers, w_rows, unused = weights[0].shape
    d_rows = d_shape[1]
    padded = -(-d_rows // 16) * 16
    shapes = [weights[0].shape] * 4 + [weights[3].shape] * 2 + [d_shape] + [(layers, w_rows)] * 2
    return pl.pallas_call(
        functools.partial(
            finish_kernel, unit_end=unit_end, w_rows=w_rows, d_rows=d_rows, padded=padded, planes=planes,
            with_out=with_out,
        ),
        in_specs=[pl.BlockSpec(memory_space=pltpu.SMEM)] + in_vmem(7 + 2 * LAYERS),
        out_specs=in_vmem(9),
        out_shape=[jax.ShapeDtypeStruct(shape, jnp.float32) for shape in shapes],
        compiler_params=pltpu.CompilerParams(vmem_limit_bytes=VMEM_LIMIT),
        name="finish_gradients",
    )(place, came, *sums, *out_sums, *weights, *gains)


def finish_first(place, came, out_sum, weights, gain, grads, with_out):
    return pl.pallas_call(
        functools.partial(finish_first_kernel, w_rows=weights[0].shape[1], with_out=with_out),
        in_specs=[pl.BlockSpec(memory_space=pltpu.SMEM)] + in_vmem(11),
        out_specs=in_vmem(5),
        out_shape=[jax.ShapeDtypeStruct(member.shape, jnp.float32) for member in grads],
        compiler_params=pltpu.CompilerParams(vmem_limit_bytes=VMEM_LIMIT),
        name="finish_first",
    )(place, came, out_sum, *weights, gain, *grads)


def on_device(
    tokens,
    w_query,
    w_key,
    w_value,
    w_out,
    w_gate,
    w_up,
    w_down,
    gain_attn,
    gain_ffn,
    variate_bias,
    doc_starts,
    variate_ids,
    time_ids,
    cotangent,
):
    seq = lax.axis_size("seq")
    planes = seq // 2
    spread = planes // QUARTER_HEADS
    tiles = planes // spread
    tok_rows = tokens.shape[0]
    cols = 4 * tok_rows
    all_rows = variate_ids.shape[0]
    w_rows = w_query.shape[1]
    d_rows = w_down.shape[1]
    padded = -(-d_rows // 16) * 16
    quarter_ff = 2 * planes * padded
    quarter_width = QUARTER_HEADS * HD
    split_heads = 2 * w_rows == HD
    here_seq, here_head = lax.axis_index("seq"), lax.axis_index("head")
    here_plane, here_lo = here_seq // 2, here_seq % 2
    here_y, here_core = here_head // 2, here_head % 2
    my_quarter = 2 * here_lo + here_y
    my_head = QUARTERS * (here_plane // spread) + my_quarter
    first_tile = (here_plane % spread) * tiles
    devices = [
        (plane, lo, y, core)
        for plane in range(planes)
        for lo in range(2)
        for y in range(2)
        for core in range(2)
    ]

    def place_of(plane, lo, y, core):
        return 8 * plane + 4 * lo + 2 * y + core

    row_groups = [
        [place_of(plane, lo, y, core) for plane in range(planes) for core in range(2)]
        for lo in range(2)
        for y in range(2)
    ]
    plane_groups = [[2 * plane + lo for plane in range(planes)] for lo in range(2)]
    x_swap = [(place, place ^ 1) for place in range(seq)]
    corner_swap = [
        (place_of(plane, lo, y, core), place_of(plane, 1 - lo, 1 - y, core))
        for plane, lo, y, core in devices
    ]

    def neighbours(across_y, across_x, across_both):
        return (
            lax.ppermute(across_y, "head", Y_SWAP),
            lax.ppermute(across_x, "seq", x_swap),
            lax.ppermute(across_both, BOTH, corner_swap),
        )

    def beside_parts(value):
        return [value, *neighbours(value, value, value)]

    def beside(value):
        return jnp.concatenate(beside_parts(value), axis=0)

    def fold(own, *others):
        return own + sum(part.astype(jnp.float32) for part in neighbours(*others))

    def four_parts(partial):
        low = partial[tok_rows:].astype(LOW).reshape(3, tok_rows, -1)
        return partial[:tok_rows], low[0], low[1], low[2]

    def flip(pair, bit):
        return jnp.where(bit == 0, pair[0], pair[1]), jnp.where(bit == 0, pair[1], pair[0])

    def xor_order(grid, high, low):
        rows = [flip(row, low) for row in grid]
        first, second = zip(*[flip(column, high) for column in zip(*rows)])
        return [list(first), list(second)]

    def cross_rows(parts):
        came = [[None, None], [None, None]]
        for high in range(2):
            for low in range(2):
                hops = [
                    (place_of(plane, lo, y, core), place_of(plane, y ^ high, core ^ low, lo))
                    for plane, lo, y, core in devices
                ]
                came[high][low] = lax.ppermute(parts[2 * high + low], BOTH, hops)
        came = xor_order(came, here_lo, here_y)
        return jnp.concatenate([*came[0], *came[1]], axis=0)

    def cross_back(rows):
        parts = [rows[place * w_rows : (place + 1) * w_rows] for place in range(4)]
        grid = xor_order([parts[:2], parts[2:]], here_lo, here_y)
        came = [[None, None], [None, None]]
        for high in range(2):
            for low in range(2):
                hops = [
                    (place_of(plane, lo, y, core), place_of(plane, core, lo ^ high, y ^ low))
                    for plane, lo, y, core in devices
                ]
                came[high][low] = lax.ppermute(grid[high][low], BOTH, hops)
        return jnp.stack([*came[0], *came[1]])

    device_groups = [[8 * plane + place for place in range(8)] for plane in range(planes)]

    def plane_exchange(value):
        return lax.all_to_all(
            value, BOTH, split_axis=0, concat_axis=0, tiled=True, axis_index_groups=device_groups
        )

    def cross_rows_at_once(sent):
        came = plane_exchange(sent)
        came = jnp.where(here_core == 0, came[:4], came[4:])
        return came.reshape(-1, sent.shape[-1])

    def cross_back_at_once(rows):
        parts = rows.reshape(4, w_rows, -1)
        zeros = jnp.zeros_like(parts)
        sent = [jnp.where(here_core == lo, parts, zeros) for lo in range(2)]
        return plane_exchange(jnp.concatenate(sent, axis=0))

    def gather(part):
        return lax.all_gather(part, BOTH, axis=0, tiled=True, axis_index_groups=row_groups)

    def blocks_of(matrix):
        rows, n = matrix.shape
        return matrix.reshape(rows, n // BLOCK, BLOCK).transpose(1, 0, 2).reshape(-1, BLOCK)

    def from_blocks(packed, rows):
        groups, count = packed.shape[0], packed.shape[1] // rows
        parts = packed.reshape(groups, count, rows, BLOCK).transpose(0, 2, 1, 3)
        return parts.reshape(groups * rows, count * BLOCK)

    def scatter(packed):
        part = lax.psum_scatter(
            packed.reshape(-1, packed.shape[-1]),
            BOTH,
            scatter_dimension=0,
            tiled=True,
            axis_index_groups=row_groups,
        )
        return part

    def whole_out_back(grad):
        spaced = lax.dynamic_update_slice_in_dim(
            jnp.zeros((QUARTER_HEADS, QUARTERS, HD, D), LOW),
            grad.astype(LOW).reshape(QUARTER_HEADS, 1, HD, D),
            my_quarter,
            1,
        )
        return lax.psum_scatter(spaced.reshape(D, D), BOTH, scatter_dimension=0, tiled=True)

    def normalize(values):
        inverse = lax.rsqrt(jnp.mean(values * values, axis=-1, keepdims=True) + NORM_EPS)
        return values * inverse, inverse

    def normalize_back(scaled, inverse, inner):
        return inverse * (inner - scaled * jnp.mean(inner * scaled, axis=-1, keepdims=True))

    def attention_part(layer, qkv_rows):
        blocks = blocks_of(w_out[layer].astype(LOW))
        return jnp.concatenate([qkv_rows, blocks], axis=1)

    def attention_matrices(part):
        whole = gather(part)
        blocks = whole[:, 3 * quarter_width :].reshape(2 * planes, -1, BLOCK)
        return whole[:, : 3 * quarter_width], from_blocks(blocks, w_rows)

    gains = (gain_attn, gain_ffn)
    first_sent = first_parts(
        jnp.reshape(here_lo, (1,)).astype(jnp.int32), (w_query, w_key, w_value), gains[0]
    )
    first_part = attention_part(0, cross_rows_at_once(first_sent))
    first_part, time_ids, w_gate, w_up = lax.optimization_barrier((first_part, time_ids, w_gate, w_up))
    attention_weights, out_weights = [attention_matrices(first_part)], []
    start_scaled, start_inverse = normalize(tokens)
    start_normed = beside(start_scaled.astype(LOW))

    group_rows = 4 * w_rows
    unit_end = 2 * quarter_ff // BLOCK * group_rows
    ffn_end = unit_end + D // BLOCK * padded

    def ffn_part(layer, units_rows):
        down_part = jnp.pad(w_down[layer].astype(LOW), ((0, padded - d_rows), (0, 0)))
        return jnp.concatenate([blocks_of(units_rows), blocks_of(down_part)], axis=0)

    later_sent = later_parts(
        jnp.reshape(2 * here_y + here_core, (1,)).astype(jnp.int32),
        (w_query, w_key, w_value, w_gate, w_up), gains, d_rows, planes,
    )
    later_widths = [2 * quarter_ff] * LAYERS + [3 * quarter_width] * (LAYERS - 1)

    def cut(whole):
        parts, start = [], 0
        for width in later_widths:
            parts.append(whole[..., start : start + width])
            start += width
        return parts

    ffn_weights = []

    def placed_ids(ids):
        ids = ids.reshape(planes, 2, 2, 2, tok_rows)
        ids = jnp.where(here_lo == 0, ids, ids[:, ::-1])
        ids = jnp.where(here_y == 0, ids, ids[:, :, ::-1])
        ids = jnp.where(here_core == 0, ids, ids[:, :, :, ::-1])
        return ids.transpose(3, 0, 1, 2, 4).reshape(2 * planes, cols)

    def my_tiles(value):
        if spread == 1:
            return value
        return lax.dynamic_slice_in_dim(value, first_tile, tiles, 0)

    positions = jnp.arange(all_rows, dtype=jnp.int32)
    doc_ids = jnp.sum((doc_starts[None, :] <= positions[:, None]).astype(jnp.int32), axis=1)
    docs = placed_ids(doc_ids)
    variates = placed_ids(variate_ids)
    q_docs, q_variates = my_tiles(docs[:planes]), my_tiles(variates[:planes])
    extra_row = jnp.arange(HD, dtype=jnp.int32)[None, :, None]

    def one_hot(ids):
        return ids[:, None, :] == extra_row % VARIATES

    def is_doc(ids):
        return ids[:, None, :] == extra_row - 24

    doc_row = (extra_row >= 24) & (extra_row < 32)
    ones_row = (extra_row == 16) | (extra_row == 17) | ((extra_row >= 32) & (extra_row < 35))
    k_hits = one_hot(variates) & (extra_row < 16) | is_doc(docs) & doc_row | ones_row
    k_aug = jnp.where(k_hits, 1.0, 0.0).astype(LOW)

    def query_extra(layer):
        same, other = variate_bias[layer, 0, my_head], variate_bias[layer, 1, my_head]
        gap = same - other
        gap_lead, other_lead = (part.astype(LOW).astype(jnp.float32) for part in (gap, other))
        gap_part = jnp.where(extra_row < VARIATES, gap_lead, gap - gap_lead)
        other_part = jnp.where(extra_row == 16, other_lead, other - other_lead)
        spread_gap = jnp.where(one_hot(q_variates), gap_part, 0.0)
        shut = jnp.where(doc_row & ~is_doc(q_docs), FLOOR_SCORE, 0.0)
        tail = jnp.where(extra_row < 18, other_part, shut)
        return jnp.where(extra_row < 16, spread_gap, tail).astype(LOW)

    q_augs = [query_extra(layer) for layer in range(LAYERS)]
    q_onehots = (q_variates[:, None, :] == jnp.arange(VARIATES, dtype=jnp.int32)[:, None]).astype(
        jnp.float32
    )

    half_dim = HD // 2
    frequency = jnp.exp(jnp.arange(half_dim).astype(jnp.float32) * (-2.0 * math.log(10000.0) / HD))
    times = beside(time_ids.astype(jnp.float32))
    angles = frequency[:, None] * times[None, :]
    cosines, sines = jnp.cos(angles), jnp.sin(angles)
    start_normed, later_sent, k_aug, cosines, sines, *q_augs = lax.optimization_barrier(
        (start_normed, later_sent, k_aug, cosines, sines, *q_augs)
    )

    def rotate(values, sines):
        former, latter = values[:, :half_dim], values[:, half_dim:]
        return jnp.concatenate(
            [former * cosines - latter * sines, latter * cosines + former * sines], axis=1
        )

    def to_heads(value):
        if spread > 1:
            value = jnp.repeat(value, spread, axis=0)
        return lax.all_to_all(
            value, "seq", split_axis=0, concat_axis=0, tiled=True, axis_index_groups=plane_groups
        )

    def all_blocks(value):
        if spread == 1:
            return value
        zeros = jnp.zeros((planes,) + value.shape[1:], value.dtype)
        return lax.dynamic_update_slice_in_dim(zeros, value, first_tile, 0)

    def over_spread(value):
        if spread == 1:
            return value
        value = value.reshape((QUARTER_HEADS, spread) + value.shape[1:])
        return jnp.sum(value.astype(jnp.float32), axis=1).astype(LOW)

    def from_heads(value):
        return over_spread(
            lax.all_to_all(
                value, "seq", split_axis=0, concat_axis=0, tiled=True, axis_index_groups=plane_groups
            )
        )

    chip_groups = [
        [place_of(plane, lo, y, core) for plane in range(planes) for lo in range(2) for y in range(2)]
        for core in range(2)
    ]

    def over_chips(value):
        shape = value.shape
        value = value.reshape(-1, *shape[2:])
        value = lax.all_to_all(
            value, BOTH, split_axis=0, concat_axis=0, tiled=True, axis_index_groups=chip_groups
        )
        return value.reshape(shape)

    chip_flips = jnp.reshape(my_quarter, (1,)).astype(jnp.int32)

    def plane_order(value):
        grid = [[value[:, 2 * lo + y] for y in range(2)] for lo in range(2)]
        grid = xor_order(grid, here_lo, here_y)
        return jnp.stack([*grid[0], *grid[1]])

    def chip_order(value):
        grid = xor_order([[value[0], value[1]], [value[2], value[3]]], here_lo, here_y)
        return jnp.stack([*grid[0], *grid[1]], axis=1)

    def sum_everywhere(value):
        for axis, size in (("head", 4), ("seq", seq)):
            hop = 1
            while hop < size:
                swap = [(place, place ^ hop) for place in range(size)]
                value = value + lax.ppermute(value, axis, swap)
                hop *= 2
        return value

    def share_for_out(middle_low, attended):
        pieces = attended.reshape(4, quarter_width, tok_rows)
        cuts = quarter_width // tok_rows

        def joined(piece):
            parts = [piece[cut * tok_rows : (cut + 1) * tok_rows] for cut in range(cuts)]
            return jnp.concatenate([middle_low, *parts], axis=1)

        came = neighbours(*(joined(piece) for piece in pieces[1:]))
        tokens_low = jnp.concatenate([middle_low, *(part[:, :D] for part in came)], axis=0)

        def results(part):
            return jnp.concatenate(
                [part[:, D + cut * tok_rows : D + (cut + 1) * tok_rows] for cut in range(cuts)], axis=0
            )

        return tokens_low, jnp.concatenate([pieces[0], *(results(part) for part in came)], axis=1)

    stream = tokens
    saved = []
    for layer in range(LAYERS):
        qkv_matrix, out_quarter = attention_weights[layer]
        if layer == 0:
            scaled_one, inverse_one, normed = start_scaled, start_inverse, start_normed
        else:
            scaled_one, inverse_one = normalize(stream)
            normed = beside(scaled_one.astype(LOW))
        projected = dot(qkv_matrix, normed, TT).reshape(QUARTER_HEADS, 3 * HD, cols)
        query = rotate(projected[:, :HD], sines) * (1.0 / math.sqrt(HD))
        key = rotate(projected[:, HD : 2 * HD], sines)
        sent = jnp.concatenate([query, key, projected[:, 2 * HD :]], axis=1).astype(LOW)
        if layer == 0:
            later_weights = cross_rows(later_sent)
            sent, cotangent = lax.optimization_barrier((sent, cotangent))
            last_grad_parts = beside_parts(cotangent.astype(LOW))
        own = to_heads(sent)
        if layer == 0:
            own, last_grad_parts = lax.optimization_barrier((own, last_grad_parts))
        next_part = ffn_part(layer, cut(later_weights)[layer])
        own, next_part = lax.optimization_barrier((own, next_part))
        packed = gather(next_part).reshape(2 * planes, -1, BLOCK)
        ffn_weights.append(packed)
        if layer == 0:
            own, out_quarter = lax.optimization_barrier((own, out_quarter))
        halves = out_quarter.reshape(2, quarter_width // 2, D)
        half = jnp.where(here_core == 0, halves[0], halves[1])
        out_parts = neighbours(half, half, half)
        sib = lax.ppermute(own[:, HD:], "head", CORE_SWAP)
        queries = my_tiles(own)
        q_aug = q_augs[layer]
        out, lse = attention_forward(chip_flips, queries, q_aug, own, sib, k_aug)
        out, *out_parts = lax.optimization_barrier((out, *out_parts))
        mine = jnp.stack(out_parts)
        other = lax.ppermute(mine, "head", CORE_SWAP)
        pairs = jnp.where(
            here_core == 0, jnp.stack([mine, other], axis=1), jnp.stack([other, mine], axis=1)
        )
        out_matrix = jnp.concatenate([out_quarter, pairs.reshape(3 * quarter_width, D)], axis=0)
        out_weights.append(out_matrix)
        attended = over_spread(over_chips(all_blocks(out))).reshape(QUARTER_HEADS, 4, HD, tok_rows)
        attended = plane_order(attended).reshape(D, tok_rows)
        attended, out_matrix = lax.optimization_barrier((attended, out_matrix))
        middle = stream + dot(attended, out_matrix, TN)
        scaled_two, inverse_two = normalize(middle)
        normed_parts = beside_parts(scaled_two.astype(LOW))
        if layer < LAYERS - 1:
            next_part = attention_part(layer + 1, cut(later_weights)[LAYERS + layer])
            normed_parts, next_part = lax.optimization_barrier((normed_parts, next_part))
            attention_weights.append(attention_matrices(next_part))
        if layer < LAYERS - 1:
            both, hidden, *parts = ffn_forward(normed_parts, packed, quarter_ff, group_rows, padded)
        else:
            both, hidden = None, None
        saved.append(
            (
                scaled_one, inverse_one, normed, own, sib, queries, q_aug, out, lse, attended,
                scaled_two, inverse_two, normed_parts, both, hidden,
            )
        )
        if layer < LAYERS - 1:
            stream = middle + fold(*parts)
        else:
            last_middle = middle

    upstream = cotangent
    whole_grads, ffn_sums, qkv_sums = [None] * LAYERS, [None] * LAYERS, [None] * LAYERS
    bias_parts = [None] * LAYERS
    for layer in reversed(range(LAYERS)):
        qkv_matrix, unused = attention_weights[layer]
        out_matrix, packed = out_weights[layer], ffn_weights[layer]
        (
            scaled_one, inverse_one, normed, own, sib, queries, q_aug, out, lse, attended,
            scaled_two, inverse_two, normed_parts, both, hidden,
        ) = saved[layer]
        if layer < LAYERS - 1:
            upstream_parts = beside_parts(upstream.astype(LOW))
        else:
            upstream_parts = last_grad_parts
        if layer < LAYERS - 1:
            grad_units, *parts = ffn_backward(
                upstream_parts, packed, both, quarter_ff, group_rows, padded
            )
        else:
            grad_units, hidden, *parts = ffn_turn(
                normed_parts, upstream_parts, packed, quarter_ff, group_rows, padded
            )
        inner = fold(*parts)
        buffer = ffn_weight_grads(
            normed_parts, grad_units, hidden, upstream_parts, 2 * planes, group_rows, padded
        )
        inner, buffer = lax.optimization_barrier((inner, buffer))
        if layer < LAYERS - 1:
            buffer, qkv_sums[layer + 1] = lax.optimization_barrier((buffer, qkv_sums[layer + 1]))
        ffn_sums[layer] = scatter(buffer)
        grad_middle = upstream + normalize_back(scaled_two, inverse_two, inner)
        middle_low = grad_middle.astype(LOW)
        grad_attended = dot(out_matrix, middle_low, NT).astype(LOW)
        grad_attended = chip_order(grad_attended.reshape(4, QUARTER_HEADS, HD, tok_rows))
        if spread > 1:
            grad_attended = jnp.repeat(grad_attended, spread, axis=0)
        if layer == LAYERS - 1:
            grad_attended, last_hidden = lax.optimization_barrier((grad_attended, hidden))
            last_parts = ffn_down(last_hidden, packed, group_rows, padded)
        out_grad = my_tiles(over_chips(grad_attended))
        if layer == LAYERS - 1:
            out_grad, *last_parts = lax.optimization_barrier((out_grad, *last_parts))
        out_grad, middle_low, attended = lax.optimization_barrier((out_grad, middle_low, attended))
        middle_low, attended = share_for_out(middle_low, attended)
        grad_q, grad_kv = attention_backward(
            chip_flips, queries, q_aug, lse, out, out_grad, own, sib, k_aug
        )
        grad_kv, middle_low, attended = lax.optimization_barrier((grad_kv, middle_low, attended))
        if not split_heads:
            whole_grads[layer] = whole_out_back(dot(attended, middle_low, NN))
        else:
            out_blocks = out_weight_grad(attended, middle_low, w_rows)
        same_grad = jnp.sum(grad_q[:, HD : HD + VARIATES] * q_onehots)
        all_grad = jnp.sum(grad_q[:, HD + 16])
        crossed = lax.ppermute(grad_kv[planes:], "head", CORE_SWAP)
        grad_kv = (grad_kv[:planes].astype(jnp.float32) + crossed.astype(jnp.float32)).astype(LOW)
        grad_q = (grad_q[:, :HD] * (1.0 / math.sqrt(HD))).astype(LOW)
        if layer == LAYERS - 1:
            grad_kv, *last_parts = lax.optimization_barrier((grad_kv, *last_parts))
            stream = last_middle + fold(*last_parts)
        grad_heads = from_heads(jnp.concatenate([all_blocks(grad_q), grad_kv], axis=1))
        bias_parts[layer] = jnp.stack([same_grad, all_grad - same_grad])
        if layer == LAYERS - 1:
            grad_heads, stream, bias_parts[layer] = lax.optimization_barrier(
                (grad_heads, stream, bias_parts[layer])
            )
        if layer == 0:
            later_sums = [from_blocks(member[None, :unit_end], group_rows) for member in ffn_sums]
            later_sums += [member[:, : 3 * quarter_width] for member in qkv_sums[1:]]
            came = cross_back(jnp.concatenate(later_sums, axis=1))
            grad_heads, came = lax.optimization_barrier((grad_heads, came))
        grad_heads = jnp.concatenate(
            [
                rotate(grad_heads[:, :HD].astype(jnp.float32), -sines).astype(LOW),
                rotate(grad_heads[:, HD : 2 * HD].astype(jnp.float32), -sines).astype(LOW),
                grad_heads[:, 2 * HD :],
            ],
            axis=1,
        ).reshape(3 * quarter_width, cols)
        partial = dot(grad_heads, qkv_matrix, TT)
        qkv_grad = dot(normed, grad_heads, TT).astype(LOW)
        if split_heads:
            qkv_grad = jnp.concatenate([qkv_grad, out_blocks.reshape(-1, BLOCK)], axis=1)
        if layer > 0:
            inner = fold(*four_parts(partial))
            inner, qkv_grad = lax.optimization_barrier((inner, qkv_grad))
        qkv_grad, ffn_sums[layer] = lax.optimization_barrier((qkv_grad, ffn_sums[layer]))
        qkv_sums[layer] = scatter(qkv_grad)
        if layer > 0:
            upstream = grad_middle + normalize_back(scaled_one, inverse_one, inner)

    later_sums = [from_blocks(member[None, :unit_end], group_rows) for member in ffn_sums]
    bias_local = lax.dynamic_update_slice(
        jnp.zeros((LAYERS, 2, HEADS), jnp.float32), jnp.stack(bias_parts)[:, :, None], (0, 0, my_head)
    )
    bias_total = sum_everywhere(bias_local)
    quarters = jnp.arange(QUARTERS, dtype=jnp.int32)
    weights = (w_query, w_key, w_value, w_gate, w_up)
    *grads, gain_one, gain_two = finish_gradients(
        quarters ^ (2 * here_y + here_core), came, ffn_sums,
        qkv_sums[1:], weights, gains, w_down.shape, unit_end, planes, split_heads,
    )
    qkv_sums[0], gain_two, parts, grads = lax.optimization_barrier(
        (qkv_sums[0], gain_two, four_parts(partial), grads)
    )
    inner = fold(*parts)
    upstream = grad_middle + normalize_back(scaled_one, inverse_one, inner)
    *grads[:3], gain_one, grads[3] = finish_first(
        2 * quarters + here_lo, cross_back_at_once(qkv_sums[0][:, : 3 * quarter_width]), qkv_sums[0], weights[:3], gains[0],
        [*grads[:3], gain_one, grads[3]], split_heads,
    )
    if not split_heads:
        grads[3] = jnp.stack(whole_grads).astype(jnp.float32)
    return (stream, upstream, *grads, gain_one, gain_two, bias_total)


def solution(mesh):
    rows = P(BOTH, None)
    middle = P(None, BOTH, None)
    gains = P(None, BOTH)
    return jax.shard_map(
        on_device,
        mesh=mesh,
        in_specs=(rows,) + (middle,) * 7 + (gains,) * 2 + (P(),) * 3 + (P(BOTH), rows),
        out_specs=(rows, rows) + (middle,) * 7 + (gains,) * 2 + (P(),),
        check_vma=False,
    )
```

```python
import functools
import math

import jax
import jax.numpy as jnp
from jax import lax
from jax.experimental import pallas as pl
from jax.experimental.pallas import tpu as pltpu
from jax.sharding import PartitionSpec as P

D = 1024
HEADS = 16
HD = 64
LAYERS = 2
VARIATES = 8
BLOCK = 256

NORM_EPS = 1e-05
FLOOR_SCORE = -1e30
LOW = jnp.bfloat16
BOTH = ("seq", "head")

QUARTERS = 4
QUARTER_HEADS = HEADS // QUARTERS
Y_SWAP = [(place, place ^ 2) for place in range(4)]
CORE_SWAP = [(place, place ^ 1) for place in range(4)]

NN = (((1,), (0,)), ((), ()))
NT = (((1,), (1,)), ((), ()))
TN = (((0,), (0,)), ((), ()))
TT = (((0,), (1,)), ((), ()))
VMEM_LIMIT = 56 * 1024 * 1024


def in_vmem(count):
    return [pl.BlockSpec(memory_space=pltpu.VMEM)] * count


def cost(flops, operands, results, transcendentals=0):
    moved = sum(member.size * member.dtype.itemsize for member in [*operands, *results])
    return pl.CostEstimate(flops=flops, bytes_accessed=moved, transcendentals=transcendentals)


def dot(left, right, dims):
    return lax.dot_general(left, right, dims, preferred_element_type=jnp.float32)


def forward_kernel(flip_ref, q_ref, q_aug_ref, own_ref, sib_ref, k_aug_ref, out_ref, lse_ref):
    blocks = own_ref.shape[0]
    sources = ((own_ref, HD), (sib_ref, HD))
    spots = [(half, block) for half in range(2) for block in range(blocks)]
    cols = q_ref.shape[-1]
    q_side = jnp.concatenate([q_ref[0, :HD, :], q_aug_ref[0]], axis=0).T
    top = jnp.full((cols, 1), FLOOR_SCORE, jnp.float32)
    total = jnp.zeros((cols, 1), jnp.float32)
    acc = jnp.zeros((cols, HD), jnp.float32)

    def scores(half, block):
        ref, low_row = sources[half]
        extra = k_aug_ref[half * blocks + block]
        k_side = jnp.concatenate([ref[block, low_row : low_row + HD, :], extra], axis=0)
        return dot(q_side, k_side, NN)

    following = scores(*spots[0])
    for number, (half, block) in enumerate(spots):
        part = following
        if number + 1 < len(spots):
            following = scores(*spots[number + 1])
        fresh = jnp.maximum(top, jnp.max(part, axis=-1, keepdims=True))
        shrink = jnp.exp(top - fresh)
        prob = jnp.exp(part - fresh)
        total = total * shrink + jnp.sum(prob, axis=-1, keepdims=True)
        ref, low_row = sources[half]
        values = ref[block, low_row + HD : low_row + 2 * HD, :]
        acc = acc * shrink + dot(prob.astype(LOW), values, NT)
        top = fresh
    result = acc / total
    lse = jnp.broadcast_to(top + jnp.log(total), (cols, HD))
    both = jnp.concatenate([result, lse], axis=1).T
    piece = out_ref.shape[-1]
    for place in range(cols // piece):
        part = both[:HD, place * piece : (place + 1) * piece]
        out_ref[0, place ^ flip_ref[0]] = part.astype(LOW)
    lse_ref[0] = both[HD : HD + 8]


def split_rows(row, rows):
    one = row.astype(LOW).astype(jnp.float32)
    two = (row - one).astype(LOW).astype(jnp.float32)
    three = row - one - two
    pad = jnp.zeros((rows - 3, row.shape[-1]), jnp.float32)
    return jnp.concatenate([one, two, three, pad], axis=0).astype(LOW)


def backward_kernel(
    flip_ref, q_ref, q_aug_ref, lse_ref, out_ref, grad_ref, own_ref, sib_ref, k_aug_ref,
    dq_ref, dkv_own_ref, dkv_sib_ref, dkv_acc,
):
    step = pl.program_id(0)
    blocks = own_ref.shape[0]
    sources = ((own_ref, HD), (sib_ref, HD))
    cols, key_cols = q_ref.shape[-1], own_ref.shape[-1]

    @pl.when(step == 0)
    def _():
        dkv_acc[...] = jnp.zeros_like(dkv_acc)

    q_low = q_ref[0, :HD, :]
    places = range(grad_ref.shape[1])
    g_low = jnp.concatenate([grad_ref[0, place ^ flip_ref[0]] for place in places], axis=1)
    out = jnp.concatenate([out_ref[0, place ^ flip_ref[0]] for place in places], axis=1)
    row_dot = jnp.sum(g_low.astype(jnp.float32) * out.astype(jnp.float32), axis=0, keepdims=True)
    aug = jnp.concatenate(
        [q_aug_ref[0, :32, :], split_rows(-lse_ref[0, :1, :], 16), q_aug_ref[0, 48:, :]], axis=0
    )
    q_side = jnp.concatenate([q_low, aug], axis=0).T
    g_side = jnp.concatenate([g_low, split_rows(-row_dot, HD)], axis=0).T
    ones = jnp.concatenate(
        [jnp.ones((16, key_cols), LOW), jnp.zeros((HD - 16, key_cols), LOW)], axis=0
    )
    dq = jnp.zeros((cols, 2 * HD), jnp.float32)
    spots = [(half, block) for half in range(2) for block in range(blocks)]

    def products(half, block):
        ref, low_row = sources[half]
        k_side = jnp.concatenate(
            [ref[block, low_row : low_row + HD, :], k_aug_ref[half * blocks + block]], axis=0
        )
        v_side = jnp.concatenate([ref[block, low_row + HD : low_row + 2 * HD, :], ones], axis=0)
        return k_side, dot(q_side, k_side, NN), dot(g_side, v_side, NN)

    following = products(*spots[0])
    for spot in range(len(spots)):
        k_side, score, prob_grad = following
        if spot + 1 < len(spots):
            following = products(*spots[spot + 1])
        prob = jnp.exp(score)
        score_grad = (prob * prob_grad).astype(LOW)
        dq = dq + dot(score_grad, k_side, NT)
        dkv_acc[spot, :HD, :] += dot(q_low, score_grad, NN)
        dkv_acc[spot, HD:, :] += dot(g_low, prob.astype(LOW), NN)
    dq_ref[0] = dq.T

    @pl.when(step == pl.num_programs(0) - 1)
    def _():
        dkv_own_ref[...] = dkv_acc[:blocks].astype(LOW)
        dkv_sib_ref[...] = dkv_acc[blocks:].astype(LOW)


def whole_spec(shape):
    rank = len(shape)
    return pl.BlockSpec(shape, lambda i, flip: (0,) * rank)


def tile_spec(rows, cols):
    return pl.BlockSpec((1, rows, cols), lambda i, flip: (i, 0, 0))


def owner_spec(shape):
    return pl.BlockSpec((1, *shape[1:]), lambda i, flip: (i, 0, 0, 0))


def attention_forward(flip, queries, q_aug, own, sib, k_aug):
    tiles, unused, cols = queries.shape
    pairs = 2 * tiles * own.shape[0] * cols * cols
    out_shape = (tiles, 4, HD, cols // 4)
    results = [
        jax.ShapeDtypeStruct(out_shape, LOW),
        jax.ShapeDtypeStruct((tiles, 8, cols), jnp.float32),
    ]
    return pl.pallas_call(
        forward_kernel,
        grid_spec=pltpu.PrefetchScalarGridSpec(
            num_scalar_prefetch=1,
            grid=(tiles,),
            in_specs=[tile_spec(3 * HD, cols), tile_spec(HD, cols)]
            + [whole_spec(member.shape) for member in (own, sib, k_aug)],
            out_specs=[owner_spec(out_shape), tile_spec(8, cols)],
        ),
        out_shape=results,
        cost_estimate=cost(16 * HD * pairs, [queries, own, sib], results, pairs),
        compiler_params=pltpu.CompilerParams(vmem_limit_bytes=VMEM_LIMIT),
        name="attention_forward",
    )(flip, queries, q_aug, own, sib, k_aug)


def attention_backward(flip, queries, q_aug, lse, out, grad, own, sib, k_aug):
    tiles, unused, cols = queries.shape
    dkv_shape, half_shape = (2 * own.shape[0], 2 * HD, cols), (own.shape[0], 2 * HD, cols)
    pairs = 2 * tiles * own.shape[0] * cols * cols
    results = [
        jax.ShapeDtypeStruct((tiles, 2 * HD, cols), jnp.float32),
        *[jax.ShapeDtypeStruct(half_shape, LOW)] * 2,
    ]
    return pl.pallas_call(
        backward_kernel,
        grid_spec=pltpu.PrefetchScalarGridSpec(
            num_scalar_prefetch=1,
            grid=(tiles,),
            in_specs=[tile_spec(3 * HD, cols), tile_spec(HD, cols), tile_spec(8, cols)]
            + [owner_spec(out.shape)] * 2
            + [whole_spec(member.shape) for member in (own, sib, k_aug)],
            out_specs=[tile_spec(2 * HD, cols)] + [whole_spec(half_shape)] * 2,
            scratch_shapes=[pltpu.VMEM(dkv_shape, jnp.float32)],
        ),
        out_shape=results,
        cost_estimate=cost(32 * HD * pairs, [queries, own, sib], results, pairs),
        compiler_params=pltpu.CompilerParams(vmem_limit_bytes=VMEM_LIMIT),
        name="attention_backward",
    )(flip, queries, q_aug, lse, out, grad, own, sib, k_aug)


def silu_parts(gate):
    sigmoid = 1.0 / (1.0 + jnp.exp(-gate))
    return sigmoid, gate * sigmoid


def put_parts(values, lanes, own_ref, *low_refs):
    rows = own_ref.shape[0]
    own_ref[:, lanes] = values[:rows]
    for place, low_ref in enumerate(low_refs):
        low_ref[:, lanes] = values[(place + 1) * rows : (place + 2) * rows].astype(LOW)


def parts_of(tokens, lanes, index):
    shape = (tokens // 4, D)
    types = [jnp.float32, LOW, LOW, LOW]
    return (
        [jax.ShapeDtypeStruct(shape, kind) for kind in types],
        [pl.BlockSpec((tokens // 4, lanes), index) for unused in types],
    )


def join_rows(x_ref, refs):
    @pl.when(pl.program_id(0) == 0)
    def _():
        rows = refs[0].shape[0]
        for place, ref in enumerate(refs):
            x_ref[place * rows : (place + 1) * rows, :] = ref[...]


def ffn_forward_kernel(*refs, unit_rows, down_rows, unit_steps):
    unit_ref, down_ref, both_ref, hidden_ref = refs[4:8]
    out_refs, x_ref = refs[8:12], refs[12]
    join_rows(x_ref, refs[:4])
    step = pl.program_id(0)
    half = BLOCK // 2

    @pl.when(step < unit_steps)
    def _():
        count = unit_ref.shape[1] // unit_rows
        for place in range(count):
            matrix = unit_ref[:, place * unit_rows : (place + 1) * unit_rows, :].reshape(-1, BLOCK)
            both = dot(x_ref[...], matrix, NN)
            both_ref[place] = both.astype(both_ref.dtype)
            hidden = silu_parts(both[:, :half])[1] * both[:, half:]
            spot = step * count + place
            hidden_ref[:, pl.ds(pl.multiple_of(spot * half, half), half)] = hidden.astype(LOW)

    @pl.when(step >= unit_steps)
    def _():
        for place in range(down_ref.shape[1] // down_rows):
            matrix = down_ref[:, place * down_rows : (place + 1) * down_rows, :].reshape(-1, BLOCK)
            lanes = slice(place * BLOCK, (place + 1) * BLOCK)
            put_parts(dot(hidden_ref[...], matrix, NN), lanes, *out_refs)


def ffn_backward_kernel(*refs, unit_rows, down_rows, down_steps):
    unit_ref, down_ref, both_ref, grads_ref = refs[4:8]
    part_refs, inner_ref, hidden_grad, g_ref = refs[8:12], refs[12], refs[13], refs[14]
    join_rows(g_ref, refs[:4])
    step = pl.program_id(0)
    half = BLOCK // 2

    @pl.when(step < down_steps)
    def _():
        total = 0.0
        for place in range(down_ref.shape[1] // down_rows):
            matrix = down_ref[:, place * down_rows : (place + 1) * down_rows, :].reshape(-1, BLOCK)
            lanes = pl.ds(pl.multiple_of((step * FFN_DOWNS + place) * BLOCK, BLOCK), BLOCK)
            total = total + dot(g_ref[:, lanes], matrix, NT)

        @pl.when(step == 0)
        def _():
            hidden_grad[...] = total

        @pl.when(step > 0)
        def _():
            hidden_grad[...] += total

    @pl.when(step >= down_steps)
    def _():
        count = unit_ref.shape[1] // unit_rows
        total = 0.0
        for place in range(count):
            matrix = unit_ref[:, place * unit_rows : (place + 1) * unit_rows, :].reshape(-1, BLOCK)
            spot = (step - down_steps) * count + place
            gate = both_ref[place, :, :half].astype(jnp.float32)
            upward = both_ref[place, :, half:].astype(jnp.float32)
            above = hidden_grad[:, pl.ds(pl.multiple_of(spot * half, half), half)]
            sigmoid, silu = silu_parts(gate)
            grad_gate = above * upward * (sigmoid * (1.0 + gate * (1.0 - sigmoid)))
            grads = jnp.concatenate([grad_gate, above * silu], axis=1).astype(LOW)
            grads_ref[place] = grads
            total = total + dot(grads, matrix, NT)

        @pl.when(step == down_steps)
        def _():
            inner_ref[...] = total

        @pl.when(step > down_steps)
        def _():
            inner_ref[...] += total

    @pl.when(step == pl.num_programs(0) - 1)
    def _():
        put_parts(inner_ref[...], slice(0, D), *part_refs)


def ffn_turn_kernel(*refs, unit_rows, down_rows, down_steps):
    unit_ref, down_ref, grads_ref, hidden_ref = refs[8:12]
    part_refs, inner_ref, hidden_grad, x_ref, g_ref = refs[12:16], *refs[16:20]
    join_rows(x_ref, refs[:4])
    join_rows(g_ref, refs[4:8])
    step = pl.program_id(0)
    half = BLOCK // 2

    @pl.when(step < down_steps)
    def _():
        total = 0.0
        for place in range(down_ref.shape[1] // down_rows):
            matrix = down_ref[:, place * down_rows : (place + 1) * down_rows, :].reshape(-1, BLOCK)
            lanes = pl.ds(pl.multiple_of((step * FFN_DOWNS + place) * BLOCK, BLOCK), BLOCK)
            total = total + dot(g_ref[:, lanes], matrix, NT)

        @pl.when(step == 0)
        def _():
            hidden_grad[...] = total

        @pl.when(step > 0)
        def _():
            hidden_grad[...] += total

    @pl.when(step >= down_steps)
    def _():
        count = unit_ref.shape[1] // unit_rows
        total = 0.0
        for place in range(count):
            matrix = unit_ref[:, place * unit_rows : (place + 1) * unit_rows, :].reshape(-1, BLOCK)
            both = dot(x_ref[...], matrix, NN)
            gate, upward = both[:, :half], both[:, half:]
            spot = (step - down_steps) * count + place
            lanes = pl.ds(pl.multiple_of(spot * half, half), half)
            above = hidden_grad[:, lanes]
            sigmoid, silu = silu_parts(gate)
            hidden_ref[:, lanes] = (silu * upward).astype(LOW)
            grad_gate = above * upward * (sigmoid * (1.0 + gate * (1.0 - sigmoid)))
            grads = jnp.concatenate([grad_gate, above * silu], axis=1).astype(LOW)
            grads_ref[place] = grads
            total = total + dot(grads, matrix, NT)

        @pl.when(step == down_steps)
        def _():
            inner_ref[...] = total

        @pl.when(step > down_steps)
        def _():
            inner_ref[...] += total

    @pl.when(step == pl.num_programs(0) - 1)
    def _():
        put_parts(inner_ref[...], slice(0, D), *part_refs)


def ffn_down_kernel(hidden_ref, down_ref, *out_refs, down_rows):
    for place in range(down_ref.shape[1] // down_rows):
        matrix = down_ref[:, place * down_rows : (place + 1) * down_rows, :].reshape(-1, BLOCK)
        lanes = slice(place * BLOCK, (place + 1) * BLOCK)
        put_parts(dot(hidden_ref[...], matrix, NN), lanes, *out_refs)


FFN_DOWNS = 4


def ffn_units(cols_ff):
    return max(count for count in (1, 2, 3) if 2 * cols_ff // BLOCK % count == 0)


def ffn_specs(cols_ff, unit_rows, down_rows, groups, unit_step, down_step):
    unit_blocks, down_blocks = 2 * cols_ff // BLOCK, D // BLOCK
    units, downs = ffn_units(cols_ff) * unit_rows, FFN_DOWNS * down_rows
    first_down = unit_blocks * unit_rows // downs
    return (
        unit_blocks // ffn_units(cols_ff),
        down_blocks // FFN_DOWNS,
        [
            pl.BlockSpec((groups, units, BLOCK), lambda i: (0, unit_step(i), 0)),
            pl.BlockSpec((groups, downs, BLOCK), lambda i: (0, first_down + down_step(i), 0)),
        ],
    )


def ffn_forward(rows, packed, cols_ff, unit_rows, down_rows):
    tokens, unit_steps = 4 * rows[0].shape[0], 2 * cols_ff // BLOCK // ffn_units(cols_ff)
    unit_step = lambda i: jnp.minimum(i, unit_steps - 1)
    down_step = lambda i: jnp.maximum(i - unit_steps, 0)
    unit_steps, down_steps, specs = ffn_specs(
        cols_ff, unit_rows, down_rows, packed.shape[0], unit_step, down_step
    )
    parts, part_specs = parts_of(tokens, FFN_DOWNS * BLOCK, lambda i: (0, down_step(i)))
    results = [
        jax.ShapeDtypeStruct((2 * cols_ff // BLOCK, tokens, BLOCK), LOW),
        jax.ShapeDtypeStruct((tokens, cols_ff), LOW),
        *parts,
    ]
    return pl.pallas_call(
        functools.partial(
            ffn_forward_kernel, unit_rows=unit_rows, down_rows=down_rows, unit_steps=unit_steps
        ),
        grid=(unit_steps + down_steps,),
        in_specs=[pl.BlockSpec(rows[0].shape, lambda i: (0, 0))] * 4 + specs,
        out_specs=[
            pl.BlockSpec((ffn_units(cols_ff), tokens, BLOCK), lambda i: (unit_step(i), 0, 0)),
            pl.BlockSpec((tokens, cols_ff), lambda i: (0, 0)),
            *part_specs,
        ],
        out_shape=results,
        scratch_shapes=[pltpu.VMEM((tokens, D), LOW)],
        cost_estimate=cost(6 * tokens * D * cols_ff, [*rows, packed], results),
        compiler_params=pltpu.CompilerParams(vmem_limit_bytes=VMEM_LIMIT),
        name="ffn_forward",
    )(*rows, packed, packed)


def ffn_backward(rows, packed, both, cols_ff, unit_rows, down_rows):
    tokens, down_steps = 4 * rows[0].shape[0], D // BLOCK // FFN_DOWNS
    unit_step = lambda i: jnp.maximum(i - down_steps, 0)
    down_step = lambda i: jnp.minimum(i, down_steps - 1)
    unit_steps, down_steps, specs = ffn_specs(
        cols_ff, unit_rows, down_rows, packed.shape[0], unit_step, down_step
    )
    unit_spec = pl.BlockSpec((ffn_units(cols_ff), tokens, BLOCK), lambda i: (unit_step(i), 0, 0))
    parts, part_specs = parts_of(tokens, D, lambda i: (0, 0))
    results = [jax.ShapeDtypeStruct((2 * cols_ff // BLOCK, tokens, BLOCK), LOW), *parts]
    return pl.pallas_call(
        functools.partial(
            ffn_backward_kernel, unit_rows=unit_rows, down_rows=down_rows, down_steps=down_steps
        ),
        grid=(unit_steps + down_steps,),
        in_specs=[pl.BlockSpec(rows[0].shape, lambda i: (0, 0))] * 4 + [*specs, unit_spec],
        out_specs=[unit_spec, *part_specs],
        out_shape=results,
        scratch_shapes=[
            pltpu.VMEM((tokens, D), jnp.float32),
            pltpu.VMEM((tokens, cols_ff), jnp.float32),
            pltpu.VMEM((tokens, D), LOW),
        ],
        cost_estimate=cost(6 * tokens * D * cols_ff, [*rows, packed, both], results),
        compiler_params=pltpu.CompilerParams(vmem_limit_bytes=VMEM_LIMIT),
        name="ffn_backward",
    )(*rows, packed, packed, both)


def ffn_turn(rows, grad_rows, packed, cols_ff, unit_rows, down_rows):
    tokens, down_steps = 4 * rows[0].shape[0], D // BLOCK // FFN_DOWNS
    unit_step = lambda i: jnp.maximum(i - down_steps, 0)
    down_step = lambda i: jnp.minimum(i, down_steps - 1)
    unit_steps, down_steps, specs = ffn_specs(
        cols_ff, unit_rows, down_rows, packed.shape[0], unit_step, down_step
    )
    parts, part_specs = parts_of(tokens, D, lambda i: (0, 0))
    results = [
        jax.ShapeDtypeStruct((2 * cols_ff // BLOCK, tokens, BLOCK), LOW),
        jax.ShapeDtypeStruct((tokens, cols_ff), LOW),
        *parts,
    ]
    return pl.pallas_call(
        functools.partial(
            ffn_turn_kernel, unit_rows=unit_rows, down_rows=down_rows, down_steps=down_steps
        ),
        grid=(unit_steps + down_steps,),
        in_specs=[pl.BlockSpec(rows[0].shape, lambda i: (0, 0))] * 8 + specs,
        out_specs=[
            pl.BlockSpec((ffn_units(cols_ff), tokens, BLOCK), lambda i: (unit_step(i), 0, 0)),
            pl.BlockSpec((tokens, cols_ff), lambda i: (0, 0)),
            *part_specs,
        ],
        out_shape=results,
        scratch_shapes=[
            pltpu.VMEM((tokens, D), jnp.float32),
            pltpu.VMEM((tokens, cols_ff), jnp.float32),
            pltpu.VMEM((tokens, D), LOW),
            pltpu.VMEM((tokens, D), LOW),
        ],
        cost_estimate=cost(10 * tokens * D * cols_ff, [*rows, *grad_rows, packed], results),
        compiler_params=pltpu.CompilerParams(vmem_limit_bytes=VMEM_LIMIT),
        name="ffn_turn",
    )(*rows, *grad_rows, packed, packed)


def ffn_down(hidden, packed, unit_rows, down_rows):
    tokens, cols_ff = hidden.shape
    specs = ffn_specs(
        cols_ff, unit_rows, down_rows, packed.shape[0], lambda i: 0, lambda i: i
    )[2]
    results, part_specs = parts_of(tokens, FFN_DOWNS * BLOCK, lambda i: (0, i))
    return pl.pallas_call(
        functools.partial(ffn_down_kernel, down_rows=down_rows),
        grid=(D // BLOCK // FFN_DOWNS,),
        in_specs=[pl.BlockSpec(hidden.shape, lambda i: (0, 0)), specs[1]],
        out_specs=part_specs,
        out_shape=results,
        cost_estimate=cost(2 * tokens * D * cols_ff, [hidden], results),
        compiler_params=pltpu.CompilerParams(vmem_limit_bytes=VMEM_LIMIT),
        name="ffn_down",
    )(hidden, packed)


def ffn_weight_grads_kernel(*refs, unit_rows, down_rows):
    unit_grads_ref, hidden_ref, g_refs, out_ref, x_ref = refs[4], refs[5], refs[6:10], refs[10], refs[11]
    step, last = pl.program_id(0), pl.num_programs(0) - 1

    @pl.when(step == 0)
    def _():
        rows = refs[0].shape[0]
        for place, ref in enumerate(refs[:4]):
            x_ref[:, place * rows : (place + 1) * rows] = ref[...].T

    @pl.when(step < last)
    def _():
        for place in range(out_ref.shape[1] // unit_rows):
            grad = dot(x_ref[...], unit_grads_ref[place], NN)
            grad = grad.reshape(-1, unit_rows, BLOCK).astype(LOW)
            out_ref[:, place * unit_rows : (place + 1) * unit_rows, :] = grad

    @pl.when(step == last)
    def _():
        hidden = hidden_ref[...].T
        for place in range(out_ref.shape[1] // down_rows):
            lanes = slice(place * BLOCK, (place + 1) * BLOCK)
            right = jnp.concatenate([ref[:, lanes] for ref in g_refs], axis=0)
            grad = dot(hidden, right, NN).reshape(-1, down_rows, BLOCK).astype(LOW)
            out_ref[:, place * down_rows : (place + 1) * down_rows, :] = grad


def ffn_weight_grads(rows, unit_grads, hidden, grad_rows, groups, unit_rows, down_rows):
    tokens, cols_ff = hidden.shape
    step_rows = D // BLOCK * down_rows
    per_step = step_rows // unit_rows
    steps = unit_grads.shape[0] // per_step
    last = steps - 1
    result = jax.ShapeDtypeStruct((groups, (steps + 1) * step_rows, BLOCK), LOW)
    part_spec = pl.BlockSpec(rows[0].shape, lambda i: (0, 0))
    return pl.pallas_call(
        functools.partial(ffn_weight_grads_kernel, unit_rows=unit_rows, down_rows=down_rows),
        grid=(steps + 1,),
        in_specs=[part_spec] * 4
        + [
            pl.BlockSpec((per_step, tokens, BLOCK), lambda i: (jnp.minimum(i, last), 0, 0)),
            pl.BlockSpec(hidden.shape, lambda i: (0, 0)),
        ]
        + [part_spec] * 4,
        out_specs=pl.BlockSpec((groups, step_rows, BLOCK), lambda i: (0, i, 0)),
        out_shape=result,
        scratch_shapes=[pltpu.VMEM((D, tokens), LOW)],
        cost_estimate=cost(6 * tokens * D * cols_ff, [*rows, unit_grads, hidden, *grad_rows], [result]),
        compiler_params=pltpu.CompilerParams(vmem_limit_bytes=VMEM_LIMIT),
        name="ffn_weight_grads",
    )(*rows, unit_grads, hidden, *grad_rows)


def out_grad_kernel(left_ref, right_ref, out_ref, *, rows):
    for place in range(D // BLOCK):
        grad = dot(left_ref[...], right_ref[:, place * BLOCK : (place + 1) * BLOCK], NN)
        out_ref[:, place * rows : (place + 1) * rows, :] = grad.reshape(-1, rows, BLOCK).astype(LOW)


def out_weight_grad(left, right, rows):
    result = jax.ShapeDtypeStruct((left.shape[0] // rows, D // BLOCK * rows, BLOCK), LOW)
    return pl.pallas_call(
        functools.partial(out_grad_kernel, rows=rows),
        in_specs=in_vmem(2),
        out_specs=in_vmem(1)[0],
        out_shape=result,
        cost_estimate=cost(2 * left.size * D, [left, right], [result]),
        compiler_params=pltpu.CompilerParams(vmem_limit_bytes=VMEM_LIMIT),
        name="out_weight_grad",
    )(left, right)


def gain_column(gain_ref, layer):
    return jnp.broadcast_to(gain_ref[layer : layer + 1, :], (128, gain_ref.shape[1])).T[:, :1]


def take_qkv(room_ref, layer, quarter, weights, gain_ref):
    gain = gain_column(gain_ref, layer)
    for slot in range(QUARTER_HEADS):
        column = HD * (QUARTERS * slot + quarter)
        for which, weight_ref in enumerate(weights):
            first = (3 * slot + which) * HD
            part = weight_ref[layer, :, column : column + HD] * gain
            room_ref[:, first : first + HD] = part


def first_parts_kernel(lo_ref, *refs):
    weights, gain_ref, out_ref, room_ref = refs[:3], refs[3], refs[4], refs[5]
    for quarter in range(QUARTERS):
        take_qkv(room_ref, 0, quarter, weights, gain_ref)
        out_ref[2 * quarter + lo_ref[0]] = room_ref[...].astype(LOW)
        out_ref[2 * quarter + 1 - lo_ref[0]] = jnp.zeros(room_ref.shape, LOW)


def first_parts(lo, weights, gain):
    w_rows, width = weights[0].shape[1], 3 * QUARTER_HEADS * HD
    return pl.pallas_call(
        first_parts_kernel,
        in_specs=[pl.BlockSpec(memory_space=pltpu.SMEM)] + in_vmem(4),
        out_specs=in_vmem(1)[0],
        out_shape=jax.ShapeDtypeStruct((2 * QUARTERS, w_rows, width), LOW),
        scratch_shapes=[pltpu.VMEM((w_rows, width), jnp.float32)],
        compiler_params=pltpu.CompilerParams(vmem_limit_bytes=VMEM_LIMIT),
        name="first_parts",
    )(lo, *weights, gain)


def unit_places(d_rows, padded, planes):
    width = 2 * planes // 2 * padded
    column = lax.broadcasted_iota(jnp.int32, (1, QUARTERS * width), 1)
    quarter, rest = column // width, column % width
    group, unit = rest // padded, rest % padded
    source = d_rows * (8 * (group // 2) + 2 * quarter + group % 2) + unit
    source = jnp.where(unit < d_rows, source, -1)
    rows = lax.broadcasted_iota(jnp.int32, (4 * planes * d_rows, 1), 0)
    return jnp.where(rows == source, 1.0, 0.0).astype(LOW)


def later_parts_kernel(place_ref, *refs, d_rows, padded, planes):
    weights, gains = refs[:5], refs[5:7]
    outs, rows_ref, qkv_ref, all_ref = refs[7:11], refs[11], refs[12], refs[13]
    half, cols_ff = BLOCK // 2, 2 * planes * padded
    w_rows, width = weights[0].shape[1], cols_ff // 2
    taken = 4 * planes * d_rows
    pieces = [(layer, which, part) for layer in range(LAYERS) for which in range(2) for part in range(2)]
    for number, (layer, which, part) in enumerate(pieces):
        rows = weights[3 + which][layer, :, part * taken : (part + 1) * taken] * gain_column(gains[1], layer)
        rows_ref[number * w_rows : (number + 1) * w_rows, :] = rows
    placed = dot(rows_ref[...].astype(LOW), unit_places(d_rows, padded, planes), NN)
    for number, (layer, which, part) in enumerate(pieces):
        rows = placed[number * w_rows : (number + 1) * w_rows].astype(LOW)
        for quarter in range(QUARTERS):
            for block in range(width // half):
                first = layer * 2 * cols_ff + (part * (width // half) + block) * BLOCK + which * half
                lane = quarter * width + block * half
                all_ref[quarter, :, first : first + half] = rows[:, lane : lane + half]
    for quarter in range(QUARTERS):
        for layer in range(1, LAYERS):
            take_qkv(qkv_ref, layer, quarter, weights[:3], gains[0])
            first = LAYERS * 2 * cols_ff + (layer - 1) * qkv_ref.shape[1]
            all_ref[quarter, :, first : first + qkv_ref.shape[1]] = qkv_ref[...].astype(LOW)
    for place, out_ref in enumerate(outs):
        out_ref[...] = all_ref[place ^ place_ref[0]]


def later_parts(place, weights, gains, d_rows, planes):
    w_rows = weights[0].shape[1]
    padded = -(-d_rows // 16) * 16
    cols_ff, width = 2 * planes * padded, 3 * QUARTER_HEADS * HD
    whole = LAYERS * 2 * cols_ff + (LAYERS - 1) * width
    return pl.pallas_call(
        functools.partial(later_parts_kernel, d_rows=d_rows, padded=padded, planes=planes),
        in_specs=[pl.BlockSpec(memory_space=pltpu.SMEM)] + in_vmem(7),
        out_specs=in_vmem(4),
        out_shape=[jax.ShapeDtypeStruct((w_rows, whole), LOW)] * QUARTERS,
        scratch_shapes=[
            pltpu.VMEM((4 * LAYERS * w_rows, 4 * planes * d_rows), jnp.float32),
            pltpu.VMEM((w_rows, width), jnp.float32),
            pltpu.VMEM((QUARTERS, w_rows, whole), LOW),
        ],
        compiler_params=pltpu.CompilerParams(vmem_limit_bytes=VMEM_LIMIT),
        name="later_parts",
    )(place, *weights, *gains)


def put_qkv(came_ref, place_ref, start, outs, layer, weights, gain_ref, gain_out_ref):
    for quarter in range(QUARTERS):
        part = came_ref[place_ref[quarter], :, start : start + 3 * QUARTER_HEADS * HD]
        part = part.astype(jnp.float32)
        for slot in range(QUARTER_HEADS):
            column = HD * (QUARTERS * slot + quarter)
            for which, out_ref in enumerate(outs):
                first = (3 * slot + which) * HD
                out_ref[layer, :, column : column + HD] = part[:, first : first + HD]
    gain_grad = 0.0
    for out_ref, weight_ref in zip(outs, weights):
        grad = out_ref[layer]
        gain_grad = gain_grad + jnp.sum(grad * weight_ref[layer], axis=1, keepdims=True)
        out_ref[layer] = grad * gain_column(gain_ref, layer)
    gain_out_ref[layer : layer + 1, :] = jnp.broadcast_to(gain_grad, (gain_grad.shape[0], 128)).T[:1]


def put_units(came_ref, place_ref, start, outs, layer, weights, gain_ref, gain_out_ref, d_rows, padded, planes):
    half = BLOCK // 2
    for quarter in range(QUARTERS):
        part = came_ref[place_ref[quarter], :, start : start + 4 * planes * padded]
        part = part.astype(jnp.float32)
        for plane in range(planes):
            for core in range(2):
                column = d_rows * (8 * plane + 2 * quarter + core)
                unit, end = (2 * plane + core) * padded, (2 * plane + core) * padded + d_rows
                while unit < end:
                    stop = min(end, (unit // half + 1) * half)
                    for which, out_ref in enumerate(outs):
                        first = unit // half * BLOCK + which * half + unit % half
                        out_ref[layer, :, column : column + stop - unit] = part[
                            :, first : first + stop - unit
                        ]
                    column, unit = column + stop - unit, stop
    gain_grad = 0.0
    for out_ref, weight_ref in zip(outs, weights):
        grad = out_ref[layer]
        gain_grad = gain_grad + jnp.sum(grad * weight_ref[layer], axis=1, keepdims=True)
        out_ref[layer] = grad * gain_column(gain_ref, layer)
    gain_out_ref[layer : layer + 1, :] = jnp.broadcast_to(gain_grad, (gain_grad.shape[0], 128)).T[:1]


def finish_kernel(place_ref, *refs, unit_end, w_rows, d_rows, padded, planes, with_out):
    out_lanes = slice(3 * QUARTER_HEADS * HD, 3 * QUARTER_HEADS * HD + BLOCK)
    came_ref, *sums = refs[: 1 + LAYERS]
    out_sums, refs = refs[1 + LAYERS : 2 * LAYERS], refs[2 * LAYERS :]
    weights, gains, outs = refs[:5], refs[5:7], refs[7:]
    units_width = 4 * planes * padded
    for layer in range(LAYERS):
        put_units(
            came_ref, place_ref, layer * units_width, outs[4:6], layer, weights[3:], gains[1],
            outs[8], d_rows, padded, planes,
        )
        if layer > 0:
            start = LAYERS * units_width + (layer - 1) * 3 * QUARTER_HEADS * HD
            put_qkv(came_ref, place_ref, start, outs[:3], layer, weights[:3], gains[0], outs[7])
        for block in range(D // BLOCK):
            lanes = slice(block * BLOCK, (block + 1) * BLOCK)
            rows = sums[layer][unit_end + block * padded : unit_end + (block + 1) * padded, :]
            outs[6][layer, :, lanes] = rows.astype(jnp.float32)[:d_rows]
            if with_out and layer > 0:
                rows = out_sums[layer - 1][block * w_rows : (block + 1) * w_rows, out_lanes]
                outs[3][layer, :, lanes] = rows.astype(jnp.float32)


def finish_first_kernel(place_ref, came_ref, out_sum_ref, *refs, w_rows, with_out):
    out_lanes = slice(3 * QUARTER_HEADS * HD, 3 * QUARTER_HEADS * HD + BLOCK)
    weights, gain_ref, have, outs = refs[:3], refs[3], refs[4:9], refs[9:]
    for layer in range(1, LAYERS):
        for have_ref, out_ref in zip(have, outs):
            out_ref[layer : layer + 1] = have_ref[layer : layer + 1]
    put_qkv(came_ref, place_ref, 0, outs[:3], 0, weights, gain_ref, outs[3])
    if with_out:
        for block in range(D // BLOCK):
            rows = out_sum_ref[block * w_rows : (block + 1) * w_rows, out_lanes]
            outs[4][0, :, block * BLOCK : (block + 1) * BLOCK] = rows.astype(jnp.float32)


def finish_gradients(
    place, came, sums, out_sums, weights, gains, d_shape, unit_end, planes, with_out
):
    layers, w_rows, unused = weights[0].shape
    d_rows = d_shape[1]
    padded = -(-d_rows // 16) * 16
    shapes = [weights[0].shape] * 4 + [weights[3].shape] * 2 + [d_shape] + [(layers, w_rows)] * 2
    return pl.pallas_call(
        functools.partial(
            finish_kernel, unit_end=unit_end, w_rows=w_rows, d_rows=d_rows, padded=padded, planes=planes,
            with_out=with_out,
        ),
        in_specs=[pl.BlockSpec(memory_space=pltpu.SMEM)] + in_vmem(7 + 2 * LAYERS),
        out_specs=in_vmem(9),
        out_shape=[jax.ShapeDtypeStruct(shape, jnp.float32) for shape in shapes],
        compiler_params=pltpu.CompilerParams(vmem_limit_bytes=VMEM_LIMIT),
        name="finish_gradients",
    )(place, came, *sums, *out_sums, *weights, *gains)


def finish_first(place, came, out_sum, weights, gain, grads, with_out):
    return pl.pallas_call(
        functools.partial(finish_first_kernel, w_rows=weights[0].shape[1], with_out=with_out),
        in_specs=[pl.BlockSpec(memory_space=pltpu.SMEM)] + in_vmem(11),
        out_specs=in_vmem(5),
        out_shape=[jax.ShapeDtypeStruct(member.shape, jnp.float32) for member in grads],
        compiler_params=pltpu.CompilerParams(vmem_limit_bytes=VMEM_LIMIT),
        name="finish_first",
    )(place, came, out_sum, *weights, gain, *grads)


def on_device(
    tokens,
    w_query,
    w_key,
    w_value,
    w_out,
    w_gate,
    w_up,
    w_down,
    gain_attn,
    gain_ffn,
    variate_bias,
    doc_starts,
    variate_ids,
    time_ids,
    cotangent,
):
    seq = lax.axis_size("seq")
    planes = seq // 2
    spread = planes // QUARTER_HEADS
    tiles = planes // spread
    tok_rows = tokens.shape[0]
    cols = 4 * tok_rows
    all_rows = variate_ids.shape[0]
    w_rows = w_query.shape[1]
    d_rows = w_down.shape[1]
    padded = -(-d_rows // 16) * 16
    quarter_ff = 2 * planes * padded
    quarter_width = QUARTER_HEADS * HD
    split_heads = 2 * w_rows == HD
    here_seq, here_head = lax.axis_index("seq"), lax.axis_index("head")
    here_plane, here_lo = here_seq // 2, here_seq % 2
    here_y, here_core = here_head // 2, here_head % 2
    my_quarter = 2 * here_lo + here_y
    my_head = QUARTERS * (here_plane // spread) + my_quarter
    first_tile = (here_plane % spread) * tiles
    devices = [
        (plane, lo, y, core)
        for plane in range(planes)
        for lo in range(2)
        for y in range(2)
        for core in range(2)
    ]

    def place_of(plane, lo, y, core):
        return 8 * plane + 4 * lo + 2 * y + core

    row_groups = [
        [place_of(plane, lo, y, core) for plane in range(planes) for core in range(2)]
        for lo in range(2)
        for y in range(2)
    ]
    plane_groups = [[2 * plane + lo for plane in range(planes)] for lo in range(2)]
    x_swap = [(place, place ^ 1) for place in range(seq)]
    corner_swap = [
        (place_of(plane, lo, y, core), place_of(plane, 1 - lo, 1 - y, core))
        for plane, lo, y, core in devices
    ]

    def neighbours(across_y, across_x, across_both):
        return (
            lax.ppermute(across_y, "head", Y_SWAP),
            lax.ppermute(across_x, "seq", x_swap),
            lax.ppermute(across_both, BOTH, corner_swap),
        )

    def beside_parts(value):
        return [value, *neighbours(value, value, value)]

    def beside(value):
        return jnp.concatenate(beside_parts(value), axis=0)

    def fold(own, *others):
        return own + sum(part.astype(jnp.float32) for part in neighbours(*others))

    def four_parts(partial):
        low = partial[tok_rows:].astype(LOW).reshape(3, tok_rows, -1)
        return partial[:tok_rows], low[0], low[1], low[2]

    def flip(pair, bit):
        return jnp.where(bit == 0, pair[0], pair[1]), jnp.where(bit == 0, pair[1], pair[0])

    def xor_order(grid, high, low):
        rows = [flip(row, low) for row in grid]
        first, second = zip(*[flip(column, high) for column in zip(*rows)])
        return [list(first), list(second)]

    def cross_rows(parts):
        came = [[None, None], [None, None]]
        for high in range(2):
            for low in range(2):
                hops = [
                    (place_of(plane, lo, y, core), place_of(plane, y ^ high, core ^ low, lo))
                    for plane, lo, y, core in devices
                ]
                came[high][low] = lax.ppermute(parts[2 * high + low], BOTH, hops)
        came = xor_order(came, here_lo, here_y)
        return jnp.concatenate([*came[0], *came[1]], axis=0)

    def cross_back(rows):
        parts = [rows[place * w_rows : (place + 1) * w_rows] for place in range(4)]
        grid = xor_order([parts[:2], parts[2:]], here_lo, here_y)
        came = [[None, None], [None, None]]
        for high in range(2):
            for low in range(2):
                hops = [
                    (place_of(plane, lo, y, core), place_of(plane, core, lo ^ high, y ^ low))
                    for plane, lo, y, core in devices
                ]
                came[high][low] = lax.ppermute(grid[high][low], BOTH, hops)
        return jnp.stack([*came[0], *came[1]])

    device_groups = [[8 * plane + place for place in range(8)] for plane in range(planes)]

    def plane_exchange(value):
        return lax.all_to_all(
            value, BOTH, split_axis=0, concat_axis=0, tiled=True, axis_index_groups=device_groups
        )

    def cross_rows_at_once(sent):
        came = plane_exchange(sent)
        came = jnp.where(here_core == 0, came[:4], came[4:])
        return came.reshape(-1, sent.shape[-1])

    def cross_back_at_once(rows):
        parts = rows.reshape(4, w_rows, -1)
        zeros = jnp.zeros_like(parts)
        sent = [jnp.where(here_core == lo, parts, zeros) for lo in range(2)]
        return plane_exchange(jnp.concatenate(sent, axis=0))

    def gather(part):
        return lax.all_gather(part, BOTH, axis=0, tiled=True, axis_index_groups=row_groups)

    def blocks_of(matrix):
        rows, n = matrix.shape
        return matrix.reshape(rows, n // BLOCK, BLOCK).transpose(1, 0, 2).reshape(-1, BLOCK)

    def from_blocks(packed, rows):
        groups, count = packed.shape[0], packed.shape[1] // rows
        parts = packed.reshape(groups, count, rows, BLOCK).transpose(0, 2, 1, 3)
        return parts.reshape(groups * rows, count * BLOCK)

    def scatter(packed):
        part = lax.psum_scatter(
            packed.reshape(-1, packed.shape[-1]),
            BOTH,
            scatter_dimension=0,
            tiled=True,
            axis_index_groups=row_groups,
        )
        return part

    def whole_out_back(grad):
        spaced = lax.dynamic_update_slice_in_dim(
            jnp.zeros((QUARTER_HEADS, QUARTERS, HD, D), LOW),
            grad.astype(LOW).reshape(QUARTER_HEADS, 1, HD, D),
            my_quarter,
            1,
        )
        return lax.psum_scatter(spaced.reshape(D, D), BOTH, scatter_dimension=0, tiled=True)

    def normalize(values):
        inverse = lax.rsqrt(jnp.mean(values * values, axis=-1, keepdims=True) + NORM_EPS)
        return values * inverse, inverse

    def normalize_back(scaled, inverse, inner):
        return inverse * (inner - scaled * jnp.mean(inner * scaled, axis=-1, keepdims=True))

    def attention_part(layer, qkv_rows):
        blocks = blocks_of(w_out[layer].astype(LOW))
        return jnp.concatenate([qkv_rows, blocks], axis=1)

    def attention_matrices(part):
        whole = gather(part)
        blocks = whole[:, 3 * quarter_width :].reshape(2 * planes, -1, BLOCK)
        return whole[:, : 3 * quarter_width], from_blocks(blocks, w_rows)

    gains = (gain_attn, gain_ffn)
    first_sent = first_parts(
        jnp.reshape(here_lo, (1,)).astype(jnp.int32), (w_query, w_key, w_value), gains[0]
    )
    first_part = attention_part(0, cross_rows_at_once(first_sent))
    first_part, time_ids, w_gate, w_up = lax.optimization_barrier((first_part, time_ids, w_gate, w_up))
    attention_weights, out_weights = [attention_matrices(first_part)], []
    start_scaled, start_inverse = normalize(tokens)
    start_normed = beside(start_scaled.astype(LOW))

    group_rows = 4 * w_rows
    unit_end = 2 * quarter_ff // BLOCK * group_rows
    ffn_end = unit_end + D // BLOCK * padded

    def ffn_part(layer, units_rows):
        down_part = jnp.pad(w_down[layer].astype(LOW), ((0, padded - d_rows), (0, 0)))
        return jnp.concatenate([blocks_of(units_rows), blocks_of(down_part)], axis=0)

    later_sent = later_parts(
        jnp.reshape(2 * here_y + here_core, (1,)).astype(jnp.int32),
        (w_query, w_key, w_value, w_gate, w_up), gains, d_rows, planes,
    )
    later_widths = [2 * quarter_ff] * LAYERS + [3 * quarter_width] * (LAYERS - 1)

    def cut(whole):
        parts, start = [], 0
        for width in later_widths:
            parts.append(whole[..., start : start + width])
            start += width
        return parts

    ffn_weights = []

    def placed_ids(ids):
        ids = ids.reshape(planes, 2, 2, 2, tok_rows)
        ids = jnp.where(here_lo == 0, ids, ids[:, ::-1])
        ids = jnp.where(here_y == 0, ids, ids[:, :, ::-1])
        ids = jnp.where(here_core == 0, ids, ids[:, :, :, ::-1])
        return ids.transpose(3, 0, 1, 2, 4).reshape(2 * planes, cols)

    def my_tiles(value):
        if spread == 1:
            return value
        return lax.dynamic_slice_in_dim(value, first_tile, tiles, 0)

    positions = jnp.arange(all_rows, dtype=jnp.int32)
    doc_ids = jnp.sum((doc_starts[None, :] <= positions[:, None]).astype(jnp.int32), axis=1)
    docs = placed_ids(doc_ids)
    variates = placed_ids(variate_ids)
    q_docs, q_variates = my_tiles(docs[:planes]), my_tiles(variates[:planes])
    extra_row = jnp.arange(HD, dtype=jnp.int32)[None, :, None]

    def one_hot(ids):
        return ids[:, None, :] == extra_row % VARIATES

    def is_doc(ids):
        return ids[:, None, :] == extra_row - 24

    doc_row = (extra_row >= 24) & (extra_row < 32)
    ones_row = (extra_row == 16) | (extra_row == 17) | ((extra_row >= 32) & (extra_row < 35))
    k_hits = one_hot(variates) & (extra_row < 16) | is_doc(docs) & doc_row | ones_row
    k_aug = jnp.where(k_hits, 1.0, 0.0).astype(LOW)

    def query_extra(layer):
        same, other = variate_bias[layer, 0, my_head], variate_bias[layer, 1, my_head]
        gap = same - other
        gap_lead, other_lead = (part.astype(LOW).astype(jnp.float32) for part in (gap, other))
        gap_part = jnp.where(extra_row < VARIATES, gap_lead, gap - gap_lead)
        other_part = jnp.where(extra_row == 16, other_lead, other - other_lead)
        spread_gap = jnp.where(one_hot(q_variates), gap_part, 0.0)
        shut = jnp.where(doc_row & ~is_doc(q_docs), FLOOR_SCORE, 0.0)
        tail = jnp.where(extra_row < 18, other_part, shut)
        return jnp.where(extra_row < 16, spread_gap, tail).astype(LOW)

    q_augs = [query_extra(layer) for layer in range(LAYERS)]
    q_onehots = (q_variates[:, None, :] == jnp.arange(VARIATES, dtype=jnp.int32)[:, None]).astype(
        jnp.float32
    )

    half_dim = HD // 2
    frequency = jnp.exp(jnp.arange(half_dim).astype(jnp.float32) * (-2.0 * math.log(10000.0) / HD))
    times = beside(time_ids.astype(jnp.float32))
    angles = frequency[:, None] * times[None, :]
    cosines, sines = jnp.cos(angles), jnp.sin(angles)
    start_normed, later_sent, k_aug, cosines, sines, *q_augs = lax.optimization_barrier(
        (start_normed, later_sent, k_aug, cosines, sines, *q_augs)
    )

    def rotate(values, sines):
        former, latter = values[:, :half_dim], values[:, half_dim:]
        return jnp.concatenate(
            [former * cosines - latter * sines, latter * cosines + former * sines], axis=1
        )

    def to_heads(value):
        if spread > 1:
            value = jnp.repeat(value, spread, axis=0)
        return lax.all_to_all(
            value, "seq", split_axis=0, concat_axis=0, tiled=True, axis_index_groups=plane_groups
        )

    def all_blocks(value):
        if spread == 1:
            return value
        zeros = jnp.zeros((planes,) + value.shape[1:], value.dtype)
        return lax.dynamic_update_slice_in_dim(zeros, value, first_tile, 0)

    def over_spread(value):
        if spread == 1:
            return value
        value = value.reshape((QUARTER_HEADS, spread) + value.shape[1:])
        return jnp.sum(value.astype(jnp.float32), axis=1).astype(LOW)

    def from_heads(value):
        return over_spread(
            lax.all_to_all(
                value, "seq", split_axis=0, concat_axis=0, tiled=True, axis_index_groups=plane_groups
            )
        )

    chip_groups = [
        [place_of(plane, lo, y, core) for plane in range(planes) for lo in range(2) for y in range(2)]
        for core in range(2)
    ]

    def over_chips(value):
        shape = value.shape
        value = value.reshape(-1, *shape[2:])
        value = lax.all_to_all(
            value, BOTH, split_axis=0, concat_axis=0, tiled=True, axis_index_groups=chip_groups
        )
        return value.reshape(shape)

    chip_flips = jnp.reshape(my_quarter, (1,)).astype(jnp.int32)

    def plane_order(value):
        grid = [[value[:, 2 * lo + y] for y in range(2)] for lo in range(2)]
        grid = xor_order(grid, here_lo, here_y)
        return jnp.stack([*grid[0], *grid[1]])

    def chip_order(value):
        grid = xor_order([[value[0], value[1]], [value[2], value[3]]], here_lo, here_y)
        return jnp.stack([*grid[0], *grid[1]], axis=1)

    def sum_everywhere(value):
        for axis, size in (("head", 4), ("seq", seq)):
            hop = 1
            while hop < size:
                swap = [(place, place ^ hop) for place in range(size)]
                value = value + lax.ppermute(value, axis, swap)
                hop *= 2
        return value

    def share_for_out(middle_low, attended):
        pieces = attended.reshape(4, quarter_width, tok_rows)
        cuts = quarter_width // tok_rows

        def joined(piece):
            parts = [piece[cut * tok_rows : (cut + 1) * tok_rows] for cut in range(cuts)]
            return jnp.concatenate([middle_low, *parts], axis=1)

        came = neighbours(*(joined(piece) for piece in pieces[1:]))
        tokens_low = jnp.concatenate([middle_low, *(part[:, :D] for part in came)], axis=0)

        def results(part):
            return jnp.concatenate(
                [part[:, D + cut * tok_rows : D + (cut + 1) * tok_rows] for cut in range(cuts)], axis=0
            )

        return tokens_low, jnp.concatenate([pieces[0], *(results(part) for part in came)], axis=1)

    stream = tokens
    saved = []
    for layer in range(LAYERS):
        qkv_matrix, out_quarter = attention_weights[layer]
        if layer == 0:
            scaled_one, inverse_one, normed = start_scaled, start_inverse, start_normed
        else:
            scaled_one, inverse_one = normalize(stream)
            normed = beside(scaled_one.astype(LOW))
        projected = dot(qkv_matrix, normed, TT).reshape(QUARTER_HEADS, 3 * HD, cols)
        query = rotate(projected[:, :HD], sines) * (1.0 / math.sqrt(HD))
        key = rotate(projected[:, HD : 2 * HD], sines)
        sent = jnp.concatenate([query, key, projected[:, 2 * HD :]], axis=1).astype(LOW)
        if layer == 0:
            later_weights = cross_rows(later_sent)
            sent, cotangent = lax.optimization_barrier((sent, cotangent))
            last_grad_parts = beside_parts(cotangent.astype(LOW))
        own = to_heads(sent)
        if layer == 0:
            own, last_grad_parts = lax.optimization_barrier((own, last_grad_parts))
        next_part = ffn_part(layer, cut(later_weights)[layer])
        own, next_part = lax.optimization_barrier((own, next_part))
        packed = gather(next_part).reshape(2 * planes, -1, BLOCK)
        ffn_weights.append(packed)
        if layer == 0:
            own, out_quarter = lax.optimization_barrier((own, out_quarter))
        halves = out_quarter.reshape(2, quarter_width // 2, D)
        half = jnp.where(here_core == 0, halves[0], halves[1])
        out_parts = neighbours(half, half, half)
        sib = lax.ppermute(own, "head", CORE_SWAP)
        queries = my_tiles(own)
        q_aug = q_augs[layer]
        out, lse = attention_forward(chip_flips, queries, q_aug, own, sib, k_aug)
        out, *out_parts = lax.optimization_barrier((out, *out_parts))
        mine = jnp.stack(out_parts)
        other = lax.ppermute(mine, "head", CORE_SWAP)
        pairs = jnp.where(
            here_core == 0, jnp.stack([mine, other], axis=1), jnp.stack([other, mine], axis=1)
        )
        out_matrix = jnp.concatenate([out_quarter, pairs.reshape(3 * quarter_width, D)], axis=0)
        out_weights.append(out_matrix)
        attended = over_spread(over_chips(all_blocks(out))).reshape(QUARTER_HEADS, 4, HD, tok_rows)
        attended = plane_order(attended).reshape(D, tok_rows)
        attended, out_matrix = lax.optimization_barrier((attended, out_matrix))
        middle = stream + dot(attended, out_matrix, TN)
        scaled_two, inverse_two = normalize(middle)
        normed_parts = beside_parts(scaled_two.astype(LOW))
        if layer < LAYERS - 1:
            next_part = attention_part(layer + 1, cut(later_weights)[LAYERS + layer])
            normed_parts, next_part = lax.optimization_barrier((normed_parts, next_part))
            attention_weights.append(attention_matrices(next_part))
        if layer < LAYERS - 1:
            both, hidden, *parts = ffn_forward(normed_parts, packed, quarter_ff, group_rows, padded)
        else:
            both, hidden = None, None
        saved.append(
            (
                scaled_one, inverse_one, normed, own, sib, queries, q_aug, out, lse, attended,
                scaled_two, inverse_two, normed_parts, both, hidden,
            )
        )
        if layer < LAYERS - 1:
            stream = middle + fold(*parts)
        else:
            last_middle = middle

    upstream = cotangent
    whole_grads, ffn_sums, qkv_sums = [None] * LAYERS, [None] * LAYERS, [None] * LAYERS
    bias_parts = [None] * LAYERS
    for layer in reversed(range(LAYERS)):
        qkv_matrix, unused = attention_weights[layer]
        out_matrix, packed = out_weights[layer], ffn_weights[layer]
        (
            scaled_one, inverse_one, normed, own, sib, queries, q_aug, out, lse, attended,
            scaled_two, inverse_two, normed_parts, both, hidden,
        ) = saved[layer]
        if layer < LAYERS - 1:
            upstream_parts = beside_parts(upstream.astype(LOW))
        else:
            upstream_parts = last_grad_parts
        if layer < LAYERS - 1:
            grad_units, *parts = ffn_backward(
                upstream_parts, packed, both, quarter_ff, group_rows, padded
            )
        else:
            grad_units, hidden, *parts = ffn_turn(
                normed_parts, upstream_parts, packed, quarter_ff, group_rows, padded
            )
        inner = fold(*parts)
        buffer = ffn_weight_grads(
            normed_parts, grad_units, hidden, upstream_parts, 2 * planes, group_rows, padded
        )
        inner, buffer = lax.optimization_barrier((inner, buffer))
        if layer < LAYERS - 1:
            buffer, qkv_sums[layer + 1] = lax.optimization_barrier((buffer, qkv_sums[layer + 1]))
        ffn_sums[layer] = scatter(buffer)
        grad_middle = upstream + normalize_back(scaled_two, inverse_two, inner)
        middle_low = grad_middle.astype(LOW)
        grad_attended = dot(out_matrix, middle_low, NT).astype(LOW)
        grad_attended = chip_order(grad_attended.reshape(4, QUARTER_HEADS, HD, tok_rows))
        if spread > 1:
            grad_attended = jnp.repeat(grad_attended, spread, axis=0)
        if layer == LAYERS - 1:
            grad_attended, last_hidden = lax.optimization_barrier((grad_attended, hidden))
            last_parts = ffn_down(last_hidden, packed, group_rows, padded)
        out_grad = my_tiles(over_chips(grad_attended))
        if layer == LAYERS - 1:
            out_grad, *last_parts = lax.optimization_barrier((out_grad, *last_parts))
        out_grad, middle_low, attended = lax.optimization_barrier((out_grad, middle_low, attended))
        middle_low, attended = share_for_out(middle_low, attended)
        grad_q, grad_kv, sent_kv = attention_backward(
            chip_flips, queries, q_aug, lse, out, out_grad, own, sib, k_aug
        )
        grad_kv, middle_low, attended = lax.optimization_barrier((grad_kv, middle_low, attended))
        if not split_heads:
            whole_grads[layer] = whole_out_back(dot(attended, middle_low, NN))
        else:
            out_blocks = out_weight_grad(attended, middle_low, w_rows)
        same_grad = jnp.sum(grad_q[:, HD : HD + VARIATES] * q_onehots)
        all_grad = jnp.sum(grad_q[:, HD + 16])
        crossed = lax.ppermute(sent_kv, "head", CORE_SWAP)
        grad_kv = (grad_kv.astype(jnp.float32) + crossed.astype(jnp.float32)).astype(LOW)
        grad_q = (grad_q[:, :HD] * (1.0 / math.sqrt(HD))).astype(LOW)
        if layer == LAYERS - 1:
            grad_kv, *last_parts = lax.optimization_barrier((grad_kv, *last_parts))
            stream = last_middle + fold(*last_parts)
        grad_heads = from_heads(jnp.concatenate([all_blocks(grad_q), grad_kv], axis=1))
        bias_parts[layer] = jnp.stack([same_grad, all_grad - same_grad])
        if layer == LAYERS - 1:
            grad_heads, stream, bias_parts[layer] = lax.optimization_barrier(
                (grad_heads, stream, bias_parts[layer])
            )
        if layer == 0:
            later_sums = [from_blocks(member[None, :unit_end], group_rows) for member in ffn_sums]
            later_sums += [member[:, : 3 * quarter_width] for member in qkv_sums[1:]]
            came = cross_back(jnp.concatenate(later_sums, axis=1))
            grad_heads, came = lax.optimization_barrier((grad_heads, came))
        grad_heads = jnp.concatenate(
            [
                rotate(grad_heads[:, :HD].astype(jnp.float32), -sines).astype(LOW),
                rotate(grad_heads[:, HD : 2 * HD].astype(jnp.float32), -sines).astype(LOW),
                grad_heads[:, 2 * HD :],
            ],
            axis=1,
        ).reshape(3 * quarter_width, cols)
        partial = dot(grad_heads, qkv_matrix, TT)
        qkv_grad = dot(normed, grad_heads, TT).astype(LOW)
        if split_heads:
            qkv_grad = jnp.concatenate([qkv_grad, out_blocks.reshape(-1, BLOCK)], axis=1)
        if layer > 0:
            inner = fold(*four_parts(partial))
            inner, qkv_grad = lax.optimization_barrier((inner, qkv_grad))
        qkv_grad, ffn_sums[layer] = lax.optimization_barrier((qkv_grad, ffn_sums[layer]))
        qkv_sums[layer] = scatter(qkv_grad)
        if layer > 0:
            upstream = grad_middle + normalize_back(scaled_one, inverse_one, inner)

    later_sums = [from_blocks(member[None, :unit_end], group_rows) for member in ffn_sums]
    bias_local = lax.dynamic_update_slice(
        jnp.zeros((LAYERS, 2, HEADS), jnp.float32), jnp.stack(bias_parts)[:, :, None], (0, 0, my_head)
    )
    bias_total = sum_everywhere(bias_local)
    quarters = jnp.arange(QUARTERS, dtype=jnp.int32)
    weights = (w_query, w_key, w_value, w_gate, w_up)
    *grads, gain_one, gain_two = finish_gradients(
        quarters ^ (2 * here_y + here_core), came, ffn_sums,
        qkv_sums[1:], weights, gains, w_down.shape, unit_end, planes, split_heads,
    )
    qkv_sums[0], gain_two, parts, grads = lax.optimization_barrier(
        (qkv_sums[0], gain_two, four_parts(partial), grads)
    )
    inner = fold(*parts)
    upstream = grad_middle + normalize_back(scaled_one, inverse_one, inner)
    *grads[:3], gain_one, grads[3] = finish_first(
        2 * quarters + here_lo, cross_back_at_once(qkv_sums[0][:, : 3 * quarter_width]), qkv_sums[0], weights[:3], gains[0],
        [*grads[:3], gain_one, grads[3]], split_heads,
    )
    if not split_heads:
        grads[3] = jnp.stack(whole_grads).astype(jnp.float32)
    return (stream, upstream, *grads, gain_one, gain_two, bias_total)


def solution(mesh):
    rows = P(BOTH, None)
    middle = P(None, BOTH, None)
    gains = P(None, BOTH)
    return jax.shard_map(
        on_device,
        mesh=mesh,
        in_specs=(rows,) + (middle,) * 7 + (gains,) * 2 + (P(),) * 3 + (P(BOTH), rows),
        out_specs=(rows, rows) + (middle,) * 7 + (gains,) * 2 + (P(),),
        check_vma=False,
    )
```
